32 devices in a mesh: section: 2 (over y), seq: 4 (over x, core), fsdp: 4 (over z).
Axes of the slice: x: 2, y: 2, z: 4, core: 2. Of those that a mesh axis runs over, the one named last changes fastest.
Arguments:
- section_ends: bfloat16 [2, 2, 4, 1024, 1536], P('section', None, 'fsdp', 'seq'), may hold values from -6 to 6
- norm_gain: bfloat16 [2, 1536], P('section', 'fsdp'), may hold values from 0.5 to 1.5
- in_weight: bfloat16 [2, 1536, 6448], P('section', 'fsdp'), may hold values from -0.15625 to 0.15625
- conv_weight: bfloat16 [2, 4, 3328], P('section', None, 'fsdp'), may hold values from -3 to 3
- conv_bias: bfloat16 [2, 3328], P('section', 'fsdp'), may hold values from -3 to 3
- step_bias: bfloat16 [2, 48], P('section', 'fsdp'), may hold values from -5 to -2
- log_decay: bfloat16 [2, 48], P('section', 'fsdp'), may hold values from -8 to 0
- skip_gain: bfloat16 [2, 48], P('section', 'fsdp'), may hold values from 0.5 to 2
- gate_gain: bfloat16 [2, 3072], P('section', 'fsdp'), may hold values from 0.5 to 1.5
- out_weight: bfloat16 [2, 3072, 1536], P('section', 'fsdp'), may hold values from -0.109375 to 0.109375
Outputs:
- section_results: float32 [2, 2, 4, 1024, 1536], P('section', None, 'fsdp', 'seq')
- grad_norm_gain: float32 [2, 1536], P('section', 'fsdp')
- grad_in_weight: float32 [2, 1536, 6448], P('section', 'fsdp')
- grad_conv_weight: float32 [2, 4, 3328], P('section', None, 'fsdp')
- grad_conv_bias: float32 [2, 3328], P('section', 'fsdp')
- grad_step_bias: float32 [2, 48], P('section', 'fsdp')
- grad_log_decay: float32 [2, 48], P('section', 'fsdp')
- grad_skip_gain: float32 [2, 48], P('section', 'fsdp')
- grad_gate_gain: float32 [2, 3072], P('section', 'fsdp')
- grad_out_weight: float32 [2, 3072, 1536], P('section', 'fsdp')
The draws below stay inside these ranges and needn't reach their ends.
All inputs are finite; a program needn't handle non-finite values.
Results may differ from the reference program's by a relative error of at most 0.038.
Values may be sent and summed in bfloat16 or wider, within the bound.
A program may use at most 384 MiB of HBM per device.

```python
import jax
import jax.numpy as jnp
from jax import lax

D = 1536
H = 48
P_SIZE = 64
NS = 128
CONVK = 4
SPAN = 256
MICRO = 2
DI = 3072
CONVCH = 3328
PROJ = 6448
LEN = 1024
GROUPS = 4
LAYERS = 2


def level_of(rng, extent, shards, smallest, top_value):
    def one(dim, blocks):
        draws = jax.random.uniform(jax.random.fold_in(jax.random.fold_in(rng, 6), dim), (blocks,), jnp.float32, smallest / len(shards), top_value / len(shards))
        return jnp.repeat(jnp.exp(draws), extent[dim] // blocks).reshape((-1,) + (1,) * (len(extent) - dim - 1))

    factor_of = one(*shards[0])
    for cut in shards[1:]:
        factor_of = factor_of * one(*cut)
    return factor_of


def gaussian(stream_key, shape, scale, limit, cuts=(), kind=jnp.bfloat16):
    drawn = scale * jax.random.normal(stream_key, shape, jnp.float32)
    if cuts:
        drawn = drawn * level_of(stream_key, shape, cuts, -0.22, 0.18)
    return jnp.clip(drawn, -limit, limit).astype(kind)


def setup_inputs(seed: int = 0) -> dict:
    seeds = jax.random.split(jax.random.key(seed), 11)
    section_ends = gaussian(seeds[0], (LAYERS, MICRO, GROUPS, LEN, D), 1.0, 6.0, ((0, 2), (2, 4), (3, 4)))
    norm_gain = jnp.clip(1.0 + 0.1 * jax.random.normal(seeds[1], (LAYERS, D), jnp.float32), 0.5, 1.5).astype(jnp.bfloat16)
    in_weight = gaussian(seeds[2], (LAYERS, D, PROJ), D ** -0.5, 0.15625, ((0, 2), (1, 4)))
    conv_weight = gaussian(seeds[3], (LAYERS, CONVK, CONVCH), CONVK ** -0.5, 3.0, ((0, 2), (2, 4)))
    conv_bias = gaussian(seeds[4], (LAYERS, CONVCH), 0.5, 3.0, ((0, 2), (1, 4)))
    step_bias = jnp.clip(-5.0 + 3.0 * jax.random.uniform(seeds[5], (LAYERS, H), jnp.float32) ** level_of(seeds[5], (LAYERS, H), ((0, 2), (1, 4)), -0.2, 0.2), -5.0, -2.0).astype(jnp.bfloat16)
    log_decay = jnp.clip(-8.0 + 8.0 * jax.random.uniform(seeds[6], (LAYERS, H), jnp.float32) ** level_of(seeds[6], (LAYERS, H), ((0, 2), (1, 4)), -0.2, 0.2), -8.0, 0.0).astype(jnp.bfloat16)
    skip_gain = jnp.clip(0.5 + 1.5 * jax.random.uniform(seeds[7], (LAYERS, H), jnp.float32) ** level_of(seeds[7], (LAYERS, H), ((0, 2), (1, 4)), -0.2, 0.2), 0.5, 2.0).astype(jnp.bfloat16)
    gate_gain = jnp.clip(1.0 + 0.1 * jax.random.normal(seeds[8], (LAYERS, DI), jnp.float32), 0.5, 1.5).astype(jnp.bfloat16)
    out_weight = gaussian(seeds[9], (LAYERS, DI, D), DI ** -0.5, 0.109375, ((0, 2), (1, 4)))
    return dict(section_ends=section_ends, norm_gain=norm_gain, in_weight=in_weight, conv_weight=conv_weight, conv_bias=conv_bias, step_bias=step_bias, log_decay=log_decay, skip_gain=skip_gain, gate_gain=gate_gain, out_weight=out_weight)


epsilon = 1e-05
highest = lax.Precision.HIGHEST

@jax.custom_vjp
def low(v):
    return lax.optimization_barrier(v.astype(jnp.bfloat16)).astype(jnp.float32)

@jax.custom_vjp
def low_back(v):
    return v

def low_keep(v):
    return (low(v), None)

def low_pass(kept, grad):
    return (grad,)

def back_keep(v):
    return (v, None)

def back_low(kept, grad):
    return (low(grad),)
low.defvjp(low_keep, low_pass)
low_back.defvjp(back_keep, back_low)

def round_both(value):
    return low_back(low(value))

def rms_scale(value):
    return value * lax.rsqrt(lax.optimization_barrier(jnp.mean(value * value, axis=-1, keepdims=True)) + epsilon)

def pre_norm(hidden, norm_gain):
    return rms_scale(hidden) * norm_gain

def post_norm(result, gate_part, gate_gain):
    return rms_scale(result * jax.nn.silu(gate_part)) * gate_gain

def conv_part(padded, conv_weight, conv_bias):
    length = padded.shape[0] - (conv_weight.shape[0] - 1)
    running = conv_bias + conv_weight[0] * padded[0:length]
    for offset in range(1, conv_weight.shape[0]):
        running = running + conv_weight[offset] * padded[offset:offset + length]
    return jax.nn.silu(running)

def decays(scores, b_rows, dt_raw, step_bias, log_decay):
    blocks, block_len = (scores.shape[0], scores.shape[1])
    dt_value = jax.nn.softplus(dt_raw + step_bias)
    log_rate = -dt_value * jnp.exp(log_decay)
    dt_value = jnp.transpose(dt_value.reshape(blocks, block_len, -1), (0, 2, 1))
    log_rate = jnp.transpose(log_rate.reshape(blocks, block_len, -1), (0, 2, 1))
    triangle = jnp.tril(jnp.ones((block_len, block_len), jnp.float32))
    cumulative = jnp.einsum('chj,ij->chi', log_rate, triangle, precision=highest)
    inside = triangle > 0.5
    spread = cumulative[:, :, :, None] - cumulative[:, :, None, :]
    fading_inner = jnp.where(inside, jnp.exp(jnp.where(inside, spread, 0.0)), 0.0)
    mixing = scores[:, None, :, :] * fading_inner * dt_value[:, :, None, :]
    tail = jnp.exp(cumulative[:, :, -1:] - cumulative) * dt_value
    weighted = b_rows[:, None, :, :] * tail[:, :, :, None]
    return (mixing, weighted, jnp.exp(cumulative), jnp.exp(cumulative[:, :, -1]))

def carry_states(local_part, fading):

    def advance(carried, inputs):
        block_part, fade_now = inputs
        return (fade_now[:, None, None] * carried + block_part, carried)
    initial = jnp.zeros(local_part.shape[1:], local_part.dtype)
    finished, entering = lax.scan(advance, initial, (local_part, fading))
    return entering

def mixer(head_in, b_all, c_all, dt_raw, step_bias, log_decay, skip_gain):
    length = head_in.shape[0]
    blocks = length // SPAN
    head_rows = head_in.reshape(blocks, SPAN, H, P_SIZE)
    b_rows = b_all.reshape(blocks, SPAN, NS)
    c_rows = c_all.reshape(blocks, SPAN, NS)
    scores = low_back(jnp.einsum('cin,cjn->cij', c_rows, b_rows, precision=highest))
    mixing, weighted, growth, fading = decays(scores, b_rows, dt_raw, step_bias, log_decay)
    mixing = low(mixing)
    weighted = low(weighted)
    within = jnp.einsum('chij,cjhp->cihp', mixing, head_rows, precision=highest)
    local_part = low_back(jnp.einsum('cjhp,chjn->chpn', head_rows, weighted, precision=highest))
    entering = low(carry_states(local_part, fading))
    reach_part = low_back(jnp.einsum('cin,chpn->cihp', c_rows, entering, precision=highest))
    growth_rows = jnp.transpose(growth, (0, 2, 1))[:, :, :, None]
    result = within + growth_rows * reach_part + skip_gain[:, None] * head_rows
    return result.reshape(length, H * P_SIZE)

def layer(hidden, params):
    norm_gain, in_weight, conv_weight, conv_bias, step_bias, log_decay, skip_gain, gate_gain, out_weight = params
    normed = low(pre_norm(hidden, norm_gain))
    projected = round_both(jnp.dot(normed, in_weight, precision=highest))
    gate_part = projected[:, :DI]
    before = projected[:, DI:DI + CONVCH]
    dt_raw = projected[:, DI + CONVCH:]
    padded = jnp.concatenate([jnp.zeros((CONVK - 1, CONVCH), hidden.dtype), before], 0)
    mixed_in = round_both(conv_part(padded, conv_weight, conv_bias))
    head_in = mixed_in[:, :DI]
    b_all = mixed_in[:, DI:DI + NS]
    c_all = mixed_in[:, DI + NS:]
    result = round_both(mixer(head_in, b_all, c_all, dt_raw, step_bias, log_decay, skip_gain))
    normed_out = low(post_norm(result, gate_part, gate_gain))
    branch = low_back(jnp.dot(normed_out, out_weight, precision=highest))
    return hidden + branch

def reference(section_ends, norm_gain, in_weight, conv_weight, conv_bias, step_bias, log_decay, skip_gain, gate_gain, out_weight):
    inputs = section_ends[0].astype(jnp.float32).reshape(MICRO * GROUPS, LEN, D)
    cotangent = section_ends[1].astype(jnp.float32).reshape(MICRO * GROUPS, LEN, D)
    weights = (norm_gain.astype(jnp.float32), in_weight.astype(jnp.float32), conv_weight.astype(jnp.float32), conv_bias.astype(jnp.float32), step_bias.astype(jnp.float32), log_decay.astype(jnp.float32), skip_gain.astype(jnp.float32), gate_gain.astype(jnp.float32), out_weight.astype(jnp.float32))

    def forward(sequences, params):

        def run_both(value):
            first = layer(value, tuple((member[0] for member in params)))
            passed = round_both(first)
            return layer(passed, tuple((member[1] for member in params)))
        return lax.map(jax.checkpoint(run_both), sequences)
    output, pullback = jax.vjp(forward, inputs, weights)
    grad_inputs, grad_weights = pullback(cotangent)
    section_results = jnp.stack([grad_inputs, output]).reshape(2, MICRO, GROUPS, LEN, D)
    return (section_results, grad_weights[0], grad_weights[1], grad_weights[2], grad_weights[3], grad_weights[4], grad_weights[5], grad_weights[6], grad_weights[7], grad_weights[8])
```

```python
import functools

import jax
import jax.numpy as jnp
import numpy as np
from jax import lax
from jax.experimental import pallas as pl
from jax.experimental.pallas import tpu as pltpu
from jax.sharding import PartitionSpec as P

SPAN = 256
HEAD = 64
STATE = 128
EPS = 1e-05
F32 = jnp.float32
BF16 = jnp.bfloat16


def dot(a, b, ca, cb):
    return lax.dot_general(a, b, (((ca,), (cb,)), ((), ())), preferred_element_type=F32)


def split3(v):
    hi = v.astype(BF16)
    rest = v - hi.astype(F32)
    mid = rest.astype(BF16)
    low = (rest - mid.astype(F32)).astype(BF16)
    return hi, mid, low


def sigmoid(v):
    return 1.0 / (1.0 + jnp.exp(-v))


def running_conv(pad_ref, vec_ref, taps):
    run = vec_ref[taps : taps + 1, :] + vec_ref[0:1, :] * pad_ref[pl.ds(8 - taps + 1, SPAN), :]
    for k in range(1, taps):
        run = run + vec_ref[k : k + 1, :] * pad_ref[pl.ds(8 - taps + 1 + k, SPAN), :]
    return run


def step_sizes(dt_raw, vec_ref, tri):
    x = dt_raw + vec_ref[6:7, :STATE]
    e = jnp.exp(-jnp.abs(x))
    dt = jnp.maximum(x, 0.0) + jnp.log1p(e)
    decay = jnp.exp(vec_ref[7:8, :STATE])
    rate = -dt * decay
    hi, mid, low = split3(rate)
    packed = dot(tri, jnp.concatenate([hi, mid, low], 1), 1, 0)
    cum = packed[:, :STATE] + packed[:, STATE : 2 * STATE] + packed[:, 2 * STATE :]
    return x, e, dt, decay, rate, cum


def expand(v, spread3):
    return dot(jnp.concatenate(split3(v), 1), spread3, 1, 0)


def per_head(v, gather3):
    return dot(jnp.concatenate(split3(v), 1), gather3, 1, 0)


def fading(cum, cum_t, dt_t, h, inside):
    spread = cum[:, h : h + 1] - cum_t[h : h + 1, :]
    return jnp.exp(jnp.where(inside, spread, -1e30)) * dt_t[h : h + 1, :]


def inside_mask():
    rows = lax.broadcasted_iota(jnp.int32, (SPAN, SPAN), 0)
    cols = lax.broadcasted_iota(jnp.int32, (SPAN, SPAN), 1)
    return cols <= rows


def forward_kernel(
    heads, blocks, taps,
    full_ref, wgx_ref, ws_ref, wo_ref, vec_ref, tri_ref, spread_ref,
    part_ref, ss_ref, pgx_ref, ps_ref, res_ref, ent_ref,
    pad_ref, state_ref, within_ref,
):
    cw = heads * HEAD
    first = lax.rem(pl.program_id(0), blocks) == 0

    @pl.when(first)
    def _():
        pad_ref[pl.ds(SPAN, 8), :] = jnp.zeros((8, pad_ref.shape[1]), F32)
        state_ref[...] = jnp.zeros_like(state_ref)

    x = full_ref[...]
    pgx = dot(x, wgx_ref[...], 1, 0).astype(BF16)
    ps = dot(x, ws_ref[...], 1, 0).astype(BF16)
    pgx_ref[...] = pgx
    ps_ref[...] = ps
    pad_ref[pl.ds(0, 8), :] = pad_ref[pl.ds(SPAN, 8), :]
    pad_ref[pl.ds(8, SPAN), :cw] = pgx[:, cw:].astype(F32)
    pad_ref[pl.ds(8, SPAN), cw:] = ps[:, : 2 * STATE].astype(F32)
    run = running_conv(pad_ref, vec_ref, taps)
    mixed = (run * sigmoid(run)).astype(BF16)
    xs, b, c = mixed[:, :cw], mixed[:, cw : cw + STATE], mixed[:, cw + STATE :]
    _, _, dt, _, _, cum = step_sizes(ps[:, 2 * STATE :].astype(F32), vec_ref, tri_ref[...])
    cum_t, dt_t = cum.T, dt.T
    inside = inside_mask()
    scores = dot(c, b, 1, 1)
    for h in range(heads):
        mixing = (scores * fading(cum, cum_t, dt_t, h, inside)).astype(BF16)
        within_ref[:, h * HEAD : (h + 1) * HEAD] = dot(mixing, xs[:, h * HEAD : (h + 1) * HEAD], 1, 0)
    tail = jnp.exp(cum[SPAN - 1 : SPAN, :] - cum) * dt
    growth = jnp.exp(cum)
    both = expand(jnp.concatenate([tail, growth], 0), spread_ref[...])
    tail_e, growth_e = both[:SPAN], both[SPAN:]
    xs_f = xs.astype(F32)
    state = state_ref[...]
    state_low = state.astype(BF16)
    ent_ref[0] = state_low
    reach = dot(c, state_low, 1, 0)
    state_ref[...] = growth_e[SPAN - 1 : SPAN, :] * state + dot(b, (xs_f * tail_e).astype(BF16), 0, 0)
    result = (within_ref[...] + growth_e * reach + vec_ref[8:9, :cw] * xs_f).astype(BF16)
    res_ref[...] = result
    gate = pgx[:, :cw].astype(F32)
    g = result.astype(F32) * (gate * sigmoid(gate))
    ss = jnp.sum(g * g, axis=1, keepdims=True)
    ss_ref[0] = jnp.broadcast_to(ss, (SPAN, STATE)).T[:8, :]
    part_ref[...] = dot((g * vec_ref[5:6, :cw]).astype(BF16), wo_ref[...], 1, 0).astype(BF16)


def backward_kernel(
    heads, blocks, taps,
    gb_ref, sc_ref, pgx_ref, ps_ref, hgx_ref, hs_ref, res_ref, ent_ref,
    wgx_ref, ws_ref, wo_ref, vec_ref, tri_ref, spread_ref, gather_ref,
    pg_ref, gpgx_ref, gps_ref, no_ref, small_ref,
    pad_ref, next_ref, ge_ref, within_ref, gxm_ref,
):
    cw = heads * HEAD
    step = pl.program_id(0)
    place = lax.rem(step, blocks)

    @pl.when(step == 0)
    def _():
        small_ref[...] = jnp.zeros_like(small_ref)

    @pl.when(place == 0)
    def _():
        next_ref[pl.ds(0, 8), :] = jnp.zeros((8, next_ref.shape[1]), F32)
        ge_ref[...] = jnp.zeros_like(ge_ref)

    pgx, ps = pgx_ref[...], ps_ref[...]
    keep = jnp.where(place == blocks - 1, 0.0, 1.0)
    pad_ref[pl.ds(0, 8), :cw] = hgx_ref[8:, cw:].astype(F32) * keep
    pad_ref[pl.ds(0, 8), cw:] = hs_ref[8:, : 2 * STATE].astype(F32) * keep
    pad_ref[pl.ds(8, SPAN), :cw] = pgx[:, cw:].astype(F32)
    pad_ref[pl.ds(8, SPAN), cw:] = ps[:, : 2 * STATE].astype(F32)
    run = running_conv(pad_ref, vec_ref, taps)
    sig = sigmoid(run)
    mixed = (run * sig).astype(BF16)
    slope = sig * (1.0 + run * (1.0 - sig))
    xs, b, c = mixed[:, :cw], mixed[:, cw : cw + STATE], mixed[:, cw + STATE :]
    xs_f = xs.astype(F32)
    tri = tri_ref[...]
    x, e, dt, decay, rate, cum = step_sizes(ps[:, 2 * STATE :].astype(F32), vec_ref, tri)
    cum_t, dt_t = cum.T, dt.T
    tail = jnp.exp(cum[SPAN - 1 : SPAN, :] - cum) * dt
    growth = jnp.exp(cum)
    both = expand(jnp.concatenate([tail, growth], 0), spread_ref[...])
    tail_e, growth_e = both[:SPAN], both[SPAN:]

    gb = gb_ref[...]
    gu = dot(gb, wo_ref[...], 1, 1)
    columns = jnp.concatenate([sc_ref[0]] * (STATE // 8), 0).T
    r, pull = columns[:, 0:1], columns[:, 1:2]
    gain = vec_ref[5:6, :cw]
    gate = pgx[:, :cw].astype(F32)
    sg = sigmoid(gate)
    sl = gate * sg
    res = res_ref[...].astype(F32)
    g = res * sl
    rg = r * g
    no_ref[...] = (rg * gain).astype(BF16)
    dg = r * (gu * gain) - pull * g
    gr = (dg * sl).astype(BF16)
    gr_f = gr.astype(F32)
    ggate = dg * res * (sg + sl * (1.0 - sg))

    ent = ent_ref[0]
    ge = ge_ref[...]
    gl = ge.astype(BF16)
    reach = dot(c, ent, 1, 0)
    pulled = tail_e * dot(b, gl, 1, 0)
    gq = (growth_e * gr_f).astype(BF16)
    grad_c = dot(gq, ent, 1, 1)
    grad_b = dot((xs_f * tail_e).astype(BF16), gl, 1, 1)
    fade = growth_e[SPAN - 1 : SPAN, :]
    ge_ref[...] = fade * ge + dot(c, gq, 0, 0)
    grad_fade = fade * jnp.sum(ge * ent.astype(F32), axis=0, keepdims=True)
    inside = inside_mask()
    scores = dot(c, b, 1, 1)
    gs = jnp.zeros((SPAN, SPAN), F32)
    for h in range(heads):
        cols = slice(h * HEAD, (h + 1) * HEAD)
        fade_in = fading(cum, cum_t, dt_t, h, inside)
        mixing = (scores * fade_in).astype(BF16)
        gs = gs + dot(gr[:, cols], xs[:, cols], 1, 1) * fade_in
        within_ref[:, cols] = dot(mixing, xs[:, cols], 1, 0)
        gxm_ref[:, cols] = dot(mixing, gr[:, cols], 0, 0)
    gs = gs.astype(BF16)
    grad_c = grad_c + dot(gs, b, 1, 0)
    grad_b = grad_b + dot(gs, c, 0, 0)
    gxm = gxm_ref[...]
    grad_x = vec_ref[8:9, :cw] * gr_f + pulled + gxm

    gather = gather_ref[...]
    tall = jnp.concatenate([gr_f * (within_ref[...] + growth_e * reach), xs_f * gxm, xs_f * pulled], 0)
    sums = per_head(tall, gather)
    s1, s2, s3 = sums[:SPAN], sums[SPAN : 2 * SPAN], sums[2 * SPAN :]
    thin = jnp.concatenate(
        [jnp.sum(gr_f * xs_f, axis=0, keepdims=True), grad_fade, jnp.zeros((6, cw), F32)], 0
    )
    thin = per_head(thin, gather)
    hi, mid, low = split3(s1 - s2 - s3)
    packed = dot(tri, jnp.concatenate([hi, mid, low], 1), 0, 0)
    grad_rate = packed[:, :STATE] + packed[:, STATE : 2 * STATE] + packed[:, 2 * STATE :]
    grad_rate = grad_rate + (jnp.sum(s3, axis=0, keepdims=True) + thin[1:2, :])
    denominator = 1.0 + e
    slope_x = jnp.where(x >= 0, 1.0, e) / denominator
    ratio = jnp.where(x < -20.0, 1.0, slope_x / jnp.maximum(dt, 1e-12))
    grad_raw = (s2 + s3) * ratio - decay * grad_rate * slope_x
    small_ref[6:7, :STATE] += jnp.sum(grad_raw, axis=0, keepdims=True)
    small_ref[7:8, :STATE] += jnp.sum(grad_rate * rate, axis=0, keepdims=True)
    small_ref[8:9, :STATE] += thin[0:1, :]
    small_ref[5:6, :cw] += jnp.sum(gu * rg, axis=0, keepdims=True)

    grun = jnp.concatenate([grad_x, grad_b, grad_c], 1) * slope
    next_ref[pl.ds(SPAN, 8), :] = next_ref[pl.ds(0, 8), :]
    next_ref[pl.ds(0, SPAN), :] = grun
    small_ref[taps : taps + 1, :] += jnp.sum(grun, axis=0, keepdims=True)
    gbefore = jnp.zeros_like(grun)
    for k in range(taps):
        small_ref[k : k + 1, :] += jnp.sum(
            grun * pad_ref[pl.ds(8 - taps + 1 + k, SPAN), :], axis=0, keepdims=True
        )
        gbefore = gbefore + vec_ref[k : k + 1, :] * next_ref[pl.ds(taps - 1 - k, SPAN), :]
    gpgx = jnp.concatenate([ggate, gbefore[:, :cw]], 1).astype(BF16)
    gps = jnp.concatenate([gbefore[:, cw:], grad_raw], 1).astype(BF16)
    gpgx_ref[...] = gpgx
    gps_ref[...] = gps
    pg_ref[...] = (dot(gpgx, wgx_ref[...], 1, 1) + dot(gps, ws_ref[...], 1, 1)).astype(BF16)


def tables(heads):
    cw = heads * HEAD
    tri = np.tril(np.ones((SPAN, SPAN), np.float32))
    one = (np.arange(cw)[None, :] // HEAD == np.arange(STATE)[:, None]).astype(np.float32)
    spread3 = np.concatenate([one] * 3, 0)
    gather3 = np.concatenate([one.T] * 3, 0)
    return jnp.asarray(tri, BF16), jnp.asarray(spread3, BF16), jnp.asarray(gather3, BF16)


def whole(a):
    return pl.BlockSpec(memory_space=pltpu.VMEM)


def layer_forward(full, wgx, ws, wo, vec, taps, sequences):
    tokens, width = full.shape
    cw = wo.shape[0]
    heads = cw // HEAD
    steps = tokens // SPAN
    blocks = steps // sequences
    tri, spread3, _ = tables(heads)
    rows = lambda w: pl.BlockSpec((SPAN, w), lambda t: (t, 0))
    chans = cw + 2 * STATE
    return pl.pallas_call(
        functools.partial(forward_kernel, heads, blocks, taps),
        grid=(steps,),
        in_specs=[rows(width)] + [whole(a) for a in (wgx, ws, wo, vec, tri, spread3)],
        out_specs=[
            rows(width),
            pl.BlockSpec((1, 8, SPAN), lambda t: (t, 0, 0)),
            rows(2 * cw),
            rows(3 * STATE),
            rows(cw),
            pl.BlockSpec((1, STATE, cw), lambda t: (t, 0, 0)),
        ],
        out_shape=[
            jax.ShapeDtypeStruct((tokens, width), BF16),
            jax.ShapeDtypeStruct((steps, 8, SPAN), F32),
            jax.ShapeDtypeStruct((tokens, 2 * cw), BF16),
            jax.ShapeDtypeStruct((tokens, 3 * STATE), BF16),
            jax.ShapeDtypeStruct((tokens, cw), BF16),
            jax.ShapeDtypeStruct((steps, STATE, cw), BF16),
        ],
        scratch_shapes=[
            pltpu.VMEM((SPAN + 8, chans), F32),
            pltpu.VMEM((STATE, cw), F32),
            pltpu.VMEM((SPAN, cw), F32),
        ],
        compiler_params=pltpu.CompilerParams(vmem_limit_bytes=48 << 20),
        cost_estimate=pl.CostEstimate(
            flops=2 * tokens * width * (3 * cw + 3 * STATE) + 2 * tokens * cw * 700,
            bytes_accessed=4 * tokens * width + 2 * width * (3 * cw + 3 * STATE) + 8 * tokens * cw,
            transcendentals=tokens * SPAN * heads,
        ),
        name="layer_forward",
    )(full, wgx, ws, wo, vec, tri, spread3)


def layer_backward(gb, sc, pgx, ps, res, ent, wgx, ws, wo, vec, taps, sequences):
    tokens, width = gb.shape
    cw = wo.shape[0]
    heads = cw // HEAD
    steps = tokens // SPAN
    blocks = steps // sequences
    tri, spread3, gather3 = tables(heads)
    chans = cw + 2 * STATE

    def at(t):
        return t - lax.rem(t, blocks) + (blocks - 1 - lax.rem(t, blocks))

    rows = lambda w: pl.BlockSpec((SPAN, w), lambda t: (at(t), 0))
    edge = lambda w: pl.BlockSpec((16, w), lambda t: (jnp.maximum(at(t) * (SPAN // 16) - 1, 0), 0))
    return pl.pallas_call(
        functools.partial(backward_kernel, heads, blocks, taps),
        grid=(steps,),
        in_specs=[
            rows(width),
            pl.BlockSpec((1, 8, SPAN), lambda t: (at(t), 0, 0)),
            rows(2 * cw),
            rows(3 * STATE),
            edge(2 * cw),
            edge(3 * STATE),
            rows(cw),
            pl.BlockSpec((1, STATE, cw), lambda t: (at(t), 0, 0)),
        ]
        + [whole(a) for a in (wgx, ws, wo, vec, tri, spread3, gather3)],
        out_specs=[
            rows(width),
            rows(2 * cw),
            rows(3 * STATE),
            rows(cw),
            pl.BlockSpec((16, chans), lambda t: (0, 0)),
        ],
        out_shape=[
            jax.ShapeDtypeStruct((tokens, width), BF16),
            jax.ShapeDtypeStruct((tokens, 2 * cw), BF16),
            jax.ShapeDtypeStruct((tokens, 3 * STATE), BF16),
            jax.ShapeDtypeStruct((tokens, cw), BF16),
            jax.ShapeDtypeStruct((16, chans), F32),
        ],
        scratch_shapes=[
            pltpu.VMEM((SPAN + 8, chans), F32),
            pltpu.VMEM((SPAN + 8, chans), F32),
            pltpu.VMEM((STATE, cw), F32),
            pltpu.VMEM((SPAN, cw), F32),
            pltpu.VMEM((SPAN, cw), F32),
        ],
        compiler_params=pltpu.CompilerParams(vmem_limit_bytes=48 << 20),
        cost_estimate=pl.CostEstimate(
            flops=2 * tokens * width * (3 * cw + 3 * STATE) + 2 * tokens * cw * 2000,
            bytes_accessed=4 * tokens * width + 2 * width * (3 * cw + 3 * STATE) + 8 * tokens * cw,
            transcendentals=tokens * SPAN * heads,
        ),
        name="layer_backward",
    )(gb, sc, pgx, ps, pgx, ps, res, ent, wgx, ws, wo, vec, tri, spread3, gather3)


def swapped(value, axis):
    count = lax.axis_size(axis)
    return lax.ppermute(value, axis, [(i, count - 1 - i) for i in range(count)])


PLANE = ("section", "seq")
EVERY = ("section", "seq", "fsdp")


def per_device(
    section_ends, norm_gain, in_weight, conv_weight, conv_bias, step_bias, log_decay, skip_gain, gate_gain, out_weight
):
    sec, seq, dep = lax.axis_index("section"), lax.axis_index("seq"), lax.axis_index("fsdp")
    layers, ranks, depth = lax.axis_size("section"), lax.axis_size("seq"), lax.axis_size("fsdp")
    group = layers * ranks
    here = sec * ranks + seq
    there = (layers - 1 - sec) * ranks + seq
    low_layer = sec == 0
    width = in_weight.shape[1] * depth
    inner = gate_gain.shape[1] * depth
    chans = conv_bias.shape[1] * depth
    heads_all = step_bias.shape[1] * depth
    taps = conv_weight.shape[1]
    cw = inner // group
    heads = cw // HEAD
    shared = 2 * STATE

    ends = section_ends[0, :, 0]
    sent = jnp.where(low_layer, ends[1], ends[0])
    got = swapped(sent, "section")
    hidden = jnp.where(low_layer, ends[0], got).astype(F32)
    cot = jnp.where(low_layer, got, ends[1]).astype(F32)
    local = hidden.shape[0]

    flat = [norm_gain, conv_weight, conv_bias, step_bias, log_decay, skip_gain, gate_gain]
    sizes = [v.size for v in flat]
    packed = jnp.concatenate([v.reshape(-1) for v in flat])
    packed = lax.all_gather(packed, ("section", "fsdp")).reshape(layers, depth, -1).astype(F32)

    def member(layer, number):
        begin = sum(sizes[:number])
        return packed[layer, :, begin : begin + sizes[number]]

    def head_columns(v, begin, count):
        return lax.dynamic_slice_in_dim(v, begin, count, v.ndim - 1)

    def vectors(layer):
        kernel = jnp.transpose(member(layer, 1).reshape(depth, taps, -1), (1, 0, 2)).reshape(taps, chans)
        rows = jnp.concatenate([kernel, member(layer, 2).reshape(1, chans)], 0)
        rows = jnp.concatenate([head_columns(rows, here * cw, cw), rows[:, inner:]], 1)
        total = cw + shared

        def padded(v):
            return jnp.pad(v[None], ((0, 0), (0, total - v.shape[0])))

        gain = head_columns(member(layer, 6).reshape(-1), here * cw, cw)
        by_head = [head_columns(member(layer, n).reshape(-1), here * heads, heads) for n in (3, 4, 5)]
        return jnp.concatenate(
            [rows, jnp.zeros((5 - taps - 1, total), F32), padded(gain), padded(by_head[0]), padded(by_head[1]),
             padded(jnp.repeat(by_head[2], HEAD)), jnp.zeros((7, total), F32)], 0)

    gains = [member(layer, 0).reshape(1, -1) for layer in range(layers)]
    vecs = [vectors(layer) for layer in range(layers)]

    def own_columns(rank):
        return jnp.concatenate(
            [head_columns(in_weight[0], rank * cw, cw), head_columns(in_weight[0], inner + rank * cw, cw)], 1
        )

    out_rows = out_weight.shape[1]

    def own_rows(rank):
        start = rank * cw - dep * out_rows
        inside = (start >= 0) & (start < out_rows)
        block = lax.dynamic_slice_in_dim(out_weight[0], jnp.clip(start, 0, out_rows - cw), cw, 0)
        return jnp.where(inside, block, jnp.zeros_like(block))

    mine, theirs = own_columns(here), swapped(own_columns(there), "section")
    mine_o, theirs_o = own_rows(here), swapped(own_rows(there), "section")
    piece = in_weight.shape[1] // ranks
    thin = lax.dynamic_slice(in_weight[0], (seq * piece, inner + chans - shared), (piece, shared + heads_all))
    thin = lax.all_gather(thin, ("section", "fsdp", "seq"), axis=0, tiled=True).reshape(layers, width, -1)
    weights = []
    for layer in range(layers):
        own = low_layer if layer == 0 else ~low_layer
        wgx = lax.all_gather(jnp.where(own, mine, theirs), "fsdp", axis=0, tiled=True)
        wo = lax.psum(jnp.where(own, mine_o, theirs_o), "fsdp")
        steps_w = head_columns(thin[layer, :, shared:], here * heads, heads)
        ws = jnp.concatenate([thin[layer, :, :shared], steps_w, jnp.zeros((width, STATE - heads), BF16)], 1)
        weights.append((wgx, ws, wo))

    def spread_rows(v):
        return lax.all_gather(v, PLANE, axis=0, tiled=True)

    def collect_rows(v):
        return lax.psum_scatter(v, PLANE, scatter_dimension=0, tiled=True).astype(F32)

    saved = []
    for layer in range(layers):
        wgx, ws, wo = weights[layer]
        rs = lax.rsqrt(jnp.mean(hidden * hidden, axis=-1, keepdims=True) + EPS)
        full = spread_rows((hidden * rs * gains[layer]).astype(BF16))
        part, ss, pgx, ps, res, ent = layer_forward(full, wgx, ws, wo, vecs[layer], taps, layers)
        raw = collect_rows(part)
        ss = lax.psum_scatter(ss[:, 0, :].reshape(-1), PLANE, scatter_dimension=0, tiled=True)[:, None]
        r = lax.rsqrt(ss / inner + EPS)
        saved.append((hidden, rs, full, pgx, ps, res, ent, raw, r))
        hidden = hidden + r * raw
        if layer + 1 < layers:
            hidden = hidden.astype(BF16).astype(F32)
    output = hidden

    grad = cot
    big, small = [None] * layers, [None] * layers
    for layer in reversed(range(layers)):
        wgx, ws, wo = weights[layer]
        before, rs, full, pgx, ps, res, ent, raw, r = saved[layer]
        low = grad.astype(BF16)
        pull = r * r * r * jnp.sum(low.astype(F32) * raw, axis=-1, keepdims=True) / inner
        sc = jnp.concatenate([r.T, pull.T, jnp.zeros((6, local), F32)], 0)
        gb = spread_rows(low)
        sc = lax.all_gather(sc, PLANE).reshape(-1, 8, local)
        if local != SPAN:
            sc = jnp.transpose(sc.reshape(-1, 8, local // SPAN, SPAN), (0, 2, 1, 3)).reshape(-1, 8, SPAN)
        pg, gpgx, gps, no, tiny = layer_backward(
            gb, sc, pgx, ps, res, ent, wgx, ws, wo, vecs[layer], taps, layers
        )
        g_gx = dot(full, gpgx, 0, 0).astype(BF16)
        g_s = dot(full, gps, 0, 0).astype(BF16)
        g_o = dot(no, gb, 0, 0).astype(BF16)
        gn = collect_rows(pg)
        unit = before * rs
        g_gain = jnp.sum(gn * unit, axis=0)
        gn = gn * gains[layer]
        grad = grad + rs * (gn - unit * jnp.mean(gn * unit, axis=-1, keepdims=True))
        if layer > 0:
            grad = grad.astype(BF16).astype(F32)

        def placed(v, count, begin):
            return lax.dynamic_update_slice(jnp.zeros((count,), F32), v, (begin,))

        conv = lax.dynamic_update_slice(jnp.zeros((taps + 1, chans), F32), tiny[: taps + 1, :cw], (0, here * cw))
        conv = conv + jnp.pad(tiny[: taps + 1, cw:], ((0, 0), (inner, 0)))
        small[layer] = jnp.concatenate(
            [g_gain, conv.reshape(-1), placed(tiny[5, :cw], inner, here * cw)]
            + [placed(tiny[n, :heads], heads_all, here * heads) for n in (6, 7, 8)]
        )
        g_gx = lax.psum_scatter(g_gx, "fsdp", scatter_dimension=0, tiled=True)
        steps_g = lax.dynamic_update_slice(jnp.zeros((width, heads_all), BF16), g_s[:, shared : shared + heads], (0, here * heads))
        g_s = jnp.concatenate([g_s[:, :shared], steps_g], 1)
        g_s = lax.psum_scatter(g_s, "fsdp", scatter_dimension=0, tiled=True)
        g_o = lax.psum(g_o, "fsdp")
        big[layer] = (g_gx, g_s, g_o)

    sent = jnp.where(low_layer, output, grad).astype(BF16)
    got = swapped(sent, "section").astype(F32)
    first = jnp.where(low_layer, grad, got)
    second = jnp.where(low_layer, got, output)
    section_results = jnp.stack([first, second])[None, :, None]

    def own_layer(values):
        own = jnp.where(low_layer, values[0], values[1])
        other = jnp.where(low_layer, values[1], values[0])
        return own, other

    own, other = own_layer([b[0] for b in big])
    other = swapped(other, "section")
    pair = jnp.stack([jnp.where(low_layer, own, other), jnp.where(low_layer, other, own)])
    gx = lax.all_gather(pair, "seq")
    gx = jnp.transpose(gx, (3, 1, 0, 2, 4)) if False else gx
    rows = gx.shape[2]
    gx = gx.reshape(ranks, layers, rows, 2, cw)
    gx = jnp.transpose(gx, (2, 3, 1, 0, 4)).reshape(rows, 2 * inner)
    s_all = lax.psum(jnp.stack([b[1] for b in big]), PLANE)
    s_own, _ = own_layer([s_all[0], s_all[1]])
    grad_in = jnp.concatenate([gx.astype(F32), s_own.astype(F32)], 1)[None]

    own, other = own_layer([b[2] for b in big])
    other = swapped(other, "section")
    pair = jnp.stack([jnp.where(low_layer, own, other), jnp.where(low_layer, other, own)])
    spread = jnp.zeros((out_rows, width), BF16)
    for s in range(layers):
        start = (s * ranks + seq) * cw - dep * out_rows
        inside = (start >= 0) & (start < out_rows)
        block = jnp.where(inside, pair[s], jnp.zeros_like(pair[s]))
        spread = spread + lax.dynamic_update_slice(jnp.zeros_like(spread), block, (jnp.clip(start, 0, out_rows - cw), 0))
    grad_out = lax.psum(spread, "seq").astype(F32)[None]

    tiny = lax.psum(jnp.stack(small), EVERY)
    tiny = jnp.where(low_layer, tiny[0], tiny[1])
    cuts = np.cumsum([0, width, taps * chans, chans, inner, heads_all, heads_all, heads_all])
    parts = [tiny[cuts[i] : cuts[i + 1]] for i in range(7)]

    def share(v):
        count = v.shape[-1] // depth
        return lax.dynamic_slice_in_dim(v, dep * count, count, v.ndim - 1)[None]

    return (
        section_results,
        share(parts[0]),
        grad_in,
        share(parts[1].reshape(taps, chans)),
        share(parts[2]),
        share(parts[4]),
        share(parts[5]),
        share(parts[6]),
        share(parts[3]),
        grad_out,
    )


def solution(mesh):
    weight = P("section", "fsdp")
    matrix = P("section", "fsdp", None)
    ends = P("section", None, "fsdp", "seq", None)
    kernel = P("section", None, "fsdp")
    return jax.shard_map(
        per_device,
        mesh=mesh,
        in_specs=(ends, weight, matrix, kernel, weight, weight, weight, weight, weight, matrix),
        out_specs=(ends, weight, matrix, kernel, weight, weight, weight, weight, weight, matrix),
        check_vma=False,
    )
```

```python
import functools

import jax
import jax.numpy as jnp
import numpy as np
from jax import lax
from jax.experimental import pallas as pl
from jax.experimental.pallas import tpu as pltpu
from jax.sharding import PartitionSpec as P

SPAN = 256
HEAD = 64
STATE = 128
EPS = 1e-05
F32 = jnp.float32
BF16 = jnp.bfloat16


def dot(a, b, ca, cb):
    return lax.dot_general(a, b, (((ca,), (cb,)), ((), ())), preferred_element_type=F32)


def split3(v):
    hi = v.astype(BF16)
    rest = v - hi.astype(F32)
    mid = rest.astype(BF16)
    low = (rest - mid.astype(F32)).astype(BF16)
    return hi, mid, low


def sigmoid(v):
    return 1.0 / (1.0 + jnp.exp(-v))


def running_conv(pad_ref, vec_ref, taps):
    run = vec_ref[taps : taps + 1, :] + vec_ref[0:1, :] * pad_ref[pl.ds(8 - taps + 1, SPAN), :]
    for k in range(1, taps):
        run = run + vec_ref[k : k + 1, :] * pad_ref[pl.ds(8 - taps + 1 + k, SPAN), :]
    return run


def step_sizes(dt_raw, vec_ref, tri):
    x = dt_raw + vec_ref[6:7, :STATE]
    e = jnp.exp(-jnp.abs(x))
    dt = jnp.maximum(x, 0.0) + jnp.log1p(e)
    decay = jnp.exp(vec_ref[7:8, :STATE])
    rate = -dt * decay
    hi, mid, low = split3(rate)
    packed = dot(tri, jnp.concatenate([hi, mid, low], 1), 1, 0)
    cum = packed[:, :STATE] + packed[:, STATE : 2 * STATE] + packed[:, 2 * STATE :]
    return x, e, dt, decay, rate, cum


def expand(v, spread3):
    return dot(jnp.concatenate(split3(v), 1), spread3, 1, 0)


def per_head(v, gather3):
    return dot(jnp.concatenate(split3(v), 1), gather3, 1, 0)


def fading(cum, cum_t, dt_t, h, inside):
    spread = cum[:, h : h + 1] - cum_t[h : h + 1, :]
    return jnp.exp(jnp.where(inside, spread, -1e30)) * dt_t[h : h + 1, :]


def inside_mask():
    rows = lax.broadcasted_iota(jnp.int32, (SPAN, SPAN), 0)
    cols = lax.broadcasted_iota(jnp.int32, (SPAN, SPAN), 1)
    return cols <= rows


MESH = pl.DeviceIdType.MESH


class Plane:
    def __init__(self, layers, ranks):
        self.layers, self.ranks = layers, ranks
        self.sec, self.seq = lax.axis_index("section"), lax.axis_index("seq")
        self.low = lax.rem(self.seq, 2)
        count = ranks.bit_length() - 1
        outer = list(range(1, count + 1))
        self.size = layers * ranks
        self.orders = (outer, outer[::-1])
        self.stages = len(outer)
        self.masks = [m for m in range(self.size) if m % 2 == 0]

    def weight(self, dim):
        return 1 if dim == 0 else 1 << (dim - 1)

    def flipped(self, dim):
        w = self.weight(dim)
        return self.seq + (1 - 2 * lax.rem(self.seq // w, 2)) * w

    def partner(self, dim):
        if dim == 1:
            return {"section": self.layers - 1 - self.sec}
        return {"seq": self.flipped(dim)}

    def owner(self, mask):
        seq = self.seq
        for dim in range(self.stages + 1):
            if dim != 1 and mask >> dim & 1:
                w = self.weight(dim)
                seq = seq + (1 - 2 * lax.rem(self.seq // w, 2)) * w
        sec = self.layers - 1 - self.sec if mask & 2 else self.sec
        return sec, seq

    def device(self, mask):
        sec, seq = self.owner(mask)
        return {"section": sec, "seq": seq}

    def arrival(self, half, mask):
        order = self.orders[half]
        return max(i for i, dim in enumerate(order) if mask >> dim & 1)

    def barrier(self):
        sem = pltpu.get_barrier_semaphore()
        for mask in range(1, self.size):
            pl.semaphore_signal(sem, inc=1, device_id=self.device(mask), device_id_type=MESH)
        pl.semaphore_wait(sem, self.size - 1)


class Spread:
    def __init__(self, plane, ref, start, rows, send, recv):
        self.plane, self.ref, self.start, self.rows, self.send, self.recv = plane, ref, start, rows, send, recv

    def view(self, half, mask):
        sec, seq = self.plane.owner(mask)
        count = self.rows // 2
        return self.ref.at[pl.ds(pl.multiple_of(self.start(sec, seq) + half * count, 16), count), :]

    def copy(self, half, mask, dim):
        view = self.view(half, mask)
        key = mask ^ (1 << dim)
        return pltpu.make_async_remote_copy(
            src_ref=view, dst_ref=view, send_sem=self.send.at[half, key], recv_sem=self.recv.at[half, key],
            device_id=self.plane.partner(dim), device_id_type=MESH,
        )

    def arrived(self, half, mask):
        view = self.view(half, mask)
        pltpu.make_async_remote_copy(
            src_ref=view, dst_ref=view, send_sem=self.send.at[half, mask], recv_sem=self.recv.at[half, mask],
            device_id=self.plane.partner(0), device_id_type=MESH,
        ).wait_recv()

    def begin(self):
        for stage in range(self.plane.stages):
            for half in (0, 1):
                self.copy(half, 0, self.plane.orders[half][stage]).start()
        for half in (0, 1):
            self.copy(half, 0, 0).start()

    def hop(self, stage):
        for half in (0, 1):
            order = self.plane.orders[half]
            for mask in self.plane.masks[1:]:
                if self.plane.arrival(half, mask) == stage:
                    self.arrived(half, mask)
                    for later in order[stage + 1 :]:
                        self.copy(half, mask, later).start()
                    self.copy(half, mask, 0).start()

    def finish(self):
        for half in (0, 1):
            for mask in self.plane.masks:
                self.arrived(half, mask + 1)

    def drain(self):
        for half in (0, 1):
            for mask in range(1, self.plane.size):
                self.copy(half, mask ^ 1, 0).wait_send()


class Collect:
    def __init__(self, plane, ref, base, blocks, core_in, stage_in, core_send, core_recv, send, recv):
        self.plane, self.ref, self.base, self.blocks = plane, ref, base, blocks
        self.core_in, self.stage_in = core_in, stage_in
        self.core_send, self.core_recv, self.send, self.recv = core_send, core_recv, send, recv

    def core_copy(self, c):
        return pltpu.make_async_remote_copy(
            src_ref=self.ref.at[pl.ds(self.base + c * SPAN, SPAN), :], dst_ref=self.core_in.at[c // 2],
            send_sem=self.core_send.at[c], recv_sem=self.core_recv.at[c],
            device_id=self.plane.partner(0), device_id_type=MESH,
        )

    def block_done(self, c):
        @pl.when(self.plane.low != c % 2)
        def _():
            self.core_copy(c).start()

    def block_add(self, c):
        @pl.when(self.plane.low == c % 2)
        def _():
            self.core_copy(c).wait_recv()
            rows = pl.ds(self.base + c * SPAN, SPAN)
            self.ref[rows, :] = (self.ref[rows, :].astype(F32) + self.core_in[c // 2].astype(F32)).astype(BF16)

    def rows(self, half, mask):
        sec, seq = self.plane.owner(mask)
        count = SPAN // self.plane.layers // 2
        begin = self.base + seq * SPAN + sec * (2 * count) + half * count
        return pl.ds(pl.multiple_of(begin, 16), count)

    def copy(self, half, mask, dim):
        return pltpu.make_async_remote_copy(
            src_ref=self.ref.at[self.rows(half, mask), :], dst_ref=self.stage_in.at[half, mask // 2],
            send_sem=self.send.at[half, mask // 2], recv_sem=self.recv.at[half, mask // 2],
            device_id=self.plane.partner(dim), device_id_type=MESH,
        )

    def plan(self, stage):
        for half in (0, 1):
            order = self.plane.orders[half][::-1]
            for mask in self.plane.masks[1:]:
                if mask >> order[stage] & 1 and not any(mask >> dim & 1 for dim in order[:stage]):
                    yield half, mask, order[stage]

    def begin(self, stage):
        for half, mask, dim in self.plan(stage):
            self.copy(half, mask, dim).start()

    def add(self, stage, out_ref=None, out_base=0):
        for half, mask, dim in self.plan(stage):
            self.copy(half, mask, dim).wait_recv()
            rows = self.rows(half, mask ^ (1 << dim))
            value = self.ref[rows, :].astype(F32) + self.stage_in[half, mask // 2].astype(F32)
            if stage == self.plane.stages - 1:
                count = value.shape[0]
                out_ref[pl.ds(out_base + half * count, count), :] = value
            else:
                self.ref[rows, :] = value.astype(BF16)

    def drain(self):
        for c in range(self.blocks):
            @pl.when(self.plane.low != c % 2)
            def _(c=c):
                self.core_copy(c).wait_send()

        for stage in range(self.plane.stages):
            for half, mask, dim in self.plan(stage):
                self.copy(half, mask, dim).wait_send()


class Share:
    def __init__(self, plane, source, target, send, recv):
        self.plane, self.source, self.target, self.send, self.recv = plane, source, target, send, recv

    def copy(self, mask):
        return pltpu.make_async_remote_copy(
            src_ref=self.source, dst_ref=self.target(mask), send_sem=self.send.at[mask],
            recv_sem=self.recv.at[mask], device_id=self.plane.device(mask), device_id_type=MESH,
        )

    def begin(self):
        for mask in range(1, self.plane.size):
            self.copy(mask).start()

    def finish(self):
        for mask in range(1, self.plane.size):
            self.copy(mask).wait_recv()

    def drain(self):
        for mask in range(1, self.plane.size):
            self.copy(mask).wait_send()


def forward_kernel(
    layers, heads, blocks, taps,
    own_ref, wgx_ref, ws_ref, wo_ref, vec_ref, tri_ref, spread_ref,
    raw_ref, ss_ref, pgx_ref, ps_ref, res_ref, ent_ref, full_out_ref,
    full_ref, part_ref, pad_ref, state_ref, within_ref, ss_mine, ss_in, core_in, stage_in,
    out_sem, ag_send, ag_recv, core_send, core_recv, rs_send, rs_recv, ss_send, ss_recv,
):
    cw = heads * HEAD
    t = pl.program_id(0)
    steps = layers * blocks
    plane = Plane(layers, blocks)
    piece = SPAN // layers
    length = blocks * SPAN

    def start(m):
        return lambda sec, seq: m * length + seq * SPAN + sec * piece

    gathers = [Spread(plane, full_ref, start(m), piece, ag_send.at[m], ag_recv.at[m]) for m in range(layers)]
    sums = [
        Collect(plane, part_ref, m * length, blocks, core_in.at[m], stage_in.at[m], core_send.at[m], core_recv.at[m],
                rs_send.at[m], rs_recv.at[m])
        for m in range(layers)
    ]
    shares = [
        Share(plane, ss_mine.at[m], lambda mask, m=m: ss_in.at[m, mask], ss_send.at[m], ss_recv.at[m])
        for m in range(layers)
    ]

    def keep(m):
        rows = pl.ds(m * length, length)
        return pltpu.make_async_copy(full_ref.at[rows, :], full_out_ref.at[rows, :], out_sem.at[m])

    @pl.when(t == 0)
    def _():
        for m in range(layers):
            rows = pl.multiple_of(start(m)(plane.sec, plane.seq), 16)
            full_ref[pl.ds(rows, piece), :] = own_ref[m * piece : (m + 1) * piece, :]
        ss_mine[...] = jnp.zeros_like(ss_mine)
        plane.barrier()
        gathers[0].begin()
        gathers[0].hop(0)
        gathers[1].begin()
        for stage in range(1, plane.stages):
            gathers[0].hop(stage)
        gathers[0].finish()
        keep(0).start()

    @pl.when(t == blocks)
    def _():
        gathers[1].finish()
        keep(1).start()

    first = lax.rem(t, blocks) == 0

    @pl.when(first)
    def _():
        pad_ref[pl.ds(SPAN, 8), :] = jnp.zeros((8, pad_ref.shape[1]), F32)
        state_ref[...] = jnp.zeros_like(state_ref)

    x = full_ref[pl.ds(pl.multiple_of(t * SPAN, SPAN), SPAN), :]
    pgx = dot(x, wgx_ref[...], 1, 0).astype(BF16)
    ps = dot(x, ws_ref[...], 1, 0).astype(BF16)
    pgx_ref[...] = pgx
    ps_ref[...] = ps
    pad_ref[pl.ds(0, 8), :] = pad_ref[pl.ds(SPAN, 8), :]
    pad_ref[pl.ds(8, SPAN), :cw] = pgx[:, cw:].astype(F32)
    pad_ref[pl.ds(8, SPAN), cw:] = ps[:, : 2 * STATE].astype(F32)
    run = running_conv(pad_ref, vec_ref, taps)
    mixed = (run * sigmoid(run)).astype(BF16)
    xs, b, c = mixed[:, :cw], mixed[:, cw : cw + STATE], mixed[:, cw + STATE :]
    _, _, dt, _, _, cum = step_sizes(ps[:, 2 * STATE :].astype(F32), vec_ref, tri_ref[...])
    cum_t, dt_t = cum.T, dt.T
    inside = inside_mask()
    scores = dot(c, b, 1, 1)
    for h in range(heads):
        mixing = (scores * fading(cum, cum_t, dt_t, h, inside)).astype(BF16)
        within_ref[:, h * HEAD : (h + 1) * HEAD] = dot(mixing, xs[:, h * HEAD : (h + 1) * HEAD], 1, 0)
    tail = jnp.exp(cum[SPAN - 1 : SPAN, :] - cum) * dt
    growth = jnp.exp(cum)
    both = expand(jnp.concatenate([tail, growth], 0), spread_ref[...])
    tail_e, growth_e = both[:SPAN], both[SPAN:]
    xs_f = xs.astype(F32)
    state = state_ref[...]
    state_low = state.astype(BF16)
    ent_ref[0] = state_low
    reach = dot(c, state_low, 1, 0)
    state_ref[...] = growth_e[SPAN - 1 : SPAN, :] * state + dot(b, (xs_f * tail_e).astype(BF16), 0, 0)
    result = (within_ref[...] + growth_e * reach + vec_ref[8:9, :cw] * xs_f).astype(BF16)
    res_ref[...] = result
    gate = pgx[:, :cw].astype(F32)
    g = result.astype(F32) * (gate * sigmoid(gate))
    ss = jnp.sum(g * g, axis=1, keepdims=True)
    ss_mine[t // blocks, pl.ds(lax.rem(t, blocks), 1), :] = jnp.broadcast_to(ss, (SPAN, STATE)).T[0:1, :]
    part_ref[pl.ds(pl.multiple_of(t * SPAN, SPAN), SPAN), :] = dot(
        (g * vec_ref[5:6, :cw]).astype(BF16), wo_ref[...], 1, 0
    ).astype(BF16)

    for m in range(layers):
        for c in range(blocks):
            @pl.when(t == m * blocks + c)
            def _(m=m, c=c):
                sums[m].block_done(c)

    for stage in range(plane.stages):
        @pl.when(t == min(stage * 2, blocks - 1))
        def _(stage=stage):
            gathers[1].hop(stage)

    @pl.when(t == blocks - 1)
    def _():
        shares[0].begin()

    @pl.when(t == blocks)
    def _():
        for c in range(blocks):
            sums[0].block_add(c)
        sums[0].begin(0)

    for stage in range(plane.stages):
        @pl.when(t == blocks + 1 + stage)
        def _(stage=stage):
            sums[0].add(stage, raw_ref, 0)
            if stage + 1 < plane.stages:
                sums[0].begin(stage + 1)

    for c in range(blocks - 1):
        @pl.when(t == blocks + c + 1)
        def _(c=c):
            sums[1].block_add(c)

    @pl.when(t == steps - 1)
    def _():
        shares[1].begin()
        sums[1].block_add(blocks - 1)
        sums[1].begin(0)
        for m in range(layers):
            shares[m].finish()
            total = ss_mine[m]
            for mask in range(1, plane.size):
                total = total + ss_in[m, mask]
            ss_ref[m] = total
        for m in range(layers):
            gathers[m].drain()
            keep(m).wait()
            shares[m].drain()
        sums[0].drain()
        for stage in range(plane.stages):
            sums[1].add(stage, raw_ref, piece)
            if stage + 1 < plane.stages:
                sums[1].begin(stage + 1)
        sums[1].drain()


def backward_kernel(
    heads, blocks, taps,
    gb_ref, sc_ref, pgx_ref, ps_ref, hgx_ref, hs_ref, res_ref, ent_ref,
    wgx_ref, ws_ref, wo_ref, vec_ref, tri_ref, spread_ref, gather_ref,
    pg_ref, gpgx_ref, gps_ref, no_ref, small_ref,
    pad_ref, next_ref, ge_ref, within_ref, gxm_ref,
):
    cw = heads * HEAD
    step = pl.program_id(0)
    place = lax.rem(step, blocks)

    @pl.when(step == 0)
    def _():
        small_ref[...] = jnp.zeros_like(small_ref)

    @pl.when(place == 0)
    def _():
        next_ref[pl.ds(0, 8), :] = jnp.zeros((8, next_ref.shape[1]), F32)
        ge_ref[...] = jnp.zeros_like(ge_ref)

    pgx, ps = pgx_ref[...], ps_ref[...]
    keep = jnp.where(place == blocks - 1, 0.0, 1.0)
    pad_ref[pl.ds(0, 8), :cw] = hgx_ref[8:, cw:].astype(F32) * keep
    pad_ref[pl.ds(0, 8), cw:] = hs_ref[8:, : 2 * STATE].astype(F32) * keep
    pad_ref[pl.ds(8, SPAN), :cw] = pgx[:, cw:].astype(F32)
    pad_ref[pl.ds(8, SPAN), cw:] = ps[:, : 2 * STATE].astype(F32)
    run = running_conv(pad_ref, vec_ref, taps)
    sig = sigmoid(run)
    mixed = (run * sig).astype(BF16)
    slope = sig * (1.0 + run * (1.0 - sig))
    xs, b, c = mixed[:, :cw], mixed[:, cw : cw + STATE], mixed[:, cw + STATE :]
    xs_f = xs.astype(F32)
    tri = tri_ref[...]
    x, e, dt, decay, rate, cum = step_sizes(ps[:, 2 * STATE :].astype(F32), vec_ref, tri)
    cum_t, dt_t = cum.T, dt.T
    tail = jnp.exp(cum[SPAN - 1 : SPAN, :] - cum) * dt
    growth = jnp.exp(cum)
    both = expand(jnp.concatenate([tail, growth], 0), spread_ref[...])
    tail_e, growth_e = both[:SPAN], both[SPAN:]

    gb = gb_ref[...]
    gu = dot(gb, wo_ref[...], 1, 1)
    columns = jnp.concatenate([sc_ref[0]] * (STATE // 8), 0).T
    r, pull = columns[:, 0:1], columns[:, 1:2]
    gain = vec_ref[5:6, :cw]
    gate = pgx[:, :cw].astype(F32)
    sg = sigmoid(gate)
    sl = gate * sg
    res = res_ref[...].astype(F32)
    g = res * sl
    rg = r * g
    no_ref[...] = (rg * gain).astype(BF16)
    dg = r * (gu * gain) - pull * g
    gr = (dg * sl).astype(BF16)
    gr_f = gr.astype(F32)
    ggate = dg * res * (sg + sl * (1.0 - sg))

    ent = ent_ref[0]
    ge = ge_ref[...]
    gl = ge.astype(BF16)
    reach = dot(c, ent, 1, 0)
    pulled = tail_e * dot(b, gl, 1, 0)
    gq = (growth_e * gr_f).astype(BF16)
    grad_c = dot(gq, ent, 1, 1)
    grad_b = dot((xs_f * tail_e).astype(BF16), gl, 1, 1)
    fade = growth_e[SPAN - 1 : SPAN, :]
    ge_ref[...] = fade * ge + dot(c, gq, 0, 0)
    grad_fade = fade * jnp.sum(ge * ent.astype(F32), axis=0, keepdims=True)
    inside = inside_mask()
    scores = dot(c, b, 1, 1)
    gs = jnp.zeros((SPAN, SPAN), F32)
    for h in range(heads):
        cols = slice(h * HEAD, (h + 1) * HEAD)
        fade_in = fading(cum, cum_t, dt_t, h, inside)
        mixing = (scores * fade_in).astype(BF16)
        gs = gs + dot(gr[:, cols], xs[:, cols], 1, 1) * fade_in
        within_ref[:, cols] = dot(mixing, xs[:, cols], 1, 0)
        gxm_ref[:, cols] = dot(mixing, gr[:, cols], 0, 0)
    gs = gs.astype(BF16)
    grad_c = grad_c + dot(gs, b, 1, 0)
    grad_b = grad_b + dot(gs, c, 0, 0)
    gxm = gxm_ref[...]
    grad_x = vec_ref[8:9, :cw] * gr_f + pulled + gxm

    gather = gather_ref[...]
    tall = jnp.concatenate([gr_f * (within_ref[...] + growth_e * reach), xs_f * gxm, xs_f * pulled], 0)
    sums = per_head(tall, gather)
    s1, s2, s3 = sums[:SPAN], sums[SPAN : 2 * SPAN], sums[2 * SPAN :]
    thin = jnp.concatenate(
        [jnp.sum(gr_f * xs_f, axis=0, keepdims=True), grad_fade, jnp.zeros((6, cw), F32)], 0
    )
    thin = per_head(thin, gather)
    hi, mid, low = split3(s1 - s2 - s3)
    packed = dot(tri, jnp.concatenate([hi, mid, low], 1), 0, 0)
    grad_rate = packed[:, :STATE] + packed[:, STATE : 2 * STATE] + packed[:, 2 * STATE :]
    grad_rate = grad_rate + (jnp.sum(s3, axis=0, keepdims=True) + thin[1:2, :])
    denominator = 1.0 + e
    slope_x = jnp.where(x >= 0, 1.0, e) / denominator
    ratio = jnp.where(x < -20.0, 1.0, slope_x / jnp.maximum(dt, 1e-12))
    grad_raw = (s2 + s3) * ratio - decay * grad_rate * slope_x
    small_ref[6:7, :STATE] += jnp.sum(grad_raw, axis=0, keepdims=True)
    small_ref[7:8, :STATE] += jnp.sum(grad_rate * rate, axis=0, keepdims=True)
    small_ref[8:9, :STATE] += thin[0:1, :]
    small_ref[5:6, :cw] += jnp.sum(gu * rg, axis=0, keepdims=True)

    grun = jnp.concatenate([grad_x, grad_b, grad_c], 1) * slope
    next_ref[pl.ds(SPAN, 8), :] = next_ref[pl.ds(0, 8), :]
    next_ref[pl.ds(0, SPAN), :] = grun
    small_ref[taps : taps + 1, :] += jnp.sum(grun, axis=0, keepdims=True)
    gbefore = jnp.zeros_like(grun)
    for k in range(taps):
        small_ref[k : k + 1, :] += jnp.sum(
            grun * pad_ref[pl.ds(8 - taps + 1 + k, SPAN), :], axis=0, keepdims=True
        )
        gbefore = gbefore + vec_ref[k : k + 1, :] * next_ref[pl.ds(taps - 1 - k, SPAN), :]
    gpgx = jnp.concatenate([ggate, gbefore[:, :cw]], 1).astype(BF16)
    gps = jnp.concatenate([gbefore[:, cw:], grad_raw], 1).astype(BF16)
    gpgx_ref[...] = gpgx
    gps_ref[...] = gps
    pg_ref[...] = (dot(gpgx, wgx_ref[...], 1, 1) + dot(gps, ws_ref[...], 1, 1)).astype(BF16)


def tables(heads):
    cw = heads * HEAD
    tri = np.tril(np.ones((SPAN, SPAN), np.float32))
    one = (np.arange(cw)[None, :] // HEAD == np.arange(STATE)[:, None]).astype(np.float32)
    spread3 = np.concatenate([one] * 3, 0)
    gather3 = np.concatenate([one.T] * 3, 0)
    return jnp.asarray(tri, BF16), jnp.asarray(spread3, BF16), jnp.asarray(gather3, BF16)


def whole(a):
    return pl.BlockSpec(memory_space=pltpu.VMEM)


def plane_scratch(layers, blocks, width):
    size, piece = layers * blocks, SPAN // layers
    dma = pltpu.SemaphoreType.DMA
    return [
        pltpu.VMEM((layers, blocks // 2, SPAN, width), BF16),
        pltpu.VMEM((layers, 2, size // 2, piece // 2, width), BF16),
        dma((layers,)),
        dma((layers, 2, size)),
        dma((layers, 2, size)),
        dma((layers, blocks)),
        dma((layers, blocks)),
        dma((layers, 2, size // 2)),
        dma((layers, 2, size // 2)),
    ]


def layer_forward(own, wgx, ws, wo, vec, taps, number):
    layers, blocks = lax.axis_size("section"), lax.axis_size("seq")
    width = own.shape[1]
    cw = wo.shape[0]
    heads = cw // HEAD
    steps = layers * blocks
    tokens = steps * SPAN
    tri, spread3, _ = tables(heads)
    rows = lambda w: pl.BlockSpec((SPAN, w), lambda t: (t, 0))
    chans = cw + 2 * STATE
    vmem = pl.BlockSpec(memory_space=pltpu.VMEM)
    dma = pltpu.SemaphoreType.DMA
    return pl.pallas_call(
        functools.partial(forward_kernel, layers, heads, blocks, taps),
        grid=(steps,),
        in_specs=[vmem] * 7,
        out_specs=[
            vmem,
            vmem,
            rows(2 * cw),
            rows(3 * STATE),
            rows(cw),
            pl.BlockSpec((1, STATE, cw), lambda t: (t, 0, 0)),
            pl.BlockSpec(memory_space=pl.ANY),
        ],
        out_shape=[
            jax.ShapeDtypeStruct(own.shape, F32),
            jax.ShapeDtypeStruct((layers, 8, SPAN), F32),
            jax.ShapeDtypeStruct((tokens, 2 * cw), BF16),
            jax.ShapeDtypeStruct((tokens, 3 * STATE), BF16),
            jax.ShapeDtypeStruct((tokens, cw), BF16),
            jax.ShapeDtypeStruct((steps, STATE, cw), BF16),
            jax.ShapeDtypeStruct((tokens, width), BF16),
        ],
        scratch_shapes=[
            pltpu.VMEM((tokens, width), BF16),
            pltpu.VMEM((tokens, width), BF16),
            pltpu.VMEM((SPAN + 8, chans), F32),
            pltpu.VMEM((STATE, cw), F32),
            pltpu.VMEM((SPAN, cw), F32),
            pltpu.VMEM((layers, 8, SPAN), F32),
            pltpu.VMEM((layers, steps, 8, SPAN), F32),
        ]
        + plane_scratch(layers, blocks, width)
        + [dma((layers, steps)), dma((layers, steps))],
        compiler_params=pltpu.CompilerParams(
            vmem_limit_bytes=60 << 20, collective_id=number, has_side_effects=True
        ),
        cost_estimate=pl.CostEstimate(
            flops=2 * tokens * width * (3 * cw + 3 * STATE) + 2 * tokens * cw * 700,
            bytes_accessed=4 * tokens * width + 2 * width * (3 * cw + 3 * STATE) + 8 * tokens * cw,
            transcendentals=tokens * SPAN * heads,
        ),
        name="layer_forward",
    )(own, wgx, ws, wo, vec, tri, spread3)


def layer_backward(gb, sc, pgx, ps, res, ent, wgx, ws, wo, vec, taps, sequences):
    tokens, width = gb.shape
    cw = wo.shape[0]
    heads = cw // HEAD
    steps = tokens // SPAN
    blocks = steps // sequences
    tri, spread3, gather3 = tables(heads)
    chans = cw + 2 * STATE

    def at(t):
        return t - lax.rem(t, blocks) + (blocks - 1 - lax.rem(t, blocks))

    rows = lambda w: pl.BlockSpec((SPAN, w), lambda t: (at(t), 0))
    edge = lambda w: pl.BlockSpec((16, w), lambda t: (jnp.maximum(at(t) * (SPAN // 16) - 1, 0), 0))
    return pl.pallas_call(
        functools.partial(backward_kernel, heads, blocks, taps),
        grid=(steps,),
        in_specs=[
            rows(width),
            pl.BlockSpec((1, 8, SPAN), lambda t: (at(t), 0, 0)),
            rows(2 * cw),
            rows(3 * STATE),
            edge(2 * cw),
            edge(3 * STATE),
            rows(cw),
            pl.BlockSpec((1, STATE, cw), lambda t: (at(t), 0, 0)),
        ]
        + [whole(a) for a in (wgx, ws, wo, vec, tri, spread3, gather3)],
        out_specs=[
            rows(width),
            rows(2 * cw),
            rows(3 * STATE),
            rows(cw),
            pl.BlockSpec((16, chans), lambda t: (0, 0)),
        ],
        out_shape=[
            jax.ShapeDtypeStruct((tokens, width), BF16),
            jax.ShapeDtypeStruct((tokens, 2 * cw), BF16),
            jax.ShapeDtypeStruct((tokens, 3 * STATE), BF16),
            jax.ShapeDtypeStruct((tokens, cw), BF16),
            jax.ShapeDtypeStruct((16, chans), F32),
        ],
        scratch_shapes=[
            pltpu.VMEM((SPAN + 8, chans), F32),
            pltpu.VMEM((SPAN + 8, chans), F32),
            pltpu.VMEM((STATE, cw), F32),
            pltpu.VMEM((SPAN, cw), F32),
            pltpu.VMEM((SPAN, cw), F32),
        ],
        compiler_params=pltpu.CompilerParams(vmem_limit_bytes=48 << 20),
        cost_estimate=pl.CostEstimate(
            flops=2 * tokens * width * (3 * cw + 3 * STATE) + 2 * tokens * cw * 2000,
            bytes_accessed=4 * tokens * width + 2 * width * (3 * cw + 3 * STATE) + 8 * tokens * cw,
            transcendentals=tokens * SPAN * heads,
        ),
        name="layer_backward",
    )(gb, sc, pgx, ps, pgx, ps, res, ent, wgx, ws, wo, vec, tri, spread3, gather3)


def line_barrier(place, count, axis):
    sem = pltpu.get_barrier_semaphore()

    @pl.when(place > 0)
    def _():
        pl.semaphore_signal(sem, inc=1, device_id={axis: place - 1}, device_id_type=MESH)

    @pl.when(place < count - 1)
    def _():
        pl.semaphore_signal(sem, inc=1, device_id={axis: place + 1}, device_id_type=MESH)

    inner = (place > 0) & (place < count - 1)

    @pl.when(inner)
    def _():
        pl.semaphore_wait(sem, 2)

    @pl.when(~inner)
    def _():
        pl.semaphore_wait(sem, 1)


def gather_kernel(
    count, ranks, parts, axis,
    gx_ref, o_ref, full_ref, all_ref,
    own_sem, send_sem, recv_sem, osend_sem, orecv_sem,
):
    place = lax.axis_index(axis)
    rows = gx_ref.shape[0]
    piece = rows // parts
    orows = o_ref.shape[0]
    opiece = orows // parts
    here = lax.axis_index("section") * ranks + lax.axis_index("seq")
    source = (here * orows) // (ranks * lax.axis_size("section") * orows // count)
    line_barrier(place, count, axis)

    def block(j, k):
        return full_ref.at[pl.ds(pl.multiple_of(j * rows + k * piece, 16), piece), :]

    def hop(src, dst, side, d, k):
        to = place + 1 if side == 0 else place - 1
        return pltpu.make_async_remote_copy(
            src_ref=src, dst_ref=dst, send_sem=send_sem.at[side, d, k], recv_sem=recv_sem.at[side, d, k],
            device_id={axis: to}, device_id_type=MESH,
        )

    def ohop(src, k, side):
        to = place + 1 if side == 0 else place - 1
        dst = all_ref.at[pl.ds(k * opiece, opiece), :]
        return pltpu.make_async_remote_copy(
            src_ref=src, dst_ref=dst, send_sem=osend_sem.at[side, k], recv_sem=orecv_sem.at[k],
            device_id={axis: to}, device_id_type=MESH,
        )

    ends = (place < count - 1, place > 0)
    for k in range(parts):
        for side in (0, 1):
            @pl.when(ends[side])
            def _(side=side, k=k):
                hop(gx_ref.at[pl.ds(k * piece, piece), :], block(place, k), side, 0, k).start()
    own = pltpu.make_async_copy(gx_ref, full_ref.at[pl.ds(pl.multiple_of(place * rows, 16), rows), :], own_sem.at[0])
    own.start()
    oown = pltpu.make_async_copy(o_ref, all_ref, own_sem.at[1])

    @pl.when(place == source)
    def _():
        oown.start()

    for d in range(1, count):
        for k in range(parts):
            for side in (0, 1):
                j = place - d if side == 0 else place + d
                have = (j >= 0) if side == 0 else (j < count)

                @pl.when(have)
                def _(side=side, k=k, d=d, j=j):
                    hop(block(j, k), block(j, k), side, d - 1, k).wait_recv()

                if d < count - 1:
                    @pl.when(have & ends[side])
                    def _(side=side, k=k, d=d, j=j):
                        hop(block(j, k), block(j, k), side, d, k).start()

        if d == 1:
            for k in range(parts):
                for side in (0, 1):
                    @pl.when((place == source) & ends[side])
                    def _(side=side, k=k):
                        ohop(o_ref.at[pl.ds(k * opiece, opiece), :], k, side).start()

    for k in range(parts):
        part = all_ref.at[pl.ds(k * opiece, opiece), :]

        @pl.when(place != source)
        def _(k=k, part=part):
            ohop(part, k, 0).wait_recv()

        @pl.when((place > source) & ends[0])
        def _(k=k, part=part):
            ohop(part, k, 0).start()

        @pl.when((place < source) & ends[1])
        def _(k=k, part=part):
            ohop(part, k, 1).start()

    own.wait()

    @pl.when(place == source)
    def _():
        oown.wait()

    for k in range(parts):
        part = all_ref.at[pl.ds(k * opiece, opiece), :]

        @pl.when((place >= source) & ends[0])
        def _(k=k, part=part):
            ohop(part, k, 0).wait_send()

        @pl.when((place <= source) & ends[1])
        def _(k=k, part=part):
            ohop(part, k, 1).wait_send()

        for d in range(count - 1):
            for side in (0, 1):
                j = place - d if side == 0 else place + d
                have = (j >= 0) if side == 0 else (j < count)

                @pl.when(have & ends[side])
                def _(side=side, k=k, d=d, j=j):
                    hop(block(j, k), block(j, k), side, d, k).wait_send()


def gather_weights(gx, o, number):
    count, ranks = lax.axis_size("fsdp"), lax.axis_size("seq")
    parts = 4 if gx.shape[0] % 64 == 0 and o.shape[0] % 64 == 0 else 2
    anywhere = pl.BlockSpec(memory_space=pl.ANY)
    return pl.pallas_call(
        functools.partial(gather_kernel, count, ranks, parts, "fsdp"),
        in_specs=[anywhere] * 2,
        out_specs=[anywhere] * 2,
        out_shape=[
            jax.ShapeDtypeStruct((count * gx.shape[0], gx.shape[1]), BF16),
            jax.ShapeDtypeStruct(o.shape, BF16),
        ],
        scratch_shapes=[
            pltpu.SemaphoreType.DMA((2,)),
            pltpu.SemaphoreType.DMA((2, count, parts)),
            pltpu.SemaphoreType.DMA((2, count, parts)),
            pltpu.SemaphoreType.DMA((2, parts)),
            pltpu.SemaphoreType.DMA((parts,)),
        ],
        compiler_params=pltpu.CompilerParams(collective_id=number, has_side_effects=True),
        name="gather_weights",
    )(gx, o)


def reduce_kernel(
    count, ranks, parts, axis,
    full_ref, gp_ref, no_ref, gb_ref, out_ref, oout_ref,
    sum_ref, osum_ref, in_ref, oin_ref,
    send_sem, recv_sem, osend_sem, orecv_sem,
):
    place = lax.axis_index(axis)
    rows = out_ref.shape[0]
    piece = rows // parts
    orows = oout_ref.shape[0]
    opiece = orows // parts
    here = lax.axis_index("section") * ranks + lax.axis_index("seq")
    source = (here * orows) // (ranks * lax.axis_size("section") * orows // count)
    line_barrier(place, count, axis)

    def hop(j, k, side):
        to = place + 1 if side == 0 else place - 1
        return pltpu.make_async_remote_copy(
            src_ref=sum_ref.at[j, k], dst_ref=in_ref.at[side, j, k],
            send_sem=send_sem.at[j, k], recv_sem=recv_sem.at[side, j, k],
            device_id={axis: to}, device_id_type=MESH,
        )

    def ohop(k, side):
        to = place + 1 if side == 0 else place - 1
        return pltpu.make_async_remote_copy(
            src_ref=osum_ref.at[k], dst_ref=oin_ref.at[side, k],
            send_sem=osend_sem.at[k], recv_sem=orecv_sem.at[side, k],
            device_id={axis: to}, device_id_type=MESH,
        )

    ends = (place < count - 1, place > 0)
    before = (place > 0, place < count - 1)

    def work(j, k):
        sum_ref[j, k] = dot(
            full_ref[:, j * rows + k * piece : j * rows + (k + 1) * piece], gp_ref[...], 0, 0
        ).astype(BF16)

    def shift(j, k):
        for side in (0, 1):
            beyond = (place < j) if side == 0 else (place > j)

            @pl.when(beyond & before[side])
            def _(side=side):
                hop(j, k, side).wait_recv()
                sum_ref[j, k] = (sum_ref[j, k].astype(F32) + in_ref[side, j, k].astype(F32)).astype(BF16)

            @pl.when(beyond)
            def _(side=side):
                hop(j, k, side).start()

    order = []
    low, high = 0, count - 1
    while low <= high:
        order += [high] if low == high else [high, low]
        low, high = low + 1, high - 1
    order = [(j, k) for pair in range(0, len(order), 2) for k in range(parts) for j in order[pair : pair + 2]]
    for j, k in order:
        work(j, k)
        shift(j, k)
    for k in range(parts):
        osum_ref[k] = dot(no_ref[:, k * opiece : (k + 1) * opiece], gb_ref[...], 0, 0).astype(BF16)
        for side in (0, 1):
            beyond = (place < source) if side == 0 else (place > source)

            @pl.when(beyond & before[side])
            def _(side=side, k=k):
                ohop(k, side).wait_recv()
                osum_ref[k] = (osum_ref[k].astype(F32) + oin_ref[side, k].astype(F32)).astype(BF16)

            @pl.when(beyond)
            def _(side=side, k=k):
                ohop(k, side).start()

    for k in range(parts):
        for j in range(count):
            for side in (0, 1):
                @pl.when((place == j) & before[side])
                def _(side=side, k=k, j=j):
                    hop(j, k, side).wait_recv()
                    sum_ref[j, k] = (sum_ref[j, k].astype(F32) + in_ref[side, j, k].astype(F32)).astype(BF16)

            @pl.when(place == j)
            def _(k=k, j=j):
                out_ref[pl.ds(k * piece, piece), :] = sum_ref[j, k]

    for k in range(parts):
        for side in (0, 1):
            @pl.when((place == source) & before[side])
            def _(side=side, k=k):
                ohop(k, side).wait_recv()
                osum_ref[k] = (osum_ref[k].astype(F32) + oin_ref[side, k].astype(F32)).astype(BF16)

        oout_ref[pl.ds(k * opiece, opiece), :] = osum_ref[k]

        @pl.when(place != source)
        def _(k=k):
            ohop(k, 0).wait_send()

        for j in range(count):
            @pl.when(place != j)
            def _(k=k, j=j):
                hop(j, k, 0).wait_send()


def reduce_gradients(full, gp, no, gb, number):
    count, ranks = lax.axis_size("fsdp"), lax.axis_size("seq")
    tokens, width = full.shape
    rows, cols, orows = width // count, gp.shape[1], no.shape[1]
    parts = 3 if rows % 384 == 0 and orows % 384 == 0 else 1
    return pl.pallas_call(
        functools.partial(reduce_kernel, count, ranks, parts, "fsdp"),
        in_specs=[whole(a) for a in (full, gp, no, gb)],
        out_specs=[pl.BlockSpec(memory_space=pltpu.VMEM)] * 2,
        out_shape=[jax.ShapeDtypeStruct((rows, cols), BF16), jax.ShapeDtypeStruct((orows, width), BF16)],
        scratch_shapes=[
            pltpu.VMEM((count, parts, rows // parts, cols), BF16),
            pltpu.VMEM((parts, orows // parts, width), BF16),
            pltpu.VMEM((2, count, parts, rows // parts, cols), BF16),
            pltpu.VMEM((2, parts, orows // parts, width), BF16),
            pltpu.SemaphoreType.DMA((count, parts)),
            pltpu.SemaphoreType.DMA((2, count, parts)),
            pltpu.SemaphoreType.DMA((parts,)),
            pltpu.SemaphoreType.DMA((2, parts)),
        ],
        compiler_params=pltpu.CompilerParams(
            collective_id=number, has_side_effects=True, vmem_limit_bytes=56 << 20
        ),
        cost_estimate=pl.CostEstimate(
            flops=2 * tokens * (width * cols + orows * width), bytes_accessed=2 * tokens * (2 * width + cols + orows),
            transcendentals=0,
        ),
        name="reduce_gradients",
    )(full, gp, no, gb)


def swapped(value, axis):
    count = lax.axis_size(axis)
    return lax.ppermute(value, axis, [(i, count - 1 - i) for i in range(count)])


PLANE = ("section", "seq")
EVERY = ("section", "seq", "fsdp")


def per_device(
    section_ends, norm_gain, in_weight, conv_weight, conv_bias, step_bias, log_decay, skip_gain, gate_gain, out_weight
):
    sec, seq, dep = lax.axis_index("section"), lax.axis_index("seq"), lax.axis_index("fsdp")
    layers, ranks, depth = lax.axis_size("section"), lax.axis_size("seq"), lax.axis_size("fsdp")
    group = layers * ranks
    here = sec * ranks + seq
    there = (layers - 1 - sec) * ranks + seq
    low_layer = sec == 0
    width = in_weight.shape[1] * depth
    inner = gate_gain.shape[1] * depth
    chans = conv_bias.shape[1] * depth
    heads_all = step_bias.shape[1] * depth
    taps = conv_weight.shape[1]
    cw = inner // group
    heads = cw // HEAD
    shared = 2 * STATE

    ends = section_ends[0, :, 0]
    piece = ends.shape[1] // layers
    sent = jnp.where(low_layer, ends[:, piece:], ends[:, :piece])
    got = swapped(sent, "section")
    hidden = jnp.where(low_layer, ends[:, :piece], got).astype(F32).reshape(layers * piece, width)
    cot = jnp.where(low_layer, got, ends[:, piece:]).astype(F32).reshape(layers * piece, width)

    def own_tokens(v):
        v = lax.dynamic_slice_in_dim(v, seq, 1, 1)[:, 0]
        return lax.dynamic_slice_in_dim(v, sec * piece, piece, 1).reshape(-1, 1)

    def token_order(v):
        v = v.reshape(layers, ranks, layers, piece, -1)
        return jnp.transpose(v, (2, 1, 0, 3, 4)).reshape(layers * layers * ranks * piece, -1)

    def device_order(v):
        v = v.reshape(layers, ranks, layers, piece, -1)
        return jnp.transpose(v, (2, 1, 0, 3, 4)).reshape(layers * layers * ranks * piece, -1)

    flat = [norm_gain, conv_weight, conv_bias, step_bias, log_decay, skip_gain, gate_gain]
    sizes = [v.size for v in flat]
    packed = jnp.concatenate([v.reshape(-1) for v in flat])
    packed = lax.all_gather(packed, ("section", "fsdp")).reshape(layers, depth, -1).astype(F32)

    def member(layer, number):
        begin = sum(sizes[:number])
        return packed[layer, :, begin : begin + sizes[number]]

    def head_columns(v, begin, count):
        return lax.dynamic_slice_in_dim(v, begin, count, v.ndim - 1)

    def vectors(layer):
        kernel = jnp.transpose(member(layer, 1).reshape(depth, taps, -1), (1, 0, 2)).reshape(taps, chans)
        rows = jnp.concatenate([kernel, member(layer, 2).reshape(1, chans)], 0)
        rows = jnp.concatenate([head_columns(rows, here * cw, cw), rows[:, inner:]], 1)
        total = cw + shared

        def padded(v):
            return jnp.pad(v[None], ((0, 0), (0, total - v.shape[0])))

        gain = head_columns(member(layer, 6).reshape(-1), here * cw, cw)
        by_head = [head_columns(member(layer, n).reshape(-1), here * heads, heads) for n in (3, 4, 5)]
        return jnp.concatenate(
            [rows, jnp.zeros((5 - taps - 1, total), F32), padded(gain), padded(by_head[0]), padded(by_head[1]),
             padded(jnp.repeat(by_head[2], HEAD)), jnp.zeros((7, total), F32)], 0)

    gains = [member(layer, 0).reshape(1, -1) for layer in range(layers)]
    vecs = [vectors(layer) for layer in range(layers)]

    def own_columns(rank):
        return jnp.concatenate(
            [head_columns(in_weight[0], rank * cw, cw), head_columns(in_weight[0], inner + rank * cw, cw)], 1
        )

    out_rows = out_weight.shape[1]

    def own_rows(rank):
        start = rank * cw - dep * out_rows
        inside = (start >= 0) & (start < out_rows)
        block = lax.dynamic_slice_in_dim(out_weight[0], jnp.clip(start, 0, out_rows - cw), cw, 0)
        return jnp.where(inside, block, jnp.zeros_like(block))

    mine, theirs = own_columns(here), swapped(own_columns(there), "section")
    mine_o, theirs_o = own_rows(here), swapped(own_rows(there), "section")
    strip = in_weight.shape[1] // ranks
    thin = lax.dynamic_slice(in_weight[0], (seq * strip, inner + chans - shared), (strip, shared + heads_all))
    thin = lax.all_gather(thin, ("section", "fsdp", "seq"), axis=0, tiled=True).reshape(layers, width, -1)
    weights = []
    for layer in range(layers):
        own = low_layer if layer == 0 else ~low_layer
        wgx, wo = gather_weights(jnp.where(own, mine, theirs), jnp.where(own, mine_o, theirs_o), layer)
        steps_w = head_columns(thin[layer, :, shared:], here * heads, heads)
        ws = jnp.concatenate([thin[layer, :, :shared], steps_w, jnp.zeros((width, STATE - heads), BF16)], 1)
        weights.append((wgx, ws, wo))

    def spread_rows(v):
        return token_order(lax.all_gather(v, PLANE, axis=0, tiled=True))

    def collect_rows(v):
        return lax.psum_scatter(device_order(v), PLANE, scatter_dimension=0, tiled=True).astype(F32)

    saved = []
    for layer in range(layers):
        wgx, ws, wo = weights[layer]
        rs = lax.rsqrt(jnp.mean(hidden * hidden, axis=-1, keepdims=True) + EPS)
        raw, ss, pgx, ps, res, ent, full = layer_forward(
            (hidden * rs * gains[layer]).astype(BF16), wgx, ws, wo, vecs[layer], taps, 2 * layers + layer
        )
        r_rows = lax.rsqrt(ss / inner + EPS)
        r = own_tokens(r_rows)
        saved.append((hidden, rs, full, pgx, ps, res, ent, raw, r, r_rows))
        hidden = hidden + r * raw
        if layer + 1 < layers:
            hidden = hidden.astype(BF16).astype(F32)
    output = hidden

    grad = cot
    big, small = [None] * layers, [None] * layers
    for layer in reversed(range(layers)):
        wgx, ws, wo = weights[layer]
        before, rs, full, pgx, ps, res, ent, raw, r, r_rows = saved[layer]
        low = grad.astype(BF16)
        pull = r * r * r * jnp.sum(low.astype(F32) * raw, axis=-1, keepdims=True) / inner
        gb = spread_rows(low)
        pull = lax.all_gather(pull.reshape(layers, piece), PLANE).reshape(layers, ranks, layers, piece)
        pull = jnp.transpose(pull, (2, 1, 0, 3)).reshape(layers * ranks, SPAN)
        sc = jnp.stack([r_rows[:, :ranks].reshape(-1, SPAN), pull], 1)
        sc = jnp.pad(sc, ((0, 0), (0, 6), (0, 0)))
        pg, gpgx, gps, no, tiny = layer_backward(
            gb, sc, pgx, ps, res, ent, wgx, ws, wo, vecs[layer], taps, layers
        )
        g_gx, g_o = reduce_gradients(full, gpgx, no, gb, layers + layer)
        g_s = dot(full, gps, 0, 0).astype(BF16)
        gn = collect_rows(pg)
        unit = before * rs
        g_gain = jnp.sum(gn * unit, axis=0)
        gn = gn * gains[layer]
        grad = grad + rs * (gn - unit * jnp.mean(gn * unit, axis=-1, keepdims=True))
        if layer > 0:
            grad = grad.astype(BF16).astype(F32)

        def placed(v, count, begin):
            return lax.dynamic_update_slice(jnp.zeros((count,), F32), v, (begin,))

        conv = lax.dynamic_update_slice(jnp.zeros((taps + 1, chans), F32), tiny[: taps + 1, :cw], (0, here * cw))
        conv = conv + jnp.pad(tiny[: taps + 1, cw:], ((0, 0), (inner, 0)))
        small[layer] = jnp.concatenate(
            [g_gain, conv.reshape(-1), placed(tiny[5, :cw], inner, here * cw)]
            + [placed(tiny[n, :heads], heads_all, here * heads) for n in (6, 7, 8)]
        )
        steps_g = lax.dynamic_update_slice(jnp.zeros((width, heads_all), BF16), g_s[:, shared : shared + heads], (0, here * heads))
        g_s = jnp.concatenate([g_s[:, :shared], steps_g], 1)
        g_s = lax.psum_scatter(g_s, "fsdp", scatter_dimension=0, tiled=True)
        big[layer] = (g_gx, g_s, g_o)

    output = output.reshape(layers, piece, width)
    grad = grad.reshape(layers, piece, width)
    got = swapped(jnp.where(low_layer, output, grad).astype(BF16), "section").astype(F32)
    results = jnp.where(low_layer, jnp.concatenate([grad, got], 1), jnp.concatenate([got, output], 1))
    section_results = results[None, :, None]

    def own_layer(values):
        own = jnp.where(low_layer, values[0], values[1])
        other = jnp.where(low_layer, values[1], values[0])
        return own, other

    own, other = own_layer([b[0] for b in big])
    other = swapped(other, "section")
    pair = jnp.stack([jnp.where(low_layer, own, other), jnp.where(low_layer, other, own)])
    gx = lax.all_gather(pair, "seq")
    rows = gx.shape[2]
    gx = gx.reshape(ranks, layers, rows, 2, cw)
    gx = jnp.transpose(gx, (2, 3, 1, 0, 4)).reshape(rows, 2 * inner)
    s_all = lax.psum(jnp.stack([b[1] for b in big]), PLANE)
    s_own, _ = own_layer([s_all[0], s_all[1]])
    grad_in = jnp.concatenate([gx.astype(F32), s_own.astype(F32)], 1)[None]

    own, other = own_layer([b[2] for b in big])
    other = swapped(other, "section")
    pair = jnp.stack([jnp.where(low_layer, own, other), jnp.where(low_layer, other, own)])
    spread = jnp.zeros((out_rows, width), BF16)
    for s in range(layers):
        start = (s * ranks + seq) * cw - dep * out_rows
        inside = (start >= 0) & (start < out_rows)
        block = jnp.where(inside, pair[s], jnp.zeros_like(pair[s]))
        spread = spread + lax.dynamic_update_slice(jnp.zeros_like(spread), block, (jnp.clip(start, 0, out_rows - cw), 0))
    grad_out = lax.psum(spread, "seq").astype(F32)[None]

    tiny = lax.psum(jnp.stack(small), EVERY)
    tiny = jnp.where(low_layer, tiny[0], tiny[1])
    cuts = np.cumsum([0, width, taps * chans, chans, inner, heads_all, heads_all, heads_all])
    parts = [tiny[cuts[i] : cuts[i + 1]] for i in range(7)]

    def share(v):
        count = v.shape[-1] // depth
        return lax.dynamic_slice_in_dim(v, dep * count, count, v.ndim - 1)[None]

    return (
        section_results,
        share(parts[0]),
        grad_in,
        share(parts[1].reshape(taps, chans)),
        share(parts[2]),
        share(parts[4]),
        share(parts[5]),
        share(parts[6]),
        share(parts[3]),
        grad_out,
    )


def solution(mesh):
    weight = P("section", "fsdp")
    matrix = P("section", "fsdp", None)
    ends = P("section", None, "fsdp", "seq", None)
    kernel = P("section", None, "fsdp")
    return jax.shard_map(
        per_device,
        mesh=mesh,
        in_specs=(ends, weight, matrix, kernel, weight, weight, weight, weight, weight, matrix),
        out_specs=(ends, weight, matrix, kernel, weight, weight, weight, weight, weight, matrix),
        check_vma=False,
    )
```

```python
import functools

import jax
import jax.numpy as jnp
import numpy as np
from jax import lax
from jax.experimental import pallas as pl
from jax.experimental.pallas import tpu as pltpu
from jax.sharding import PartitionSpec as P

SPAN = 256
HEAD = 64
STATE = 128
EPS = 1e-05
F32 = jnp.float32
BF16 = jnp.bfloat16


def dot(a, b, ca, cb):
    return lax.dot_general(a, b, (((ca,), (cb,)), ((), ())), preferred_element_type=F32)


def split3(v):
    hi = v.astype(BF16)
    rest = v - hi.astype(F32)
    mid = rest.astype(BF16)
    low = (rest - mid.astype(F32)).astype(BF16)
    return hi, mid, low


def sigmoid(v):
    return 1.0 / (1.0 + jnp.exp(-v))


def running_conv(pad_ref, vec_ref, taps):
    run = vec_ref[taps : taps + 1, :] + vec_ref[0:1, :] * pad_ref[pl.ds(8 - taps + 1, SPAN), :]
    for k in range(1, taps):
        run = run + vec_ref[k : k + 1, :] * pad_ref[pl.ds(8 - taps + 1 + k, SPAN), :]
    return run


def step_sizes(dt_raw, vec_ref, tri):
    x = dt_raw + vec_ref[6:7, :STATE]
    e = jnp.exp(-jnp.abs(x))
    dt = jnp.maximum(x, 0.0) + jnp.log1p(e)
    decay = jnp.exp(vec_ref[7:8, :STATE])
    rate = -dt * decay
    hi, mid, low = split3(rate)
    packed = dot(tri, jnp.concatenate([hi, mid, low], 1), 1, 0)
    cum = packed[:, :STATE] + packed[:, STATE : 2 * STATE] + packed[:, 2 * STATE :]
    return x, e, dt, decay, rate, cum


def expand(v, spread3):
    return dot(jnp.concatenate(split3(v), 1), spread3, 1, 0)


def per_head(v, gather3):
    return dot(jnp.concatenate(split3(v), 1), gather3, 1, 0)


def fading(cum, cum_t, dt_t, h, inside):
    spread = cum[:, h : h + 1] - cum_t[h : h + 1, :]
    return jnp.exp(jnp.where(inside, spread, -1e30)) * dt_t[h : h + 1, :]


def inside_mask():
    rows = lax.broadcasted_iota(jnp.int32, (SPAN, SPAN), 0)
    cols = lax.broadcasted_iota(jnp.int32, (SPAN, SPAN), 1)
    return cols <= rows


MESH = pl.DeviceIdType.MESH


class Plane:
    def __init__(self, layers, ranks):
        self.layers, self.ranks = layers, ranks
        self.sec, self.seq = lax.axis_index("section"), lax.axis_index("seq")
        self.low = lax.rem(self.seq, 2)
        count = ranks.bit_length() - 1
        outer = list(range(1, count + 1))
        self.size = layers * ranks
        self.orders = (outer, outer[::-1])
        self.stages = len(outer)
        self.masks = [m for m in range(self.size) if m % 2 == 0]

    def weight(self, dim):
        return 1 if dim == 0 else 1 << (dim - 1)

    def flipped(self, dim):
        w = self.weight(dim)
        return self.seq + (1 - 2 * lax.rem(self.seq // w, 2)) * w

    def partner(self, dim):
        if dim == 1:
            return {"section": self.layers - 1 - self.sec}
        return {"seq": self.flipped(dim)}

    def owner(self, mask):
        seq = self.seq
        for dim in range(self.stages + 1):
            if dim != 1 and mask >> dim & 1:
                w = self.weight(dim)
                seq = seq + (1 - 2 * lax.rem(self.seq // w, 2)) * w
        sec = self.layers - 1 - self.sec if mask & 2 else self.sec
        return sec, seq

    def device(self, mask):
        sec, seq = self.owner(mask)
        return {"section": sec, "seq": seq}

    def arrival(self, half, mask):
        order = self.orders[half]
        return max(i for i, dim in enumerate(order) if mask >> dim & 1)

    def own_lanes(self, v, heads):
        return pltpu.roll(v, STATE - (self.sec * self.ranks + self.seq) * heads, 1)

    def all_lanes(self, v, heads):
        return pltpu.roll(v, (self.sec * self.ranks + self.seq) * heads, 1)

    def barrier(self):
        sem = pltpu.get_barrier_semaphore()
        for mask in range(1, self.size):
            pl.semaphore_signal(sem, inc=1, device_id=self.device(mask), device_id_type=MESH)
        pl.semaphore_wait(sem, self.size - 1)


class Spread:
    def __init__(self, plane, ref, start, rows, send, recv):
        self.plane, self.ref, self.start, self.rows, self.send, self.recv = plane, ref, start, rows, send, recv

    def view(self, half, mask):
        sec, seq = self.plane.owner(mask)
        count = self.rows // 2
        return self.ref.at[pl.ds(pl.multiple_of(self.start(sec, seq) + half * count, 16), count), :]

    def copy(self, half, mask, dim):
        view = self.view(half, mask)
        key = mask ^ (1 << dim)
        return pltpu.make_async_remote_copy(
            src_ref=view, dst_ref=view, send_sem=self.send.at[half, key], recv_sem=self.recv.at[half, key],
            device_id=self.plane.partner(dim), device_id_type=MESH,
        )

    def arrived(self, half, mask):
        view = self.view(half, mask)
        pltpu.make_async_remote_copy(
            src_ref=view, dst_ref=view, send_sem=self.send.at[half, mask], recv_sem=self.recv.at[half, mask],
            device_id=self.plane.partner(0), device_id_type=MESH,
        ).wait_recv()

    def begin(self):
        for stage in range(self.plane.stages):
            for half in (0, 1):
                self.copy(half, 0, self.plane.orders[half][stage]).start()
        for half in (0, 1):
            self.copy(half, 0, 0).start()

    def hop(self, stage):
        for half in (0, 1):
            order = self.plane.orders[half]
            for mask in self.plane.masks[1:]:
                if self.plane.arrival(half, mask) == stage:
                    self.arrived(half, mask)
                    for later in order[stage + 1 :]:
                        self.copy(half, mask, later).start()
                    self.copy(half, mask, 0).start()

    def finish(self):
        for half in (0, 1):
            for mask in self.plane.masks:
                self.arrived(half, mask + 1)

    def drain(self):
        for half in (0, 1):
            for mask in range(1, self.plane.size):
                self.copy(half, mask ^ 1, 0).wait_send()


class Collect:
    def __init__(self, plane, ref, base, span, core_in, stage_in, core_send, core_recv, send, recv):
        self.plane, self.ref, self.base, self.blocks, self.span = plane, ref, base, plane.ranks, span
        self.core_in, self.stage_in = core_in, stage_in
        self.core_send, self.core_recv, self.send, self.recv = core_send, core_recv, send, recv

    def core_copy(self, c):
        return pltpu.make_async_remote_copy(
            src_ref=self.ref.at[pl.ds(self.base + c * self.span, self.span), :], dst_ref=self.core_in.at[c // 2],
            send_sem=self.core_send.at[c], recv_sem=self.core_recv.at[c],
            device_id=self.plane.partner(0), device_id_type=MESH,
        )

    def block_done(self, c):
        @pl.when(self.plane.low != c % 2)
        def _():
            self.core_copy(c).start()

    def block_add(self, c):
        @pl.when(self.plane.low == c % 2)
        def _():
            self.core_copy(c).wait_recv()
            rows = pl.ds(self.base + c * self.span, self.span)
            self.ref[rows, :] = (self.ref[rows, :].astype(F32) + self.core_in[c // 2].astype(F32)).astype(BF16)

    def rows(self, half, mask):
        sec, seq = self.plane.owner(mask)
        count = self.span // self.plane.layers // 2
        begin = self.base + seq * self.span + sec * (2 * count) + half * count
        return pl.ds(pl.multiple_of(begin, 16), count)

    def copy(self, half, mask, dim):
        return pltpu.make_async_remote_copy(
            src_ref=self.ref.at[self.rows(half, mask), :], dst_ref=self.stage_in.at[half, mask // 2],
            send_sem=self.send.at[half, mask // 2], recv_sem=self.recv.at[half, mask // 2],
            device_id=self.plane.partner(dim), device_id_type=MESH,
        )

    def plan(self, stage):
        for half in (0, 1):
            order = self.plane.orders[half][::-1]
            for mask in self.plane.masks[1:]:
                if mask >> order[stage] & 1 and not any(mask >> dim & 1 for dim in order[:stage]):
                    yield half, mask, order[stage]

    def begin(self, stage):
        for half, mask, dim in self.plan(stage):
            self.copy(half, mask, dim).start()

    def add(self, stage, out_ref=None, out_base=0):
        for half, mask, dim in self.plan(stage):
            self.copy(half, mask, dim).wait_recv()
            rows = self.rows(half, mask ^ (1 << dim))
            value = self.ref[rows, :].astype(F32) + self.stage_in[half, mask // 2].astype(F32)
            if stage == self.plane.stages - 1:
                count = value.shape[0]
                out_ref[pl.ds(out_base + half * count, count), :] = value
            else:
                self.ref[rows, :] = value.astype(BF16)

    def drain(self):
        for c in range(self.blocks):
            @pl.when(self.plane.low != c % 2)
            def _(c=c):
                self.core_copy(c).wait_send()

        for stage in range(self.plane.stages):
            for half, mask, dim in self.plan(stage):
                self.copy(half, mask, dim).wait_send()


class Share:
    def __init__(self, plane, source, target, send, recv):
        self.plane, self.source, self.target, self.send, self.recv = plane, source, target, send, recv

    def copy(self, mask):
        return pltpu.make_async_remote_copy(
            src_ref=self.source, dst_ref=self.target(mask), send_sem=self.send.at[mask],
            recv_sem=self.recv.at[mask], device_id=self.plane.device(mask), device_id_type=MESH,
        )

    def begin(self):
        for mask in range(1, self.plane.size):
            self.copy(mask).start()

    def finish(self):
        for mask in range(1, self.plane.size):
            self.copy(mask).wait_recv()

    def drain(self):
        for mask in range(1, self.plane.size):
            self.copy(mask).wait_send()


def chain_barrier(plane, place, count):
    sem = pltpu.get_barrier_semaphore()
    for mask in range(1, plane.size):
        pl.semaphore_signal(sem, inc=1, device_id=plane.device(mask), device_id_type=MESH)
    for d in range(1, count):
        other = lax.rem(place + d, count)
        for sec in (plane.sec, plane.layers - 1 - plane.sec):
            pl.semaphore_signal(sem, inc=1, device_id={"section": sec, "fsdp": other}, device_id_type=MESH)
    pl.semaphore_wait(sem, plane.size - 1 + 2 * (count - 1))


class Row:
    def __init__(self, place, count, source, target, send, recv):
        self.place, self.count, self.source, self.target, self.send, self.recv = place, count, source, target, send, recv

    def copy(self, d):
        return pltpu.make_async_remote_copy(
            src_ref=self.source(d), dst_ref=self.target(d), send_sem=self.send.at[d], recv_sem=self.recv.at[d],
            device_id={"fsdp": lax.rem(self.place + d, self.count)}, device_id_type=MESH,
        )

    def begin(self):
        for d in range(1, self.count):
            self.copy(d).start()

    def finish(self):
        for d in range(1, self.count):
            self.copy(d).wait_recv()

    def drain(self):
        for d in range(1, self.count):
            self.copy(d).wait_send()


class Line:
    def __init__(self, place, count, block, parts, send, recv):
        self.place, self.count, self.block, self.parts, self.send, self.recv = place, count, block, parts, send, recv
        self.ends = (place < count - 1, place > 0)

    def hop(self, side, d, k):
        j = self.place - d if side == 0 else self.place + d
        return pltpu.make_async_remote_copy(
            src_ref=self.block(j, k), dst_ref=self.block(j, k), send_sem=self.send.at[side, d, k],
            recv_sem=self.recv.at[side, d, k], device_id={"fsdp": self.place + 1 if side == 0 else self.place - 1},
            device_id_type=MESH,
        )

    def arrived(self, side, d, k):
        j = self.place - d if side == 0 else self.place + d
        pltpu.make_async_remote_copy(
            src_ref=self.block(j, k), dst_ref=self.block(j, k), send_sem=self.send.at[side, d, k],
            recv_sem=self.recv.at[side, d - 1, k], device_id={"fsdp": self.place + 1 if side == 0 else self.place - 1},
            device_id_type=MESH,
        ).wait_recv()

    def have(self, side, d):
        return self.place >= d if side == 0 else self.place + d < self.count

    def begin(self, k):
        for side in (0, 1):
            @pl.when(self.ends[side])
            def _(side=side):
                self.hop(side, 0, k).start()

    def forward(self, d, k):
        for side in (0, 1):
            @pl.when(self.have(side, d))
            def _(side=side):
                self.arrived(side, d, k)

            if d < self.count - 1:
                @pl.when(self.have(side, d) & self.ends[side])
                def _(side=side):
                    self.hop(side, d, k).start()

    def drain(self):
        for k in range(self.parts):
            for d in range(self.count - 1):
                for side in (0, 1):
                    @pl.when(self.have(side, d) & self.ends[side])
                    def _(side=side, d=d, k=k):
                        self.hop(side, d, k).wait_send()


def forward_kernel(
    layers, heads, blocks, taps, ahead, *refs
):
    own_ref, wgx_ref, ws_ref, wo_ref, vec_ref, tri_ref, spread_ref = refs[:7]
    refs = refs[7:]
    if ahead:
        next_gx, next_o = refs[:2]
        refs = refs[2:]
    raw_ref, ss_ref, pgx_ref, ps_ref, res_ref, ent_ref, full_out_ref = refs[:7]
    refs = refs[7:]
    if ahead:
        ahead_gx, ahead_o = refs[:2]
        refs = refs[2:]
    full_ref, part_ref, pad_ref, state_ref, within_ref, ss_mine, ss_in, core_in, stage_in = refs[:9]
    out_sem, ag_send, ag_recv, core_send, core_recv, rs_send, rs_recv, ss_send, ss_recv = refs[9:18]
    cw = heads * HEAD
    t = pl.program_id(0)
    steps = layers * blocks
    plane = Plane(layers, blocks)
    piece = SPAN // layers
    length = blocks * SPAN

    def start(m):
        return lambda sec, seq: m * length + seq * SPAN + sec * piece

    gathers = [Spread(plane, full_ref, start(m), piece, ag_send.at[m], ag_recv.at[m]) for m in range(layers)]
    sums = [
        Collect(plane, part_ref, m * length, SPAN, core_in.at[m], stage_in.at[m], core_send.at[m], core_recv.at[m],
                rs_send.at[m], rs_recv.at[m])
        for m in range(layers)
    ]
    shares = [
        Share(plane, ss_mine.at[m], lambda mask, m=m: ss_in.at[m, mask], ss_send.at[m], ss_recv.at[m])
        for m in range(layers)
    ]

    def keep(m):
        rows = pl.ds(m * length, length)
        return pltpu.make_async_copy(full_ref.at[rows, :], full_out_ref.at[rows, :], out_sem.at[m])

    if ahead:
        own_sem, row_send, row_recv, o_send, o_recv = refs[18:]
        spot, count = lax.axis_index("fsdp"), lax.axis_size("fsdp")
        grows = next_gx.shape[0]
        target = ahead_gx.at[pl.ds(pl.multiple_of(spot * grows, 16), grows), :]
        row = Row(spot, count, lambda d: next_gx, lambda d: target, row_send, row_recv)
        orow = Row(spot, count, lambda d: next_o, lambda d: ahead_o.at[spot], o_send, o_recv)
        own_gx = pltpu.make_async_copy(next_gx, target, own_sem.at[0])
        own_o = pltpu.make_async_copy(next_o, ahead_o.at[spot], own_sem.at[1])

        @pl.when(t == 0)
        def _():
            chain_barrier(plane, spot, count)
            own_gx.start()
            own_o.start()

    @pl.when(t == 0)
    def _():
        for m in range(layers):
            rows = pl.multiple_of(start(m)(plane.sec, plane.seq), 16)
            full_ref[pl.ds(rows, piece), :] = own_ref[m * piece : (m + 1) * piece, :]
        ss_mine[...] = jnp.zeros_like(ss_mine)
        if not ahead:
            plane.barrier()
        gathers[0].begin()
        if ahead:
            row.begin()
            orow.begin()
        gathers[0].hop(0)
        gathers[1].begin()
        for stage in range(1, plane.stages):
            gathers[0].hop(stage)
        gathers[0].finish()
        keep(0).start()

    @pl.when(t == blocks)
    def _():
        gathers[1].finish()
        keep(1).start()

    first = lax.rem(t, blocks) == 0

    @pl.when(first)
    def _():
        pad_ref[pl.ds(SPAN, 8), :] = jnp.zeros((8, pad_ref.shape[1]), F32)
        state_ref[...] = jnp.zeros_like(state_ref)

    x = full_ref[pl.ds(pl.multiple_of(t * SPAN, SPAN), SPAN), :]
    pgx = dot(x, wgx_ref[...], 1, 0).astype(BF16)
    ps = dot(x, ws_ref[...], 1, 0).astype(BF16)
    pgx_ref[...] = pgx
    ps_ref[...] = ps
    pad_ref[pl.ds(0, 8), :] = pad_ref[pl.ds(SPAN, 8), :]
    pad_ref[pl.ds(8, SPAN), :cw] = pgx[:, cw:].astype(F32)
    pad_ref[pl.ds(8, SPAN), cw:] = ps[:, : 2 * STATE].astype(F32)
    run = running_conv(pad_ref, vec_ref, taps)
    mixed = (run * sigmoid(run)).astype(BF16)
    xs, b, c = mixed[:, :cw], mixed[:, cw : cw + STATE], mixed[:, cw + STATE :]
    _, _, dt, _, _, cum = step_sizes(plane.own_lanes(ps[:, 2 * STATE :].astype(F32), heads), vec_ref, tri_ref[...])
    cum_t, dt_t = cum.T, dt.T
    inside = inside_mask()
    scores = dot(c, b, 1, 1)
    for h in range(heads):
        mixing = (scores * fading(cum, cum_t, dt_t, h, inside)).astype(BF16)
        within_ref[:, h * HEAD : (h + 1) * HEAD] = dot(mixing, xs[:, h * HEAD : (h + 1) * HEAD], 1, 0)
    tail = jnp.exp(cum[SPAN - 1 : SPAN, :] - cum) * dt
    growth = jnp.exp(cum)
    both = expand(jnp.concatenate([tail, growth], 0), spread_ref[...])
    tail_e, growth_e = both[:SPAN], both[SPAN:]
    xs_f = xs.astype(F32)
    state = state_ref[...]
    state_low = state.astype(BF16)
    ent_ref[0] = state_low
    reach = dot(c, state_low, 1, 0)
    state_ref[...] = growth_e[SPAN - 1 : SPAN, :] * state + dot(b, (xs_f * tail_e).astype(BF16), 0, 0)
    result = (within_ref[...] + growth_e * reach + vec_ref[8:9, :cw] * xs_f).astype(BF16)
    res_ref[...] = result
    gate = pgx[:, :cw].astype(F32)
    g = result.astype(F32) * (gate * sigmoid(gate))
    ss = jnp.sum(g * g, axis=1, keepdims=True)
    ss_mine[t // blocks, pl.ds(lax.rem(t, blocks), 1), :] = jnp.broadcast_to(ss, (SPAN, STATE)).T[0:1, :]
    part_ref[pl.ds(pl.multiple_of(t * SPAN, SPAN), SPAN), :] = dot(
        (g * vec_ref[5:6, :cw]).astype(BF16), wo_ref[...], 1, 0
    ).astype(BF16)

    for m in range(layers):
        for c in range(blocks):
            @pl.when(t == m * blocks + c)
            def _(m=m, c=c):
                sums[m].block_done(c)

    for stage in range(plane.stages):
        @pl.when(t == min(stage * 2, blocks - 1))
        def _(stage=stage):
            gathers[1].hop(stage)

    @pl.when(t == blocks - 1)
    def _():
        shares[0].begin()

    @pl.when(t == blocks)
    def _():
        for c in range(blocks):
            sums[0].block_add(c)
        sums[0].begin(0)

    for stage in range(plane.stages):
        @pl.when(t == blocks + 1 + stage)
        def _(stage=stage):
            sums[0].add(stage, raw_ref, 0)
            if stage + 1 < plane.stages:
                sums[0].begin(stage + 1)

    for c in range(blocks - 1):
        @pl.when(t == blocks + c + 1)
        def _(c=c):
            sums[1].block_add(c)

    @pl.when(t == steps - 1)
    def _():
        shares[1].begin()
        sums[1].block_add(blocks - 1)
        sums[1].begin(0)
        for m in range(layers):
            shares[m].finish()
            total = ss_mine[m]
            for mask in range(1, plane.size):
                total = total + ss_in[m, mask]
            ss_ref[m] = total
        for m in range(layers):
            gathers[m].drain()
            keep(m).wait()
            shares[m].drain()
        sums[0].drain()
        for stage in range(plane.stages):
            sums[1].add(stage, raw_ref, piece)
            if stage + 1 < plane.stages:
                sums[1].begin(stage + 1)
        sums[1].drain()
        if ahead:
            own_gx.wait()
            own_o.wait()
            for each in (row, orow):
                each.finish()
                each.drain()


def backward_kernel(
    layers, heads, blocks, taps,
    own_ref, pull_own, r_ref, pgx_ref, ps_ref, hgx_ref, hs_ref, res_ref, ent_ref,
    wgx_ref, ws_ref, wo_ref, vec_ref, tri_ref, spread_ref, gather_ref,
    raw_ref, gpgx_ref, gps_ref, no_ref, small_ref, full_out_ref,
    full_ref, part_ref, pad_ref, next_ref, ge_ref, within_ref, gxm_ref, pull_ref, core_in, stage_in,
    out_sem, ag_send, ag_recv, core_send, core_recv, rs_send, rs_recv, ss_send, ss_recv,
):
    cw = heads * HEAD
    t = pl.program_id(0)
    steps = layers * blocks
    place = lax.rem(t, blocks)
    micro, block = t // blocks, blocks - 1 - place
    plane = Plane(layers, blocks)
    piece = SPAN // layers
    length = blocks * SPAN
    rows_now = pl.ds(pl.multiple_of(micro * length + block * SPAN, SPAN), SPAN)

    def start(m):
        return lambda sec, seq: m * length + seq * SPAN + sec * piece

    gathers = [Spread(plane, full_ref, start(m), piece, ag_send.at[m], ag_recv.at[m]) for m in range(layers)]
    collects = [
        Collect(plane, part_ref, m * length, SPAN, core_in.at[m], stage_in.at[m], core_send.at[m], core_recv.at[m],
                rs_send.at[m], rs_recv.at[m])
        for m in range(layers)
    ]

    def pull_place(sec, seq):
        return pull_ref.at[:, seq, :, pl.ds(pl.multiple_of(sec * piece, piece), piece)]

    share = Share(plane, pull_own, lambda mask: pull_place(plane.sec, plane.seq), ss_send, ss_recv)

    def saving(m):
        rows = pl.ds(m * length, length)
        return pltpu.make_async_copy(full_ref.at[rows, :], full_out_ref.at[rows, :], out_sem.at[m])

    @pl.when(t == 0)
    def _():
        small_ref[...] = jnp.zeros_like(small_ref)
        for m in range(layers):
            rows = pl.multiple_of(start(m)(plane.sec, plane.seq), 16)
            full_ref[pl.ds(rows, piece), :] = own_ref[m * piece : (m + 1) * piece, :]
        for m in range(layers):
            pull_ref[m, plane.seq, :, pl.ds(pl.multiple_of(plane.sec * piece, piece), piece)] = pull_own[m]
        plane.barrier()
        share.begin()
        gathers[0].begin()
        gathers[0].hop(0)
        gathers[1].begin()
        for stage in range(1, plane.stages):
            gathers[0].hop(stage)
        gathers[0].finish()
        share.finish()
        saving(0).start()

    @pl.when(t == blocks)
    def _():
        gathers[1].finish()
        saving(1).start()

    @pl.when(place == 0)
    def _():
        next_ref[pl.ds(0, 8), :] = jnp.zeros((8, next_ref.shape[1]), F32)
        ge_ref[...] = jnp.zeros_like(ge_ref)

    pgx, ps = pgx_ref[...], ps_ref[...]
    keep = jnp.where(place == blocks - 1, 0.0, 1.0)
    pad_ref[pl.ds(0, 8), :cw] = hgx_ref[8:, cw:].astype(F32) * keep
    pad_ref[pl.ds(0, 8), cw:] = hs_ref[8:, : 2 * STATE].astype(F32) * keep
    pad_ref[pl.ds(8, SPAN), :cw] = pgx[:, cw:].astype(F32)
    pad_ref[pl.ds(8, SPAN), cw:] = ps[:, : 2 * STATE].astype(F32)
    run = running_conv(pad_ref, vec_ref, taps)
    sig = sigmoid(run)
    mixed = (run * sig).astype(BF16)
    slope = sig * (1.0 + run * (1.0 - sig))
    xs, b, c = mixed[:, :cw], mixed[:, cw : cw + STATE], mixed[:, cw + STATE :]
    xs_f = xs.astype(F32)
    tri = tri_ref[...]
    x, e, dt, decay, rate, cum = step_sizes(plane.own_lanes(ps[:, 2 * STATE :].astype(F32), heads), vec_ref, tri)
    cum_t, dt_t = cum.T, dt.T
    tail = jnp.exp(cum[SPAN - 1 : SPAN, :] - cum) * dt
    growth = jnp.exp(cum)
    both = expand(jnp.concatenate([tail, growth], 0), spread_ref[...])
    tail_e, growth_e = both[:SPAN], both[SPAN:]

    gu = dot(full_ref[rows_now, :], wo_ref[...], 1, 1)
    r = jnp.broadcast_to(r_ref[micro, pl.ds(block, 1), :], (STATE, SPAN)).T[:, 0:1]
    pull = jnp.broadcast_to(pull_ref[micro, block][0:1, :], (STATE, SPAN)).T[:, 0:1]
    gain = vec_ref[5:6, :cw]
    gate = pgx[:, :cw].astype(F32)
    sg = sigmoid(gate)
    sl = gate * sg
    res = res_ref[...].astype(F32)
    g = res * sl
    rg = r * g
    no_ref[...] = (rg * gain).astype(BF16)
    dg = r * (gu * gain) - pull * g
    gr = (dg * sl).astype(BF16)
    gr_f = gr.astype(F32)
    ggate = dg * res * (sg + sl * (1.0 - sg))

    ent = ent_ref[0]
    ge = ge_ref[...]
    gl = ge.astype(BF16)
    reach = dot(c, ent, 1, 0)
    pulled = tail_e * dot(b, gl, 1, 0)
    gq = (growth_e * gr_f).astype(BF16)
    grad_c = dot(gq, ent, 1, 1)
    grad_b = dot((xs_f * tail_e).astype(BF16), gl, 1, 1)
    fade = growth_e[SPAN - 1 : SPAN, :]
    ge_ref[...] = fade * ge + dot(c, gq, 0, 0)
    grad_fade = fade * jnp.sum(ge * ent.astype(F32), axis=0, keepdims=True)
    inside = inside_mask()
    scores = dot(c, b, 1, 1)
    gs = jnp.zeros((SPAN, SPAN), F32)
    for h in range(heads):
        cols = slice(h * HEAD, (h + 1) * HEAD)
        fade_in = fading(cum, cum_t, dt_t, h, inside)
        mixing = (scores * fade_in).astype(BF16)
        gs = gs + dot(gr[:, cols], xs[:, cols], 1, 1) * fade_in
        within_ref[:, cols] = dot(mixing, xs[:, cols], 1, 0)
        gxm_ref[:, cols] = dot(mixing, gr[:, cols], 0, 0)
    gs = gs.astype(BF16)
    grad_c = grad_c + dot(gs, b, 1, 0)
    grad_b = grad_b + dot(gs, c, 0, 0)
    gxm = gxm_ref[...]
    grad_x = vec_ref[8:9, :cw] * gr_f + pulled + gxm

    gather = gather_ref[...]
    tall = jnp.concatenate([gr_f * (within_ref[...] + growth_e * reach), xs_f * gxm, xs_f * pulled], 0)
    sums = per_head(tall, gather)
    s1, s2, s3 = sums[:SPAN], sums[SPAN : 2 * SPAN], sums[2 * SPAN :]
    thin = jnp.concatenate(
        [jnp.sum(gr_f * xs_f, axis=0, keepdims=True), grad_fade, jnp.zeros((6, cw), F32)], 0
    )
    thin = per_head(thin, gather)
    hi, mid, low = split3(s1 - s2 - s3)
    packed = dot(tri, jnp.concatenate([hi, mid, low], 1), 0, 0)
    grad_rate = packed[:, :STATE] + packed[:, STATE : 2 * STATE] + packed[:, 2 * STATE :]
    grad_rate = grad_rate + (jnp.sum(s3, axis=0, keepdims=True) + thin[1:2, :])
    denominator = 1.0 + e
    slope_x = jnp.where(x >= 0, 1.0, e) / denominator
    ratio = jnp.where(x < -20.0, 1.0, slope_x / jnp.maximum(dt, 1e-12))
    grad_raw = (s2 + s3) * ratio - decay * grad_rate * slope_x
    small_ref[6:7, :STATE] += jnp.sum(grad_raw, axis=0, keepdims=True)
    small_ref[7:8, :STATE] += jnp.sum(grad_rate * rate, axis=0, keepdims=True)
    small_ref[8:9, :STATE] += thin[0:1, :]
    small_ref[5:6, :cw] += jnp.sum(gu * rg, axis=0, keepdims=True)

    grun = jnp.concatenate([grad_x, grad_b, grad_c], 1) * slope
    next_ref[pl.ds(SPAN, 8), :] = next_ref[pl.ds(0, 8), :]
    next_ref[pl.ds(0, SPAN), :] = grun
    small_ref[taps : taps + 1, :] += jnp.sum(grun, axis=0, keepdims=True)
    gbefore = jnp.zeros_like(grun)
    for k in range(taps):
        small_ref[k : k + 1, :] += jnp.sum(
            grun * pad_ref[pl.ds(8 - taps + 1 + k, SPAN), :], axis=0, keepdims=True
        )
        gbefore = gbefore + vec_ref[k : k + 1, :] * next_ref[pl.ds(taps - 1 - k, SPAN), :]
    gpgx = jnp.concatenate([ggate, gbefore[:, :cw]], 1).astype(BF16)
    gps = jnp.concatenate([gbefore[:, cw:], plane.all_lanes(grad_raw, heads)], 1).astype(BF16)
    gpgx_ref[...] = gpgx
    gps_ref[...] = gps
    part_ref[rows_now, :] = (dot(gpgx, wgx_ref[...], 1, 1) + dot(gps, ws_ref[...], 1, 1)).astype(BF16)

    for m in range(layers):
        for c in range(blocks):
            @pl.when(t == m * blocks + blocks - 1 - c)
            def _(m=m, c=c):
                collects[m].block_done(c)

    for stage in range(plane.stages):
        @pl.when(t == min(stage, blocks - 1))
        def _(stage=stage):
            gathers[1].hop(stage)

    @pl.when(t == blocks)
    def _():
        for c in range(blocks):
            collects[0].block_add(c)
        collects[0].begin(0)

    for stage in range(plane.stages):
        @pl.when(t == blocks + 1 + stage)
        def _(stage=stage):
            collects[0].add(stage, raw_ref, 0)
            if stage + 1 < plane.stages:
                collects[0].begin(stage + 1)

    for c in range(1, blocks):
        @pl.when(t == blocks + blocks - c)
        def _(c=c):
            collects[1].block_add(c)

    @pl.when(t == steps - 1)
    def _():
        collects[1].block_add(0)
        collects[1].begin(0)
        share.drain()
        for m in range(layers):
            gathers[m].drain()
            saving(m).wait()
        collects[0].drain()
        for stage in range(plane.stages):
            collects[1].add(stage, raw_ref, piece)
            if stage + 1 < plane.stages:
                collects[1].begin(stage + 1)
        collects[1].drain()


def tables(heads):
    cw = heads * HEAD
    tri = np.tril(np.ones((SPAN, SPAN), np.float32))
    one = (np.arange(cw)[None, :] // HEAD == np.arange(STATE)[:, None]).astype(np.float32)
    spread3 = np.concatenate([one] * 3, 0)
    gather3 = np.concatenate([one.T] * 3, 0)
    return jnp.asarray(tri, BF16), jnp.asarray(spread3, BF16), jnp.asarray(gather3, BF16)


def whole(a):
    return pl.BlockSpec(memory_space=pltpu.VMEM)


def plane_scratch(layers, blocks, width):
    size, piece = layers * blocks, SPAN // layers
    dma = pltpu.SemaphoreType.DMA
    return [
        pltpu.VMEM((layers, blocks // 2, SPAN, width), BF16),
        pltpu.VMEM((layers, 2, size // 2, piece // 2, width), BF16),
        dma((layers,)),
        dma((layers, 2, size)),
        dma((layers, 2, size)),
        dma((layers, blocks)),
        dma((layers, blocks)),
        dma((layers, 2, size // 2)),
        dma((layers, 2, size // 2)),
    ]


def layer_forward(own, wgx, ws, wo, vec, taps, number, *following):
    layers, blocks, depth = lax.axis_size("section"), lax.axis_size("seq"), lax.axis_size("fsdp")
    width = own.shape[1]
    cw = wo.shape[0]
    heads = cw // HEAD
    steps = layers * blocks
    tokens = steps * SPAN
    tri, spread3, _ = tables(heads)
    rows = lambda w: pl.BlockSpec((SPAN, w), lambda t: (t, 0))
    chans = cw + 2 * STATE
    vmem = pl.BlockSpec(memory_space=pltpu.VMEM)
    dma = pltpu.SemaphoreType.DMA
    return pl.pallas_call(
        functools.partial(forward_kernel, layers, heads, blocks, taps, bool(following)),
        grid=(steps,),
        in_specs=[vmem] * 7 + [pl.BlockSpec(memory_space=pl.ANY)] * len(following),
        out_specs=[
            vmem,
            vmem,
            rows(2 * cw),
            rows(3 * STATE),
            rows(cw),
            pl.BlockSpec((1, STATE, cw), lambda t: (t, 0, 0)),
            pl.BlockSpec(memory_space=pl.ANY),
        ]
        + [pl.BlockSpec(memory_space=pl.ANY)] * len(following),
        out_shape=[
            jax.ShapeDtypeStruct(own.shape, F32),
            jax.ShapeDtypeStruct((layers, 8, SPAN), F32),
            jax.ShapeDtypeStruct((tokens, 2 * cw), BF16),
            jax.ShapeDtypeStruct((tokens, 3 * STATE), BF16),
            jax.ShapeDtypeStruct((tokens, cw), BF16),
            jax.ShapeDtypeStruct((steps, STATE, cw), BF16),
            jax.ShapeDtypeStruct((tokens, width), BF16),
        ]
        + ([jax.ShapeDtypeStruct(wgx.shape, BF16), jax.ShapeDtypeStruct((depth,) + following[1].shape, BF16)] if following else []),
        scratch_shapes=[
            pltpu.VMEM((tokens, width), BF16),
            pltpu.VMEM((tokens, width), BF16),
            pltpu.VMEM((SPAN + 8, chans), F32),
            pltpu.VMEM((STATE, cw), F32),
            pltpu.VMEM((SPAN, cw), F32),
            pltpu.VMEM((layers, 8, SPAN), F32),
            pltpu.VMEM((layers, steps, 8, SPAN), F32),
        ]
        + plane_scratch(layers, blocks, width)
        + [dma((layers, steps)), dma((layers, steps))]
        + ([dma((2,))] + [dma((depth,))] * 4 if following else []),
        compiler_params=pltpu.CompilerParams(
            vmem_limit_bytes=60 << 20, collective_id=number, has_side_effects=True
        ),
        cost_estimate=pl.CostEstimate(
            flops=2 * tokens * width * (3 * cw + 3 * STATE) + 2 * tokens * cw * 700,
            bytes_accessed=4 * tokens * width + 2 * width * (3 * cw + 3 * STATE) + 8 * tokens * cw,
            transcendentals=tokens * SPAN * heads,
        ),
        name="layer_forward",
    )(own, wgx, ws, wo, vec, tri, spread3, *following)


def layer_backward(own, pull, r_rows, pgx, ps, res, ent, wgx, ws, wo, vec, taps, number):
    layers, blocks = lax.axis_size("section"), lax.axis_size("seq")
    width = own.shape[1]
    cw = wo.shape[0]
    heads = cw // HEAD
    steps = layers * blocks
    tokens = steps * SPAN
    tri, spread3, gather3 = tables(heads)
    chans = cw + 2 * STATE
    vmem = pl.BlockSpec(memory_space=pltpu.VMEM)
    dma = pltpu.SemaphoreType.DMA

    def at(t):
        return t - lax.rem(t, blocks) + (blocks - 1 - lax.rem(t, blocks))

    rows = lambda w: pl.BlockSpec((SPAN, w), lambda t: (at(t), 0))
    edge = lambda w: pl.BlockSpec((16, w), lambda t: (jnp.maximum(at(t) * (SPAN // 16) - 1, 0), 0))
    return pl.pallas_call(
        functools.partial(backward_kernel, layers, heads, blocks, taps),
        grid=(steps,),
        in_specs=[
            vmem,
            vmem,
            vmem,
            rows(2 * cw),
            rows(3 * STATE),
            edge(2 * cw),
            edge(3 * STATE),
            rows(cw),
            pl.BlockSpec((1, STATE, cw), lambda t: (at(t), 0, 0)),
        ]
        + [vmem] * 7,
        out_specs=[
            vmem,
            rows(2 * cw),
            rows(3 * STATE),
            rows(cw),
            vmem,
            pl.BlockSpec(memory_space=pl.ANY),
        ],
        out_shape=[
            jax.ShapeDtypeStruct(own.shape, F32),
            jax.ShapeDtypeStruct((tokens, 2 * cw), BF16),
            jax.ShapeDtypeStruct((tokens, 3 * STATE), BF16),
            jax.ShapeDtypeStruct((tokens, cw), BF16),
            jax.ShapeDtypeStruct((16, chans), F32),
            jax.ShapeDtypeStruct((tokens, width), BF16),
        ],
        scratch_shapes=[
            pltpu.VMEM((tokens, width), BF16),
            pltpu.VMEM((tokens, width), BF16),
            pltpu.VMEM((SPAN + 8, chans), F32),
            pltpu.VMEM((SPAN + 8, chans), F32),
            pltpu.VMEM((STATE, cw), F32),
            pltpu.VMEM((SPAN, cw), F32),
            pltpu.VMEM((SPAN, cw), F32),
            pltpu.VMEM((layers, blocks, 8, SPAN), F32),
        ]
        + plane_scratch(layers, blocks, width)
        + [dma((steps,)), dma((steps,))],
        compiler_params=pltpu.CompilerParams(
            vmem_limit_bytes=60 << 20, collective_id=number, has_side_effects=True
        ),
        cost_estimate=pl.CostEstimate(
            flops=2 * tokens * width * (3 * cw + 3 * STATE) + 2 * tokens * cw * 2000,
            bytes_accessed=4 * tokens * width + 2 * width * (3 * cw + 3 * STATE) + 8 * tokens * cw,
            transcendentals=tokens * SPAN * heads,
        ),
        name="layer_backward",
    )(own, pull, r_rows, pgx, ps, pgx, ps, res, ent, wgx, ws, wo, vec, tri, spread3, gather3)


def line_barrier(place, count, axis):
    sem = pltpu.get_barrier_semaphore()

    @pl.when(place > 0)
    def _():
        pl.semaphore_signal(sem, inc=1, device_id={axis: place - 1}, device_id_type=MESH)

    @pl.when(place < count - 1)
    def _():
        pl.semaphore_signal(sem, inc=1, device_id={axis: place + 1}, device_id_type=MESH)

    inner = (place > 0) & (place < count - 1)

    @pl.when(inner)
    def _():
        pl.semaphore_wait(sem, 2)

    @pl.when(~inner)
    def _():
        pl.semaphore_wait(sem, 1)


def reduce_kernel(
    count, ranks, parts, axis,
    full_ref, gp_ref, no_ref, gb_ref, out_ref, oout_ref,
    sum_ref, osum_ref, in_ref, oin_ref,
    send_sem, recv_sem, osend_sem, orecv_sem,
):
    place = lax.axis_index(axis)
    rows = out_ref.shape[0]
    piece = rows // parts
    orows = oout_ref.shape[0]
    opiece = orows // parts
    here = lax.axis_index("section") * ranks + lax.axis_index("seq")
    source = (here * orows) // (ranks * lax.axis_size("section") * orows // count)
    line_barrier(place, count, axis)

    def hop(j, k, side):
        to = place + 1 if side == 0 else place - 1
        return pltpu.make_async_remote_copy(
            src_ref=sum_ref.at[j, k], dst_ref=in_ref.at[side, j, k],
            send_sem=send_sem.at[j, k], recv_sem=recv_sem.at[side, j, k],
            device_id={axis: to}, device_id_type=MESH,
        )

    def ohop(k, side):
        to = place + 1 if side == 0 else place - 1
        return pltpu.make_async_remote_copy(
            src_ref=osum_ref.at[k], dst_ref=oin_ref.at[side, k],
            send_sem=osend_sem.at[k], recv_sem=orecv_sem.at[side, k],
            device_id={axis: to}, device_id_type=MESH,
        )

    ends = (place < count - 1, place > 0)
    before = (place > 0, place < count - 1)

    def work(j, k):
        sum_ref[j, k] = dot(
            full_ref[:, j * rows + k * piece : j * rows + (k + 1) * piece], gp_ref[...], 0, 0
        ).astype(BF16)

    def shift(j, k):
        for side in (0, 1):
            beyond = (place < j) if side == 0 else (place > j)

            @pl.when(beyond & before[side])
            def _(side=side):
                hop(j, k, side).wait_recv()
                sum_ref[j, k] = (sum_ref[j, k].astype(F32) + in_ref[side, j, k].astype(F32)).astype(BF16)

            @pl.when(beyond)
            def _(side=side):
                hop(j, k, side).start()

    order = []
    low, high = 0, count - 1
    while low <= high:
        order += [high] if low == high else [high, low]
        low, high = low + 1, high - 1
    order = [(j, k) for pair in range(0, len(order), 2) for k in range(parts) for j in order[pair : pair + 2]]
    for j, k in order:
        work(j, k)
        shift(j, k)
    for k in range(parts):
        osum_ref[k] = dot(no_ref[:, k * opiece : (k + 1) * opiece], gb_ref[...], 0, 0).astype(BF16)
        for side in (0, 1):
            beyond = (place < source) if side == 0 else (place > source)

            @pl.when(beyond & before[side])
            def _(side=side, k=k):
                ohop(k, side).wait_recv()
                osum_ref[k] = (osum_ref[k].astype(F32) + oin_ref[side, k].astype(F32)).astype(BF16)

            @pl.when(beyond)
            def _(side=side, k=k):
                ohop(k, side).start()

    for k in range(parts):
        for j in range(count):
            for side in (0, 1):
                @pl.when((place == j) & before[side])
                def _(side=side, k=k, j=j):
                    hop(j, k, side).wait_recv()
                    sum_ref[j, k] = (sum_ref[j, k].astype(F32) + in_ref[side, j, k].astype(F32)).astype(BF16)

            @pl.when(place == j)
            def _(k=k, j=j):
                out_ref[pl.ds(k * piece, piece), :] = sum_ref[j, k]

    for k in range(parts):
        for side in (0, 1):
            @pl.when((place == source) & before[side])
            def _(side=side, k=k):
                ohop(k, side).wait_recv()
                osum_ref[k] = (osum_ref[k].astype(F32) + oin_ref[side, k].astype(F32)).astype(BF16)

        oout_ref[pl.ds(k * opiece, opiece), :] = osum_ref[k]

        @pl.when(place != source)
        def _(k=k):
            ohop(k, 0).wait_send()

        for j in range(count):
            @pl.when(place != j)
            def _(k=k, j=j):
                hop(j, k, 0).wait_send()


def reduce_gradients(full, gp, no, gb, number):
    count, ranks = lax.axis_size("fsdp"), lax.axis_size("seq")
    tokens, width = full.shape
    rows, cols, orows = width // count, gp.shape[1], no.shape[1]
    parts = 3 if rows % 384 == 0 and orows % 384 == 0 else 1
    return pl.pallas_call(
        functools.partial(reduce_kernel, count, ranks, parts, "fsdp"),
        in_specs=[whole(a) for a in (full, gp, no, gb)],
        out_specs=[pl.BlockSpec(memory_space=pltpu.VMEM)] * 2,
        out_shape=[jax.ShapeDtypeStruct((rows, cols), BF16), jax.ShapeDtypeStruct((orows, width), BF16)],
        scratch_shapes=[
            pltpu.VMEM((count, parts, rows // parts, cols), BF16),
            pltpu.VMEM((parts, orows // parts, width), BF16),
            pltpu.VMEM((2, count, parts, rows // parts, cols), BF16),
            pltpu.VMEM((2, parts, orows // parts, width), BF16),
            pltpu.SemaphoreType.DMA((count, parts)),
            pltpu.SemaphoreType.DMA((2, count, parts)),
            pltpu.SemaphoreType.DMA((parts,)),
            pltpu.SemaphoreType.DMA((2, parts)),
        ],
        compiler_params=pltpu.CompilerParams(
            collective_id=number, has_side_effects=True, vmem_limit_bytes=56 << 20
        ),
        cost_estimate=pl.CostEstimate(
            flops=2 * tokens * (width * cols + orows * width), bytes_accessed=2 * tokens * (2 * width + cols + orows),
            transcendentals=0,
        ),
        name="reduce_gradients",
    )(full, gp, no, gb)


def start_kernel(
    layers, ranks, parts, oparts,
    mine, theirs, mine_o, theirs_o, ends_ref, strip_ref, packed_ref,
    full, all_o, next_gx, next_o, got_ref, thin_ref, params_ref,
    own_sem, y_send, y_recv, x_send, x_recv, send, recv, o_send, o_recv, cut_send, cut_recv,
    st_send, st_recv, ag_send, ag_recv, pa_send, pa_recv,
):
    place, count = lax.axis_index("fsdp"), lax.axis_size("fsdp")
    plane = Plane(layers, ranks)
    low = plane.sec == 0
    rows = mine.shape[0]
    piece = rows // parts
    opiece = mine_o.shape[1] // oparts
    orows = mine_o.shape[0] * mine_o.shape[1]
    out_rows = layers * ranks * orows // count
    here = plane.sec * ranks + plane.seq
    there = (layers - 1 - plane.sec) * ranks + plane.seq
    source = (here * orows) // out_rows == place
    source_there = (there * orows) // out_rows == place
    across = plane.partner(1)

    def block(j, k):
        return full.at[pl.ds(pl.multiple_of(j * rows + k * piece, 16), piece), :]

    def oblock(j, k):
        return all_o.at[j, pl.ds(k * opiece, opiece), :]

    def y_copy(k, dst):
        return pltpu.make_async_remote_copy(
            src_ref=theirs.at[pl.ds(k * piece, piece), :], dst_ref=dst, send_sem=y_send.at[k], recv_sem=y_recv.at[k],
            device_id=across, device_id_type=MESH,
        )

    def cut(d, same, first):
        spot = lax.rem(place + d, count)
        return pltpu.make_async_remote_copy(
            src_ref=(mine_o if same else theirs_o).at[spot], dst_ref=all_o.at[spot] if first else next_o,
            send_sem=cut_send.at[0 if same else 1, d], recv_sem=cut_recv.at[0 if first else 1],
            device_id={"section": plane.sec if same else layers - 1 - plane.sec, "fsdp": spot}, device_id_type=MESH,
        )

    def own_cut(first):
        return pltpu.make_async_copy(mine_o.at[place], all_o.at[place] if first else next_o, own_sem.at[3])

    def begin_cuts(same, first, condition):
        @pl.when(condition)
        def _():
            if same:
                own_cut(first).start()
            for d in range(1 if same else 0, count):
                cut(d, same, first).start()

    half = ends_ref.shape[1] // layers
    x_copy = pltpu.make_async_remote_copy(
        src_ref=ends_ref.at[:, pl.ds(pl.multiple_of((layers - 1 - plane.sec) * half, 16), half), :], dst_ref=got_ref,
        send_sem=x_send.at[0], recv_sem=x_recv.at[0], device_id=across, device_id_type=MESH,
    )
    strips = Row(
        place, count, lambda d: strip_ref, lambda d: thin_ref.at[plane.sec, plane.seq, place], st_send, st_recv
    )
    hold = count // 2
    spread = Spread(plane, thin_ref, None, 0, ag_send, ag_recv)
    spread.view = lambda h, mask: thin_ref.at[plane.owner(mask)[0], plane.owner(mask)[1], pl.ds(h * hold, hold)]

    def p_copy(d, same):
        sec = plane.sec if same else layers - 1 - plane.sec
        number = d if same else count + d
        return pltpu.make_async_remote_copy(
            src_ref=packed_ref, dst_ref=params_ref.at[plane.sec, place], send_sem=pa_send.at[number],
            recv_sem=pa_recv.at[number], device_id={"section": sec, "fsdp": lax.rem(place + d, count)},
            device_id_type=MESH,
        )

    pairs = [(d, same) for d in range(count) for same in (True, False) if d or not same]
    own_strip = pltpu.make_async_copy(strip_ref, thin_ref.at[plane.sec, plane.seq, place], own_sem.at[0])
    own_packed = pltpu.make_async_copy(packed_ref, params_ref.at[plane.sec, place], own_sem.at[1])
    own_block = pltpu.make_async_copy(mine, full.at[pl.ds(pl.multiple_of(place * rows, 16), rows), :], own_sem.at[2])
    own_next = pltpu.make_async_copy(mine, next_gx, own_sem.at[2])
    line = Line(place, count, block, parts, send, recv)
    oline = Line(place, count, oblock, oparts, o_send, o_recv)

    chain_barrier(plane, place, count)
    own_strip.start()
    own_packed.start()

    @pl.when(low)
    def _():
        own_block.start()
        for k in range(parts):
            y_copy(k, block(place, k)).start()

    strips.begin()
    for d, same in pairs:
        p_copy(d, same).start()
    begin_cuts(True, True, low & source)

    @pl.when(low)
    def _():
        own_block.wait()

    for k in range(parts):
        @pl.when(~low)
        def _(k=k):
            y_copy(k, block(place, k)).wait_recv()

        line.begin(k)

    @pl.when(low)
    def _():
        for k in range(parts):
            y_copy(k, block(place, k)).wait_send()

    begin_cuts(False, True, low & source_there)
    x_copy.start()
    for k in range(parts):
        line.forward(1, k)

    @pl.when(~low)
    def _():
        own_next.start()
        for k in range(parts):
            y_copy(k, next_gx.at[pl.ds(k * piece, piece), :]).start()

    own_strip.wait()
    strips.finish()
    spread.begin()

    @pl.when(low & source)
    def _():
        own_cut(True).wait()

    @pl.when(~(low & source))
    def _():
        cut(0, True, True).wait_recv()

    for k in range(oparts):
        oline.begin(k)
    spread.hop(0)
    begin_cuts(True, False, ~low & source)
    begin_cuts(False, False, ~low & source_there)
    for d in range(2, count):
        for k in range(parts):
            line.forward(d, k)
        for k in range(oparts):
            oline.forward(d - 1, k)
        if d == 2:
            for stage in range(1, plane.stages):
                spread.hop(stage)
    for k in range(oparts):
        oline.forward(count - 1, k)
    spread.finish()

    own_packed.wait()
    x_copy.wait()

    @pl.when(low)
    def _():
        for k in range(parts):
            y_copy(k, next_gx.at[pl.ds(k * piece, piece), :]).wait_recv()

    @pl.when(~low)
    def _():
        own_next.wait()
        for k in range(parts):
            y_copy(k, block(place, k)).wait_send()

    @pl.when(~low & source)
    def _():
        own_cut(False).wait()

    @pl.when(~(~low & source))
    def _():
        cut(0, True, False).wait_recv()

    @pl.when(source)
    def _():
        for d in range(1, count):
            cut(d, True, False).wait_send()

    @pl.when(source_there)
    def _():
        for d in range(count):
            cut(d, False, False).wait_send()

    for d, same in pairs:
        p_copy(d, same).wait()
    strips.drain()
    spread.drain()
    line.drain()
    oline.drain()


def start_up(mine, theirs, mine_o, theirs_o, ends, strip, packed, number):
    layers, ranks, count = lax.axis_size("section"), lax.axis_size("seq"), lax.axis_size("fsdp")
    parts = 4 if mine.shape[0] % 64 == 0 else 2
    mine_o = mine_o.reshape(count, -1, mine_o.shape[1])
    theirs_o = theirs_o.reshape(mine_o.shape)
    oparts = 2 if mine_o.shape[1] % 32 == 0 else 1
    anywhere = pl.BlockSpec(memory_space=pl.ANY)
    dma = pltpu.SemaphoreType.DMA
    size = layers * ranks
    half = ends.shape[1] // layers
    return pl.pallas_call(
        functools.partial(start_kernel, layers, ranks, parts, oparts),
        in_specs=[anywhere] * 7,
        out_specs=[anywhere] * 7,
        out_shape=[
            jax.ShapeDtypeStruct((count * mine.shape[0], mine.shape[1]), BF16),
            jax.ShapeDtypeStruct(mine_o.shape, BF16),
            jax.ShapeDtypeStruct(mine.shape, BF16),
            jax.ShapeDtypeStruct(mine_o.shape[1:], BF16),
            jax.ShapeDtypeStruct((ends.shape[0], half, ends.shape[2]), BF16),
            jax.ShapeDtypeStruct((layers, ranks, count) + strip.shape, BF16),
            jax.ShapeDtypeStruct((layers, count) + packed.shape, BF16),
        ],
        scratch_shapes=[
            dma((4,)),
            dma((parts,)),
            dma((parts,)),
            dma((1,)),
            dma((1,)),
            dma((2, count, parts)),
            dma((2, count, parts)),
            dma((2, count, oparts)),
            dma((2, count, oparts)),
            dma((2, count)),
            dma((2,)),
            dma((count,)),
            dma((count,)),
            dma((2, size)),
            dma((2, size)),
            dma((2 * count,)),
            dma((2 * count,)),
        ],
        compiler_params=pltpu.CompilerParams(collective_id=number, has_side_effects=True),
        name="start_up",
    )(mine, theirs, mine_o, theirs_o, ends, strip, packed)


def swapped(value, axis):
    count = lax.axis_size(axis)
    return lax.ppermute(value, axis, [(i, count - 1 - i) for i in range(count)])


PLANE = ("section", "seq")
EVERY = ("section", "seq", "fsdp")


def per_device(
    section_ends, norm_gain, in_weight, conv_weight, conv_bias, step_bias, log_decay, skip_gain, gate_gain, out_weight
):
    sec, seq, dep = lax.axis_index("section"), lax.axis_index("seq"), lax.axis_index("fsdp")
    layers, ranks, depth = lax.axis_size("section"), lax.axis_size("seq"), lax.axis_size("fsdp")
    group = layers * ranks
    here = sec * ranks + seq
    there = (layers - 1 - sec) * ranks + seq
    low_layer = sec == 0
    width = in_weight.shape[1] * depth
    inner = gate_gain.shape[1] * depth
    chans = conv_bias.shape[1] * depth
    heads_all = step_bias.shape[1] * depth
    taps = conv_weight.shape[1]
    cw = inner // group
    heads = cw // HEAD
    shared = 2 * STATE

    ends = section_ends[0, :, 0]
    piece = ends.shape[1] // layers

    def head_columns(v, begin, count):
        return lax.dynamic_slice_in_dim(v, begin, count, v.ndim - 1)

    def own_columns(rank):
        return jnp.concatenate(
            [head_columns(in_weight[0], rank * cw, cw), head_columns(in_weight[0], inner + rank * cw, cw)], 1
        )

    out_rows = out_weight.shape[1]

    def own_rows(rank):
        start = jnp.clip(rank * cw - dep * out_rows, 0, out_rows - cw)
        return lax.dynamic_slice_in_dim(out_weight[0], start, cw, 0)

    strip = in_weight.shape[1] // ranks
    thin = lax.dynamic_slice(in_weight[0], (seq * strip, inner + chans - shared), (strip, shared + heads_all))
    thin = jnp.pad(thin, ((0, 0), (0, STATE - heads_all)))
    flat = [norm_gain, conv_weight, conv_bias, step_bias, log_decay, skip_gain, gate_gain]
    sizes = [v.size for v in flat]
    packed = jnp.concatenate([v.reshape(-1) for v in flat])
    packed = jnp.pad(packed, (0, -packed.size % 2048)).reshape(-1, STATE)
    wgx, wo, next_gx, next_o, got, thin, packed = start_up(
        own_columns(here), own_columns(there), own_rows(here), own_rows(there), ends, thin, packed, 0
    )
    packed = packed.reshape(layers, depth, -1).astype(F32)
    thin = jnp.transpose(thin, (0, 2, 1, 3, 4)).reshape(layers, width, -1)
    hidden = jnp.where(low_layer, ends[:, :piece], got).astype(F32).reshape(layers * piece, width)
    cot = jnp.where(low_layer, got, ends[:, piece:]).astype(F32).reshape(layers * piece, width)

    def own_tokens(v):
        v = lax.dynamic_slice_in_dim(v, seq, 1, 1)[:, 0]
        return lax.dynamic_slice_in_dim(v, sec * piece, piece, 1).reshape(-1, 1)

    def member(layer, number):
        begin = sum(sizes[:number])
        return packed[layer, :, begin : begin + sizes[number]]

    def vectors(layer):
        kernel = jnp.transpose(member(layer, 1).reshape(depth, taps, -1), (1, 0, 2)).reshape(taps, chans)
        rows = jnp.concatenate([kernel, member(layer, 2).reshape(1, chans)], 0)
        rows = jnp.concatenate([head_columns(rows, here * cw, cw), rows[:, inner:]], 1)
        total = cw + shared

        def padded(v):
            return jnp.pad(v[None], ((0, 0), (0, total - v.shape[0])))

        gain = head_columns(member(layer, 6).reshape(-1), here * cw, cw)
        by_head = [head_columns(member(layer, n).reshape(-1), here * heads, heads) for n in (3, 4, 5)]
        return jnp.concatenate(
            [rows, jnp.zeros((5 - taps - 1, total), F32), padded(gain), padded(by_head[0]), padded(by_head[1]),
             padded(jnp.repeat(by_head[2], HEAD)), jnp.zeros((7, total), F32)], 0)

    gains = [member(layer, 0).reshape(1, -1) for layer in range(layers)]
    vecs = [vectors(layer) for layer in range(layers)]

    saved, weights = [], []
    for layer in range(layers):
        ws, wo = thin[layer], wo.reshape(cw, width)
        weights.append((wgx, ws, wo))
        rs = lax.rsqrt(jnp.mean(hidden * hidden, axis=-1, keepdims=True) + EPS)
        following = (next_gx, next_o) if layer + 1 < layers else ()
        raw, ss, pgx, ps, res, ent, full, *after = layer_forward(
            (hidden * rs * gains[layer]).astype(BF16), wgx, ws, wo, vecs[layer], taps, 2 * layers + layer, *following
        )
        if after:
            wgx, wo = after
        r_rows = lax.rsqrt(ss / inner + EPS)
        r = own_tokens(r_rows)
        saved.append((hidden, rs, full, pgx, ps, res, ent, raw, r, r_rows))
        hidden = hidden + r * raw
        if layer + 1 < layers:
            hidden = hidden.astype(BF16).astype(F32)
    output = hidden

    grad = cot
    big, small = [None] * layers, [None] * layers
    for layer in reversed(range(layers)):
        wgx, ws, wo = weights[layer]
        before, rs, full, pgx, ps, res, ent, raw, r, r_rows = saved[layer]
        low = grad.astype(BF16)
        pull = r * r * r * jnp.sum(low.astype(F32) * raw, axis=-1, keepdims=True) / inner
        pull = jnp.broadcast_to(pull.reshape(layers, 1, piece), (layers, 8, piece))
        gn, gpgx, gps, no, tiny, gb = layer_backward(
            low, pull, r_rows, pgx, ps, res, ent, wgx, ws, wo, vecs[layer], taps, 3 * layers + layer
        )
        g_gx, g_o = reduce_gradients(full, gpgx, no, gb, layers + layer)
        g_s = dot(full, gps, 0, 0).astype(BF16)
        unit = before * rs
        g_gain = jnp.sum(gn * unit, axis=0)
        gn = gn * gains[layer]
        grad = grad + rs * (gn - unit * jnp.mean(gn * unit, axis=-1, keepdims=True))
        if layer > 0:
            grad = grad.astype(BF16).astype(F32)

        def placed(v, count, begin):
            return lax.dynamic_update_slice(jnp.zeros((count,), F32), v, (begin,))

        conv = lax.dynamic_update_slice(jnp.zeros((taps + 1, chans), F32), tiny[: taps + 1, :cw], (0, here * cw))
        conv = conv + jnp.pad(tiny[: taps + 1, cw:], ((0, 0), (inner, 0)))
        small[layer] = jnp.concatenate(
            [g_gain, conv.reshape(-1), placed(tiny[5, :cw], inner, here * cw)]
            + [placed(tiny[n, :heads], heads_all, here * heads) for n in (6, 7, 8)]
        )
        g_s = g_s[:, : shared + heads_all]
        g_s = lax.psum_scatter(g_s, "fsdp", scatter_dimension=0, tiled=True)
        big[layer] = (g_gx, g_s, g_o)

    output = output.reshape(layers, piece, width)
    grad = grad.reshape(layers, piece, width)
    got = swapped(jnp.where(low_layer, output, grad).astype(BF16), "section").astype(F32)
    results = jnp.where(low_layer, jnp.concatenate([grad, got], 1), jnp.concatenate([got, output], 1))
    section_results = results[None, :, None]

    def own_layer(values):
        own = jnp.where(low_layer, values[0], values[1])
        other = jnp.where(low_layer, values[1], values[0])
        return own, other

    own, other = own_layer([b[0] for b in big])
    other = swapped(other, "section")
    pair = jnp.stack([jnp.where(low_layer, own, other), jnp.where(low_layer, other, own)])
    gx = lax.all_gather(pair, "seq")
    rows = gx.shape[2]
    gx = gx.reshape(ranks, layers, rows, 2, cw)
    gx = jnp.transpose(gx, (2, 3, 1, 0, 4)).reshape(rows, 2 * inner)
    s_all = lax.psum(jnp.stack([b[1] for b in big]), PLANE)
    s_own, _ = own_layer([s_all[0], s_all[1]])
    grad_in = jnp.concatenate([gx.astype(F32), s_own.astype(F32)], 1)[None]

    own, other = own_layer([b[2] for b in big])
    other = swapped(other, "section")
    pair = jnp.stack([jnp.where(low_layer, own, other), jnp.where(low_layer, other, own)])
    spread = jnp.zeros((out_rows, width), BF16)
    for s in range(layers):
        start = (s * ranks + seq) * cw - dep * out_rows
        inside = (start >= 0) & (start < out_rows)
        block = jnp.where(inside, pair[s], jnp.zeros_like(pair[s]))
        spread = spread + lax.dynamic_update_slice(jnp.zeros_like(spread), block, (jnp.clip(start, 0, out_rows - cw), 0))
    grad_out = lax.psum(spread, "seq").astype(F32)[None]

    tiny = lax.psum(jnp.stack(small), EVERY)
    tiny = jnp.where(low_layer, tiny[0], tiny[1])
    cuts = np.cumsum([0, width, taps * chans, chans, inner, heads_all, heads_all, heads_all])
    parts = [tiny[cuts[i] : cuts[i + 1]] for i in range(7)]

    def share(v):
        count = v.shape[-1] // depth
        return lax.dynamic_slice_in_dim(v, dep * count, count, v.ndim - 1)[None]

    return (
        section_results,
        share(parts[0]),
        grad_in,
        share(parts[1].reshape(taps, chans)),
        share(parts[2]),
        share(parts[4]),
        share(parts[5]),
        share(parts[6]),
        share(parts[3]),
        grad_out,
    )


def solution(mesh):
    weight = P("section", "fsdp")
    matrix = P("section", "fsdp", None)
    ends = P("section", None, "fsdp", "seq", None)
    kernel = P("section", None, "fsdp")
    return jax.shard_map(
        per_device,
        mesh=mesh,
        in_specs=(ends, weight, matrix, kernel, weight, weight, weight, weight, weight, matrix),
        out_specs=(ends, weight, matrix, kernel, weight, weight, weight, weight, weight, matrix),
        check_vma=False,
    )
```

```python
import functools

import jax
import jax.numpy as jnp
import numpy as np
from jax import lax
from jax.experimental import pallas as pl
from jax.experimental.pallas import tpu as pltpu
from jax.sharding import PartitionSpec as P

SPAN = 256
HEAD = 64
STATE = 128
EPS = 1e-05
F32 = jnp.float32
BF16 = jnp.bfloat16


def dot(a, b, ca, cb):
    return lax.dot_general(a, b, (((ca,), (cb,)), ((), ())), preferred_element_type=F32)


def split3(v):
    hi = v.astype(BF16)
    rest = v - hi.astype(F32)
    mid = rest.astype(BF16)
    low = (rest - mid.astype(F32)).astype(BF16)
    return hi, mid, low


def sigmoid(v):
    return 1.0 / (1.0 + jnp.exp(-v))


def running_conv(pad_ref, vec_ref, taps):
    run = vec_ref[taps : taps + 1, :] + vec_ref[0:1, :] * pad_ref[pl.ds(8 - taps + 1, SPAN), :]
    for k in range(1, taps):
        run = run + vec_ref[k : k + 1, :] * pad_ref[pl.ds(8 - taps + 1 + k, SPAN), :]
    return run


def step_sizes(dt_raw, vec_ref, tri):
    x = dt_raw + vec_ref[6:7, :STATE]
    e = jnp.exp(-jnp.abs(x))
    dt = jnp.maximum(x, 0.0) + jnp.log1p(e)
    decay = jnp.exp(vec_ref[7:8, :STATE])
    rate = -dt * decay
    hi, mid, low = split3(rate)
    packed = dot(tri, jnp.concatenate([hi, mid, low], 1), 1, 0)
    cum = packed[:, :STATE] + packed[:, STATE : 2 * STATE] + packed[:, 2 * STATE :]
    return x, e, dt, decay, rate, cum


def expand(v, spread3):
    return dot(jnp.concatenate(split3(v), 1), spread3, 1, 0)


def per_head(v, gather3):
    return dot(jnp.concatenate(split3(v), 1), gather3, 1, 0)


def fading(cum, cum_t, dt_t, h, inside):
    spread = cum[:, h : h + 1] - cum_t[h : h + 1, :]
    return jnp.exp(jnp.where(inside, spread, -1e30)) * dt_t[h : h + 1, :]


def inside_mask():
    rows = lax.broadcasted_iota(jnp.int32, (SPAN, SPAN), 0)
    cols = lax.broadcasted_iota(jnp.int32, (SPAN, SPAN), 1)
    return cols <= rows


MESH = pl.DeviceIdType.MESH


class Plane:
    def __init__(self, layers, ranks):
        self.layers, self.ranks = layers, ranks
        self.sec, self.seq = lax.axis_index("section"), lax.axis_index("seq")
        self.low = lax.rem(self.seq, 2)
        count = ranks.bit_length() - 1
        outer = list(range(1, count + 1))
        self.size = layers * ranks
        self.orders = (outer, outer[::-1])
        self.stages = len(outer)
        self.masks = [m for m in range(self.size) if m % 2 == 0]

    def weight(self, dim):
        return 1 if dim == 0 else 1 << (dim - 1)

    def flipped(self, dim):
        w = self.weight(dim)
        return self.seq + (1 - 2 * lax.rem(self.seq // w, 2)) * w

    def partner(self, dim):
        if dim == 1:
            return {"section": self.layers - 1 - self.sec}
        return {"seq": self.flipped(dim)}

    def owner(self, mask):
        seq = self.seq
        for dim in range(self.stages + 1):
            if dim != 1 and mask >> dim & 1:
                w = self.weight(dim)
                seq = seq + (1 - 2 * lax.rem(self.seq // w, 2)) * w
        sec = self.layers - 1 - self.sec if mask & 2 else self.sec
        return sec, seq

    def device(self, mask):
        sec, seq = self.owner(mask)
        return {"section": sec, "seq": seq}

    def arrival(self, half, mask):
        order = self.orders[half]
        return max(i for i, dim in enumerate(order) if mask >> dim & 1)

    def own_lanes(self, v, heads):
        return pltpu.roll(v, STATE - (self.sec * self.ranks + self.seq) * heads, 1)

    def all_lanes(self, v, heads):
        return pltpu.roll(v, (self.sec * self.ranks + self.seq) * heads, 1)

    def barrier(self):
        sem = pltpu.get_barrier_semaphore()
        for mask in range(1, self.size):
            pl.semaphore_signal(sem, inc=1, device_id=self.device(mask), device_id_type=MESH)
        pl.semaphore_wait(sem, self.size - 1)


class Spread:
    def __init__(self, plane, ref, start, rows, send, recv):
        self.plane, self.ref, self.start, self.rows, self.send, self.recv = plane, ref, start, rows, send, recv

    def view(self, half, mask):
        sec, seq = self.plane.owner(mask)
        count = self.rows // 2
        return self.ref.at[pl.ds(pl.multiple_of(self.start(sec, seq) + half * count, 16), count), :]

    def copy(self, half, mask, dim):
        view = self.view(half, mask)
        key = mask ^ (1 << dim)
        return pltpu.make_async_remote_copy(
            src_ref=view, dst_ref=view, send_sem=self.send.at[half, key], recv_sem=self.recv.at[half, key],
            device_id=self.plane.partner(dim), device_id_type=MESH,
        )

    def arrived(self, half, mask):
        view = self.view(half, mask)
        pltpu.make_async_remote_copy(
            src_ref=view, dst_ref=view, send_sem=self.send.at[half, mask], recv_sem=self.recv.at[half, mask],
            device_id=self.plane.partner(0), device_id_type=MESH,
        ).wait_recv()

    def begin(self):
        for stage in range(self.plane.stages):
            for half in (0, 1):
                self.copy(half, 0, self.plane.orders[half][stage]).start()
        for half in (0, 1):
            self.copy(half, 0, 0).start()

    def hop(self, stage):
        for half in (0, 1):
            order = self.plane.orders[half]
            for mask in self.plane.masks[1:]:
                if self.plane.arrival(half, mask) == stage:
                    self.arrived(half, mask)
                    for later in order[stage + 1 :]:
                        self.copy(half, mask, later).start()
                    self.copy(half, mask, 0).start()

    def finish(self):
        for half in (0, 1):
            for mask in self.plane.masks:
                self.arrived(half, mask + 1)

    def drain(self):
        for half in (0, 1):
            for mask in range(1, self.plane.size):
                self.copy(half, mask ^ 1, 0).wait_send()


class Collect:
    def __init__(self, plane, ref, base, span, core_in, stage_in, core_send, core_recv, send, recv):
        self.plane, self.ref, self.base, self.blocks, self.span = plane, ref, base, plane.ranks, span
        self.core_in, self.stage_in = core_in, stage_in
        self.core_send, self.core_recv, self.send, self.recv = core_send, core_recv, send, recv

    def core_copy(self, c):
        return pltpu.make_async_remote_copy(
            src_ref=self.ref.at[pl.ds(self.base + c * self.span, self.span), :], dst_ref=self.core_in.at[c // 2],
            send_sem=self.core_send.at[c], recv_sem=self.core_recv.at[c],
            device_id=self.plane.partner(0), device_id_type=MESH,
        )

    def block_done(self, c):
        @pl.when(self.plane.low != c % 2)
        def _():
            self.core_copy(c).start()

    def block_add(self, c):
        @pl.when(self.plane.low == c % 2)
        def _():
            self.core_copy(c).wait_recv()
            rows = pl.ds(self.base + c * self.span, self.span)
            self.ref[rows, :] = (self.ref[rows, :].astype(F32) + self.core_in[c // 2].astype(F32)).astype(BF16)

    def rows(self, half, mask):
        sec, seq = self.plane.owner(mask)
        count = self.span // self.plane.layers // 2
        begin = self.base + seq * self.span + sec * (2 * count) + half * count
        return pl.ds(pl.multiple_of(begin, 16), count)

    def copy(self, half, mask, dim):
        return pltpu.make_async_remote_copy(
            src_ref=self.ref.at[self.rows(half, mask), :], dst_ref=self.stage_in.at[half, mask // 2],
            send_sem=self.send.at[half, mask // 2], recv_sem=self.recv.at[half, mask // 2],
            device_id=self.plane.partner(dim), device_id_type=MESH,
        )

    def plan(self, stage):
        for half in (0, 1):
            order = self.plane.orders[half][::-1]
            for mask in self.plane.masks[1:]:
                if mask >> order[stage] & 1 and not any(mask >> dim & 1 for dim in order[:stage]):
                    yield half, mask, order[stage]

    def begin(self, stage):
        for half, mask, dim in self.plan(stage):
            self.copy(half, mask, dim).start()

    def add(self, stage, out_ref=None, out_base=0):
        for half, mask, dim in self.plan(stage):
            self.copy(half, mask, dim).wait_recv()
            rows = self.rows(half, mask ^ (1 << dim))
            value = self.ref[rows, :].astype(F32) + self.stage_in[half, mask // 2].astype(F32)
            if stage == self.plane.stages - 1:
                count = value.shape[0]
                out_ref[pl.ds(out_base + half * count, count), :] = value
            else:
                self.ref[rows, :] = value.astype(BF16)

    def drain(self):
        for c in range(self.blocks):
            @pl.when(self.plane.low != c % 2)
            def _(c=c):
                self.core_copy(c).wait_send()

        for stage in range(self.plane.stages):
            for half, mask, dim in self.plan(stage):
                self.copy(half, mask, dim).wait_send()


class Share:
    def __init__(self, plane, source, target, send, recv):
        self.plane, self.source, self.target, self.send, self.recv = plane, source, target, send, recv

    def copy(self, mask):
        return pltpu.make_async_remote_copy(
            src_ref=self.source, dst_ref=self.target(mask), send_sem=self.send.at[mask],
            recv_sem=self.recv.at[mask], device_id=self.plane.device(mask), device_id_type=MESH,
        )

    def begin(self):
        for mask in range(1, self.plane.size):
            self.copy(mask).start()

    def finish(self):
        for mask in range(1, self.plane.size):
            self.copy(mask).wait_recv()

    def drain(self):
        for mask in range(1, self.plane.size):
            self.copy(mask).wait_send()


def chain_barrier(plane, place, count):
    sem = pltpu.get_barrier_semaphore()
    for mask in range(1, plane.size):
        pl.semaphore_signal(sem, inc=1, device_id=plane.device(mask), device_id_type=MESH)
    for d in range(1, count):
        other = lax.rem(place + d, count)
        for sec in (plane.sec, plane.layers - 1 - plane.sec):
            pl.semaphore_signal(sem, inc=1, device_id={"section": sec, "fsdp": other}, device_id_type=MESH)
    pl.semaphore_wait(sem, plane.size - 1 + 2 * (count - 1))


class Row:
    def __init__(self, place, count, source, target, send, recv):
        self.place, self.count, self.source, self.target, self.send, self.recv = place, count, source, target, send, recv

    def copy(self, d):
        return pltpu.make_async_remote_copy(
            src_ref=self.source(d), dst_ref=self.target(d), send_sem=self.send.at[d], recv_sem=self.recv.at[d],
            device_id={"fsdp": lax.rem(self.place + d, self.count)}, device_id_type=MESH,
        )

    def begin(self):
        for d in range(1, self.count):
            self.copy(d).start()

    def finish(self):
        for d in range(1, self.count):
            self.copy(d).wait_recv()

    def drain(self):
        for d in range(1, self.count):
            self.copy(d).wait_send()


class Line:
    def __init__(self, place, count, block, parts, send, recv):
        self.place, self.count, self.block, self.parts, self.send, self.recv = place, count, block, parts, send, recv
        self.ends = (place < count - 1, place > 0)

    def hop(self, side, d, k):
        j = self.place - d if side == 0 else self.place + d
        return pltpu.make_async_remote_copy(
            src_ref=self.block(j, k), dst_ref=self.block(j, k), send_sem=self.send.at[side, d, k],
            recv_sem=self.recv.at[side, d, k], device_id={"fsdp": self.place + 1 if side == 0 else self.place - 1},
            device_id_type=MESH,
        )

    def arrived(self, side, d, k):
        j = self.place - d if side == 0 else self.place + d
        pltpu.make_async_remote_copy(
            src_ref=self.block(j, k), dst_ref=self.block(j, k), send_sem=self.send.at[side, d, k],
            recv_sem=self.recv.at[side, d - 1, k], device_id={"fsdp": self.place + 1 if side == 0 else self.place - 1},
            device_id_type=MESH,
        ).wait_recv()

    def have(self, side, d):
        return self.place >= d if side == 0 else self.place + d < self.count

    def begin(self, k):
        for side in (0, 1):
            @pl.when(self.ends[side])
            def _(side=side):
                self.hop(side, 0, k).start()

    def forward(self, d, k):
        for side in (0, 1):
            @pl.when(self.have(side, d))
            def _(side=side):
                self.arrived(side, d, k)

            if d < self.count - 1:
                @pl.when(self.have(side, d) & self.ends[side])
                def _(side=side):
                    self.hop(side, d, k).start()

    def drain(self):
        for k in range(self.parts):
            for d in range(self.count - 1):
                for side in (0, 1):
                    @pl.when(self.have(side, d) & self.ends[side])
                    def _(side=side, d=d, k=k):
                        self.hop(side, d, k).wait_send()


def forward_kernel(
    layers, heads, blocks, taps, ahead, *refs
):
    own_ref, wgx_ref, ws_ref, wo_ref, vec_ref, tri_ref, spread_ref = refs[:7]
    refs = refs[7:]
    if ahead:
        next_gx, next_o = refs[:2]
        refs = refs[2:]
    raw_ref, ss_ref, pgx_ref, ps_ref, res_ref, ent_ref, full_out_ref = refs[:7]
    refs = refs[7:]
    if ahead:
        ahead_gx, ahead_o = refs[:2]
        refs = refs[2:]
    full_ref, part_ref, pad_ref, state_ref, within_ref, ss_mine, ss_in, core_in, stage_in = refs[:9]
    out_sem, ag_send, ag_recv, core_send, core_recv, rs_send, rs_recv, ss_send, ss_recv = refs[9:18]
    cw = heads * HEAD
    t = pl.program_id(0)
    steps = layers * blocks
    plane = Plane(layers, blocks)
    piece = SPAN // layers
    length = blocks * SPAN

    def start(m):
        return lambda sec, seq: m * length + seq * SPAN + sec * piece

    gathers = [Spread(plane, full_ref, start(m), piece, ag_send.at[m], ag_recv.at[m]) for m in range(layers)]
    sums = [
        Collect(plane, part_ref, m * length, SPAN, core_in.at[m], stage_in.at[m], core_send.at[m], core_recv.at[m],
                rs_send.at[m], rs_recv.at[m])
        for m in range(layers)
    ]
    shares = [
        Share(plane, ss_mine.at[m], lambda mask, m=m: ss_in.at[m, mask], ss_send.at[m], ss_recv.at[m])
        for m in range(layers)
    ]

    def keep(m):
        rows = pl.ds(m * length, length)
        return pltpu.make_async_copy(full_ref.at[rows, :], full_out_ref.at[rows, :], out_sem.at[m])

    if ahead:
        own_sem, row_send, row_recv, o_send, o_recv = refs[18:]
        spot, count = lax.axis_index("fsdp"), lax.axis_size("fsdp")
        grows = next_gx.shape[0]
        target = ahead_gx.at[pl.ds(pl.multiple_of(spot * grows, 16), grows), :]
        row = Row(spot, count, lambda d: next_gx, lambda d: target, row_send, row_recv)
        orow = Row(spot, count, lambda d: next_o, lambda d: ahead_o.at[spot], o_send, o_recv)
        own_gx = pltpu.make_async_copy(next_gx, target, own_sem.at[0])
        own_o = pltpu.make_async_copy(next_o, ahead_o.at[spot], own_sem.at[1])

        @pl.when(t == 0)
        def _():
            chain_barrier(plane, spot, count)
            own_gx.start()
            own_o.start()

    @pl.when(t == 0)
    def _():
        for m in range(layers):
            rows = pl.multiple_of(start(m)(plane.sec, plane.seq), 16)
            full_ref[pl.ds(rows, piece), :] = own_ref[m * piece : (m + 1) * piece, :]
        ss_mine[...] = jnp.zeros_like(ss_mine)
        if not ahead:
            plane.barrier()
        gathers[0].begin()
        if ahead:
            row.begin()
            orow.begin()
        gathers[0].hop(0)
        gathers[1].begin()
        for stage in range(1, plane.stages):
            gathers[0].hop(stage)
        gathers[0].finish()
        keep(0).start()

    @pl.when(t == blocks)
    def _():
        gathers[1].finish()
        keep(1).start()

    first = lax.rem(t, blocks) == 0

    @pl.when(first)
    def _():
        pad_ref[pl.ds(SPAN, 8), :] = jnp.zeros((8, pad_ref.shape[1]), F32)
        state_ref[...] = jnp.zeros_like(state_ref)

    x = full_ref[pl.ds(pl.multiple_of(t * SPAN, SPAN), SPAN), :]
    pgx = dot(x, wgx_ref[...], 1, 0).astype(BF16)
    ps = dot(x, ws_ref[...], 1, 0).astype(BF16)
    pgx_ref[...] = pgx
    ps_ref[...] = ps
    pad_ref[pl.ds(0, 8), :] = pad_ref[pl.ds(SPAN, 8), :]
    pad_ref[pl.ds(8, SPAN), :cw] = pgx[:, cw:].astype(F32)
    pad_ref[pl.ds(8, SPAN), cw:] = ps[:, : 2 * STATE].astype(F32)
    run = running_conv(pad_ref, vec_ref, taps)
    mixed = (run * sigmoid(run)).astype(BF16)
    xs, b, c = mixed[:, :cw], mixed[:, cw : cw + STATE], mixed[:, cw + STATE :]
    _, _, dt, _, _, cum = step_sizes(plane.own_lanes(ps[:, 2 * STATE :].astype(F32), heads), vec_ref, tri_ref[...])
    cum_t, dt_t = cum.T, dt.T
    inside = inside_mask()
    scores = dot(c, b, 1, 1)
    for h in range(heads):
        mixing = (scores * fading(cum, cum_t, dt_t, h, inside)).astype(BF16)
        within_ref[:, h * HEAD : (h + 1) * HEAD] = dot(mixing, xs[:, h * HEAD : (h + 1) * HEAD], 1, 0)
    tail = jnp.exp(cum[SPAN - 1 : SPAN, :] - cum) * dt
    growth = jnp.exp(cum)
    both = expand(jnp.concatenate([tail, growth], 0), spread_ref[...])
    tail_e, growth_e = both[:SPAN], both[SPAN:]
    xs_f = xs.astype(F32)
    state = state_ref[...]
    state_low = state.astype(BF16)
    ent_ref[0] = state_low
    reach = dot(c, state_low, 1, 0)
    state_ref[...] = growth_e[SPAN - 1 : SPAN, :] * state + dot(b, (xs_f * tail_e).astype(BF16), 0, 0)
    result = (within_ref[...] + growth_e * reach + vec_ref[8:9, :cw] * xs_f).astype(BF16)
    res_ref[...] = result
    gate = pgx[:, :cw].astype(F32)
    g = result.astype(F32) * (gate * sigmoid(gate))
    ss = jnp.sum(g * g, axis=1, keepdims=True)
    ss_mine[t // blocks, pl.ds(lax.rem(t, blocks), 1), :] = jnp.broadcast_to(ss, (SPAN, STATE)).T[0:1, :]
    part_ref[pl.ds(pl.multiple_of(t * SPAN, SPAN), SPAN), :] = dot(
        (g * vec_ref[5:6, :cw]).astype(BF16), wo_ref[...], 1, 0
    ).astype(BF16)

    for m in range(layers):
        for c in range(blocks):
            @pl.when(t == m * blocks + c)
            def _(m=m, c=c):
                sums[m].block_done(c)

    for stage in range(plane.stages):
        @pl.when(t == min(stage * 2, blocks - 1))
        def _(stage=stage):
            gathers[1].hop(stage)

    @pl.when(t == blocks - 1)
    def _():
        shares[0].begin()

    @pl.when(t == blocks)
    def _():
        for c in range(blocks):
            sums[0].block_add(c)
        sums[0].begin(0)

    for stage in range(plane.stages):
        @pl.when(t == blocks + 1 + stage)
        def _(stage=stage):
            sums[0].add(stage, raw_ref, 0)
            if stage + 1 < plane.stages:
                sums[0].begin(stage + 1)

    for c in range(blocks - 1):
        @pl.when(t == blocks + c + 1)
        def _(c=c):
            sums[1].block_add(c)

    @pl.when(t == steps - 1)
    def _():
        shares[1].begin()
        sums[1].block_add(blocks - 1)
        sums[1].begin(0)
        for m in range(layers):
            shares[m].finish()
            total = ss_mine[m]
            for mask in range(1, plane.size):
                total = total + ss_in[m, mask]
            ss_ref[m] = total
        for m in range(layers):
            gathers[m].drain()
            keep(m).wait()
            shares[m].drain()
        sums[0].drain()
        for stage in range(plane.stages):
            sums[1].add(stage, raw_ref, piece)
            if stage + 1 < plane.stages:
                sums[1].begin(stage + 1)
        sums[1].drain()
        if ahead:
            own_gx.wait()
            own_o.wait()
            for each in (row, orow):
                each.finish()
                each.drain()


def backward_kernel(
    layers, heads, blocks, taps,
    own_ref, pull_own, r_ref, pgx_ref, ps_ref, hgx_ref, hs_ref, res_ref, ent_ref,
    wgx_ref, ws_ref, wo_ref, vec_ref, tri_ref, spread_ref, gather_ref,
    raw_ref, gpgx_ref, gps_ref, no_ref, small_ref, full_out_ref,
    full_ref, part_ref, pad_ref, next_ref, ge_ref, within_ref, gxm_ref, pull_ref, core_in, stage_in,
    out_sem, ag_send, ag_recv, core_send, core_recv, rs_send, rs_recv, ss_send, ss_recv,
):
    cw = heads * HEAD
    t = pl.program_id(0)
    steps = layers * blocks
    place = lax.rem(t, blocks)
    micro, block = t // blocks, blocks - 1 - place
    plane = Plane(layers, blocks)
    piece = SPAN // layers
    length = blocks * SPAN
    rows_now = pl.ds(pl.multiple_of(micro * length + block * SPAN, SPAN), SPAN)

    def start(m):
        return lambda sec, seq: m * length + seq * SPAN + sec * piece

    gathers = [Spread(plane, full_ref, start(m), piece, ag_send.at[m], ag_recv.at[m]) for m in range(layers)]
    collects = [
        Collect(plane, part_ref, m * length, SPAN, core_in.at[m], stage_in.at[m], core_send.at[m], core_recv.at[m],
                rs_send.at[m], rs_recv.at[m])
        for m in range(layers)
    ]

    def pull_place(sec, seq):
        return pull_ref.at[:, seq, :, pl.ds(pl.multiple_of(sec * piece, piece), piece)]

    share = Share(plane, pull_own, lambda mask: pull_place(plane.sec, plane.seq), ss_send, ss_recv)

    def saving(m):
        rows = pl.ds(m * length, length)
        return pltpu.make_async_copy(full_ref.at[rows, :], full_out_ref.at[rows, :], out_sem.at[m])

    @pl.when(t == 0)
    def _():
        small_ref[...] = jnp.zeros_like(small_ref)
        for m in range(layers):
            rows = pl.multiple_of(start(m)(plane.sec, plane.seq), 16)
            full_ref[pl.ds(rows, piece), :] = own_ref[m * piece : (m + 1) * piece, :]
        for m in range(layers):
            pull_ref[m, plane.seq, :, pl.ds(pl.multiple_of(plane.sec * piece, piece), piece)] = pull_own[m]
        plane.barrier()
        share.begin()
        gathers[0].begin()
        gathers[0].hop(0)
        gathers[1].begin()
        for stage in range(1, plane.stages):
            gathers[0].hop(stage)
        gathers[0].finish()
        share.finish()
        saving(0).start()

    @pl.when(t == blocks)
    def _():
        gathers[1].finish()
        saving(1).start()

    @pl.when(place == 0)
    def _():
        next_ref[pl.ds(0, 8), :] = jnp.zeros((8, next_ref.shape[1]), F32)
        ge_ref[...] = jnp.zeros_like(ge_ref)

    pgx, ps = pgx_ref[...], ps_ref[...]
    keep = jnp.where(place == blocks - 1, 0.0, 1.0)
    pad_ref[pl.ds(0, 8), :cw] = hgx_ref[8:, cw:].astype(F32) * keep
    pad_ref[pl.ds(0, 8), cw:] = hs_ref[8:, : 2 * STATE].astype(F32) * keep
    pad_ref[pl.ds(8, SPAN), :cw] = pgx[:, cw:].astype(F32)
    pad_ref[pl.ds(8, SPAN), cw:] = ps[:, : 2 * STATE].astype(F32)
    run = running_conv(pad_ref, vec_ref, taps)
    sig = sigmoid(run)
    mixed = (run * sig).astype(BF16)
    slope = sig * (1.0 + run * (1.0 - sig))
    xs, b, c = mixed[:, :cw], mixed[:, cw : cw + STATE], mixed[:, cw + STATE :]
    xs_f = xs.astype(F32)
    tri = tri_ref[...]
    x, e, dt, decay, rate, cum = step_sizes(plane.own_lanes(ps[:, 2 * STATE :].astype(F32), heads), vec_ref, tri)
    cum_t, dt_t = cum.T, dt.T
    tail = jnp.exp(cum[SPAN - 1 : SPAN, :] - cum) * dt
    growth = jnp.exp(cum)
    both = expand(jnp.concatenate([tail, growth], 0), spread_ref[...])
    tail_e, growth_e = both[:SPAN], both[SPAN:]

    gu = dot(full_ref[rows_now, :], wo_ref[...], 1, 1)
    r = jnp.broadcast_to(r_ref[micro, pl.ds(block, 1), :], (STATE, SPAN)).T[:, 0:1]
    pull = jnp.broadcast_to(pull_ref[micro, block][0:1, :], (STATE, SPAN)).T[:, 0:1]
    gain = vec_ref[5:6, :cw]
    gate = pgx[:, :cw].astype(F32)
    sg = sigmoid(gate)
    sl = gate * sg
    res = res_ref[...].astype(F32)
    g = res * sl
    rg = r * g
    no_ref[...] = (rg * gain).astype(BF16)
    dg = r * (gu * gain) - pull * g
    gr = (dg * sl).astype(BF16)
    gr_f = gr.astype(F32)
    ggate = dg * res * (sg + sl * (1.0 - sg))

    ent = ent_ref[0]
    ge = ge_ref[...]
    gl = ge.astype(BF16)
    reach = dot(c, ent, 1, 0)
    pulled = tail_e * dot(b, gl, 1, 0)
    gq = (growth_e * gr_f).astype(BF16)
    grad_c = dot(gq, ent, 1, 1)
    grad_b = dot((xs_f * tail_e).astype(BF16), gl, 1, 1)
    fade = growth_e[SPAN - 1 : SPAN, :]
    ge_ref[...] = fade * ge + dot(c, gq, 0, 0)
    grad_fade = fade * jnp.sum(ge * ent.astype(F32), axis=0, keepdims=True)
    inside = inside_mask()
    scores = dot(c, b, 1, 1)
    gs = jnp.zeros((SPAN, SPAN), F32)
    for h in range(heads):
        cols = slice(h * HEAD, (h + 1) * HEAD)
        fade_in = fading(cum, cum_t, dt_t, h, inside)
        mixing = (scores * fade_in).astype(BF16)
        gs = gs + dot(gr[:, cols], xs[:, cols], 1, 1) * fade_in
        within_ref[:, cols] = dot(mixing, xs[:, cols], 1, 0)
        gxm_ref[:, cols] = dot(mixing, gr[:, cols], 0, 0)
    gs = gs.astype(BF16)
    grad_c = grad_c + dot(gs, b, 1, 0)
    grad_b = grad_b + dot(gs, c, 0, 0)
    gxm = gxm_ref[...]
    grad_x = vec_ref[8:9, :cw] * gr_f + pulled + gxm

    gather = gather_ref[...]
    tall = jnp.concatenate([gr_f * (within_ref[...] + growth_e * reach), xs_f * gxm, xs_f * pulled], 0)
    sums = per_head(tall, gather)
    s1, s2, s3 = sums[:SPAN], sums[SPAN : 2 * SPAN], sums[2 * SPAN :]
    thin = jnp.concatenate(
        [jnp.sum(gr_f * xs_f, axis=0, keepdims=True), grad_fade, jnp.zeros((6, cw), F32)], 0
    )
    thin = per_head(thin, gather)
    hi, mid, low = split3(s1 - s2 - s3)
    packed = dot(tri, jnp.concatenate([hi, mid, low], 1), 0, 0)
    grad_rate = packed[:, :STATE] + packed[:, STATE : 2 * STATE] + packed[:, 2 * STATE :]
    grad_rate = grad_rate + (jnp.sum(s3, axis=0, keepdims=True) + thin[1:2, :])
    denominator = 1.0 + e
    slope_x = jnp.where(x >= 0, 1.0, e) / denominator
    ratio = jnp.where(x < -20.0, 1.0, slope_x / jnp.maximum(dt, 1e-12))
    grad_raw = (s2 + s3) * ratio - decay * grad_rate * slope_x
    small_ref[6:7, :STATE] += jnp.sum(grad_raw, axis=0, keepdims=True)
    small_ref[7:8, :STATE] += jnp.sum(grad_rate * rate, axis=0, keepdims=True)
    small_ref[8:9, :STATE] += thin[0:1, :]
    small_ref[5:6, :cw] += jnp.sum(gu * rg, axis=0, keepdims=True)

    grun = jnp.concatenate([grad_x, grad_b, grad_c], 1) * slope
    next_ref[pl.ds(SPAN, 8), :] = next_ref[pl.ds(0, 8), :]
    next_ref[pl.ds(0, SPAN), :] = grun
    small_ref[taps : taps + 1, :] += jnp.sum(grun, axis=0, keepdims=True)
    gbefore = jnp.zeros_like(grun)
    for k in range(taps):
        small_ref[k : k + 1, :] += jnp.sum(
            grun * pad_ref[pl.ds(8 - taps + 1 + k, SPAN), :], axis=0, keepdims=True
        )
        gbefore = gbefore + vec_ref[k : k + 1, :] * next_ref[pl.ds(taps - 1 - k, SPAN), :]
    gpgx = jnp.concatenate([ggate, gbefore[:, :cw]], 1).astype(BF16)
    gps = jnp.concatenate([gbefore[:, cw:], plane.all_lanes(grad_raw, heads)], 1).astype(BF16)
    gpgx_ref[...] = gpgx
    gps_ref[...] = gps
    part_ref[rows_now, :] = (dot(gpgx, wgx_ref[...], 1, 1) + dot(gps, ws_ref[...], 1, 1)).astype(BF16)

    for m in range(layers):
        for c in range(blocks):
            @pl.when(t == m * blocks + blocks - 1 - c)
            def _(m=m, c=c):
                collects[m].block_done(c)

    for stage in range(plane.stages):
        @pl.when(t == min(stage, blocks - 1))
        def _(stage=stage):
            gathers[1].hop(stage)

    @pl.when(t == blocks)
    def _():
        for c in range(blocks):
            collects[0].block_add(c)
        collects[0].begin(0)

    for stage in range(plane.stages):
        @pl.when(t == blocks + 1 + stage)
        def _(stage=stage):
            collects[0].add(stage, raw_ref, 0)
            if stage + 1 < plane.stages:
                collects[0].begin(stage + 1)

    for c in range(1, blocks):
        @pl.when(t == blocks + blocks - c)
        def _(c=c):
            collects[1].block_add(c)

    @pl.when(t == steps - 1)
    def _():
        collects[1].block_add(0)
        collects[1].begin(0)
        share.drain()
        for m in range(layers):
            gathers[m].drain()
            saving(m).wait()
        collects[0].drain()
        for stage in range(plane.stages):
            collects[1].add(stage, raw_ref, piece)
            if stage + 1 < plane.stages:
                collects[1].begin(stage + 1)
        collects[1].drain()


def tables(heads):
    cw = heads * HEAD
    tri = np.tril(np.ones((SPAN, SPAN), np.float32))
    one = (np.arange(cw)[None, :] // HEAD == np.arange(STATE)[:, None]).astype(np.float32)
    spread3 = np.concatenate([one] * 3, 0)
    gather3 = np.concatenate([one.T] * 3, 0)
    return jnp.asarray(tri, BF16), jnp.asarray(spread3, BF16), jnp.asarray(gather3, BF16)


def whole(a):
    return pl.BlockSpec(memory_space=pltpu.VMEM)


def plane_scratch(layers, blocks, width):
    size, piece = layers * blocks, SPAN // layers
    dma = pltpu.SemaphoreType.DMA
    return [
        pltpu.VMEM((layers, blocks // 2, SPAN, width), BF16),
        pltpu.VMEM((layers, 2, size // 2, piece // 2, width), BF16),
        dma((layers,)),
        dma((layers, 2, size)),
        dma((layers, 2, size)),
        dma((layers, blocks)),
        dma((layers, blocks)),
        dma((layers, 2, size // 2)),
        dma((layers, 2, size // 2)),
    ]


def layer_forward(own, wgx, ws, wo, vec, taps, number, *following):
    layers, blocks, depth = lax.axis_size("section"), lax.axis_size("seq"), lax.axis_size("fsdp")
    width = own.shape[1]
    cw = wo.shape[0]
    heads = cw // HEAD
    steps = layers * blocks
    tokens = steps * SPAN
    tri, spread3, _ = tables(heads)
    rows = lambda w: pl.BlockSpec((SPAN, w), lambda t: (t, 0))
    chans = cw + 2 * STATE
    vmem = pl.BlockSpec(memory_space=pltpu.VMEM)
    dma = pltpu.SemaphoreType.DMA
    return pl.pallas_call(
        functools.partial(forward_kernel, layers, heads, blocks, taps, bool(following)),
        grid=(steps,),
        in_specs=[vmem] * 7 + [pl.BlockSpec(memory_space=pl.ANY)] * len(following),
        out_specs=[
            vmem,
            vmem,
            rows(2 * cw),
            rows(3 * STATE),
            rows(cw),
            pl.BlockSpec((1, STATE, cw), lambda t: (t, 0, 0)),
            pl.BlockSpec(memory_space=pl.ANY),
        ]
        + [pl.BlockSpec(memory_space=pl.ANY)] * len(following),
        out_shape=[
            jax.ShapeDtypeStruct(own.shape, F32),
            jax.ShapeDtypeStruct((layers, 8, SPAN), F32),
            jax.ShapeDtypeStruct((tokens, 2 * cw), BF16),
            jax.ShapeDtypeStruct((tokens, 3 * STATE), BF16),
            jax.ShapeDtypeStruct((tokens, cw), BF16),
            jax.ShapeDtypeStruct((steps, STATE, cw), BF16),
            jax.ShapeDtypeStruct((tokens, width), BF16),
        ]
        + ([jax.ShapeDtypeStruct(wgx.shape, BF16), jax.ShapeDtypeStruct((depth,) + following[1].shape, BF16)] if following else []),
        scratch_shapes=[
            pltpu.VMEM((tokens, width), BF16),
            pltpu.VMEM((tokens, width), BF16),
            pltpu.VMEM((SPAN + 8, chans), F32),
            pltpu.VMEM((STATE, cw), F32),
            pltpu.VMEM((SPAN, cw), F32),
            pltpu.VMEM((layers, 8, SPAN), F32),
            pltpu.VMEM((layers, steps, 8, SPAN), F32),
        ]
        + plane_scratch(layers, blocks, width)
        + [dma((layers, steps)), dma((layers, steps))]
        + ([dma((2,))] + [dma((depth,))] * 4 if following else []),
        compiler_params=pltpu.CompilerParams(
            vmem_limit_bytes=60 << 20, collective_id=number, has_side_effects=True
        ),
        cost_estimate=pl.CostEstimate(
            flops=2 * tokens * width * (3 * cw + 3 * STATE) + 2 * tokens * cw * 700,
            bytes_accessed=4 * tokens * width + 2 * width * (3 * cw + 3 * STATE) + 8 * tokens * cw,
            transcendentals=tokens * SPAN * heads,
        ),
        name="layer_forward",
    )(own, wgx, ws, wo, vec, tri, spread3, *following)


def layer_backward(own, pull, r_rows, pgx, ps, res, ent, wgx, ws, wo, vec, taps, number):
    layers, blocks = lax.axis_size("section"), lax.axis_size("seq")
    width = own.shape[1]
    cw = wo.shape[0]
    heads = cw // HEAD
    steps = layers * blocks
    tokens = steps * SPAN
    tri, spread3, gather3 = tables(heads)
    chans = cw + 2 * STATE
    vmem = pl.BlockSpec(memory_space=pltpu.VMEM)
    dma = pltpu.SemaphoreType.DMA

    def at(t):
        return t - lax.rem(t, blocks) + (blocks - 1 - lax.rem(t, blocks))

    rows = lambda w: pl.BlockSpec((SPAN, w), lambda t: (at(t), 0))
    edge = lambda w: pl.BlockSpec((16, w), lambda t: (jnp.maximum(at(t) * (SPAN // 16) - 1, 0), 0))
    return pl.pallas_call(
        functools.partial(backward_kernel, layers, heads, blocks, taps),
        grid=(steps,),
        in_specs=[
            vmem,
            vmem,
            vmem,
            rows(2 * cw),
            rows(3 * STATE),
            edge(2 * cw),
            edge(3 * STATE),
            rows(cw),
            pl.BlockSpec((1, STATE, cw), lambda t: (at(t), 0, 0)),
        ]
        + [vmem] * 7,
        out_specs=[
            vmem,
            rows(2 * cw),
            rows(3 * STATE),
            rows(cw),
            vmem,
            pl.BlockSpec(memory_space=pl.ANY),
        ],
        out_shape=[
            jax.ShapeDtypeStruct(own.shape, F32),
            jax.ShapeDtypeStruct((tokens, 2 * cw), BF16),
            jax.ShapeDtypeStruct((tokens, 3 * STATE), BF16),
            jax.ShapeDtypeStruct((tokens, cw), BF16),
            jax.ShapeDtypeStruct((16, chans), F32),
            jax.ShapeDtypeStruct((tokens, width), BF16),
        ],
        scratch_shapes=[
            pltpu.VMEM((tokens, width), BF16),
            pltpu.VMEM((tokens, width), BF16),
            pltpu.VMEM((SPAN + 8, chans), F32),
            pltpu.VMEM((SPAN + 8, chans), F32),
            pltpu.VMEM((STATE, cw), F32),
            pltpu.VMEM((SPAN, cw), F32),
            pltpu.VMEM((SPAN, cw), F32),
            pltpu.VMEM((layers, blocks, 8, SPAN), F32),
        ]
        + plane_scratch(layers, blocks, width)
        + [dma((steps,)), dma((steps,))],
        compiler_params=pltpu.CompilerParams(
            vmem_limit_bytes=60 << 20, collective_id=number, has_side_effects=True
        ),
        cost_estimate=pl.CostEstimate(
            flops=2 * tokens * width * (3 * cw + 3 * STATE) + 2 * tokens * cw * 2000,
            bytes_accessed=4 * tokens * width + 2 * width * (3 * cw + 3 * STATE) + 8 * tokens * cw,
            transcendentals=tokens * SPAN * heads,
        ),
        name="layer_backward",
    )(own, pull, r_rows, pgx, ps, pgx, ps, res, ent, wgx, ws, wo, vec, tri, spread3, gather3)


def reduce_kernel(
    layers, ranks, parts, pr,
    full_ref, gp_ref, gps_ref, no_ref, gb_ref, out_ref, oout_ref, tout_ref,
    sum_ref, osum_ref, in_ref, oin_ref, thin_ref, thin_f, tz_ref, tin_ref, core_in, stage_in,
    send_sem, recv_sem, osend_sem, orecv_sem, core_send, core_recv, rs_send, rs_recv, tz_send, tz_recv,
):
    place, count = lax.axis_index("fsdp"), lax.axis_size("fsdp")
    plane = Plane(layers, ranks)
    rows = out_ref.shape[0]
    piece = rows // parts
    orows = oout_ref.shape[0]
    chain_barrier(plane, place, count)

    thin_rows = gps_ref.shape[1]
    thin_ref[pl.ds(0, thin_rows), :] = dot(gps_ref[...], full_ref[...], 0, 0).astype(BF16)
    if thin_ref.shape[0] > thin_rows:
        rest = thin_ref.shape[0] - thin_rows
        thin_ref[pl.ds(thin_rows, rest), :] = jnp.zeros((rest, thin_ref.shape[1]), BF16)
    thin = Collect(plane, thin_ref, 0, layers * pr, core_in, stage_in, core_send, core_recv, rs_send, rs_recv)
    for c in range(ranks):
        thin.block_done(c)
    lines = Row(
        place, count, lambda d: tz_ref.at[lax.rem(place + d, count)], lambda d: tin_ref.at[place], tz_send, tz_recv
    )

    def pair(j, k, side):
        to = {"fsdp": place + 1 if side == 0 else place - 1}
        if k == parts:
            return pltpu.make_async_remote_copy(
                src_ref=osum_ref.at[j], dst_ref=oin_ref.at[side, j], send_sem=osend_sem.at[j],
                recv_sem=orecv_sem.at[side, j], device_id=to, device_id_type=MESH,
            )
        return pltpu.make_async_remote_copy(
            src_ref=sum_ref.at[j, k], dst_ref=in_ref.at[side, j, k], send_sem=send_sem.at[j, k],
            recv_sem=recv_sem.at[side, j, k], device_id=to, device_id_type=MESH,
        )

    def work(j, k):
        if k == parts:
            osum_ref[j] = dot(no_ref[:, j * orows : (j + 1) * orows], gb_ref[...], 0, 0).astype(BF16)
        else:
            cut = slice(j * rows + k * piece, j * rows + (k + 1) * piece)
            sum_ref[j, k] = dot(full_ref[:, cut], gp_ref[...], 0, 0).astype(BF16)

    def absorb(j, k, side):
        pair(j, k, side).wait_recv()
        if k == parts:
            osum_ref[j] = (osum_ref[j].astype(F32) + oin_ref[side, j].astype(F32)).astype(BF16)
        else:
            sum_ref[j, k] = (sum_ref[j, k].astype(F32) + in_ref[side, j, k].astype(F32)).astype(BF16)

    behind = (place > 0, place < count - 1)

    def shift(j, k):
        for side in (0, 1):
            beyond = (place < j) if side == 0 else (place > j)

            @pl.when(beyond & behind[side])
            def _(side=side):
                absorb(j, k, side)

            @pl.when(beyond)
            def _(side=side):
                pair(j, k, side).start()

    order = []
    low, high = 0, count - 1
    while low <= high:
        order += [high] if low == high else [high, low]
        low, high = low + 1, high - 1
    items = [(j, k) for p in range(0, len(order), 2) for k in range(parts + 1) for j in order[p : p + 2]]
    todo = [lambda: ([thin.block_add(c) for c in range(ranks)], thin.begin(0))]
    for stage in range(plane.stages):
        def advance(stage=stage):
            thin.add(stage, thin_f, 0)
            if stage + 1 < plane.stages:
                thin.begin(stage + 1)
        todo.append(advance)

    def across():
        wide = tz_ref.shape[2]
        for j in range(count):
            tz_ref[j] = thin_f[:, j * wide : (j + 1) * wide].astype(BF16)
        lines.begin()

    todo.append(across)
    for number, (j, k) in enumerate(items):
        work(j, k)
        shift(j, k)
        if number % 2 == 1 and todo:
            todo.pop(0)()
    while todo:
        todo.pop(0)()
    for k in range(parts + 1):
        for j in range(count):
            for side in (0, 1):
                @pl.when((place == j) & behind[side])
                def _(side=side, k=k, j=j):
                    absorb(j, k, side)

            @pl.when(place == j)
            def _(k=k, j=j):
                if k == parts:
                    oout_ref[...] = osum_ref[j]
                else:
                    out_ref[pl.ds(k * piece, piece), :] = sum_ref[j, k]

    lines.finish()
    total = tz_ref[place].astype(F32)
    for d in range(1, count):
        total = total + tin_ref[lax.rem(place + d, count)].astype(F32)
    tout_ref[...] = total.astype(BF16)
    lines.drain()
    thin.drain()
    for k in range(parts + 1):
        for j in range(count):
            @pl.when(place != j)
            def _(k=k, j=j):
                pair(j, k, 0).wait_send()


def reduce_gradients(full, gp, gps, no, gb, number):
    layers, ranks, count = lax.axis_size("section"), lax.axis_size("seq"), lax.axis_size("fsdp")
    size = layers * ranks
    tokens, width = full.shape
    rows, cols, orows = width // count, gp.shape[1], no.shape[1] // count
    parts = 3 if rows % 384 == 0 else 1
    pr = -(-gps.shape[1] // (32 * size)) * 32
    dma = pltpu.SemaphoreType.DMA
    return pl.pallas_call(
        functools.partial(reduce_kernel, layers, ranks, parts, pr),
        in_specs=[whole(a) for a in (full, gp, gps, no, gb)],
        out_specs=[pl.BlockSpec(memory_space=pltpu.VMEM)] * 3,
        out_shape=[
            jax.ShapeDtypeStruct((rows, cols), BF16),
            jax.ShapeDtypeStruct((orows, width), BF16),
            jax.ShapeDtypeStruct((pr, width // count), BF16),
        ],
        scratch_shapes=[
            pltpu.VMEM((count, parts, rows // parts, cols), BF16),
            pltpu.VMEM((count, orows, width), BF16),
            pltpu.VMEM((2, count, parts, rows // parts, cols), BF16),
            pltpu.VMEM((2, count, orows, width), BF16),
            pltpu.VMEM((size * pr, width), BF16),
            pltpu.VMEM((pr, width), F32),
            pltpu.VMEM((count, pr, width // count), BF16),
            pltpu.VMEM((count, pr, width // count), BF16),
            pltpu.VMEM((ranks // 2, layers * pr, width), BF16),
            pltpu.VMEM((2, size // 2, pr // 2, width), BF16),
            dma((count, parts)),
            dma((2, count, parts)),
            dma((count,)),
            dma((2, count)),
            dma((ranks,)),
            dma((ranks,)),
            dma((2, size // 2)),
            dma((2, size // 2)),
            dma((count,)),
            dma((count,)),
        ],
        compiler_params=pltpu.CompilerParams(
            collective_id=number, has_side_effects=True, vmem_limit_bytes=60 << 20
        ),
        cost_estimate=pl.CostEstimate(
            flops=2 * tokens * (width * cols + orows * count * width),
            bytes_accessed=2 * tokens * (2 * width + cols + orows), transcendentals=0,
        ),
        name="reduce_gradients",
    )(full, gp, gps, no, gb)


class Publish:
    def __init__(self, plane, cells, view, other, condition, send, recv):
        self.plane, self.cells, self.view, self.other, self.condition = plane, cells, view, other, condition
        self.send, self.recv = send, recv
        self.outer = [dim for dim in range(2, plane.stages + 1)]

    def number(self, mask):
        sec, seq = self.plane.owner(mask)
        return sec * self.plane.ranks + seq

    def copy(self, mask, dim, cell):
        dst = self.view(self.number(mask), cell)
        src = self.other(cell) if dim == 1 else dst
        key = mask ^ (1 << dim)
        return pltpu.make_async_remote_copy(
            src_ref=src, dst_ref=dst, send_sem=self.send.at[key, cell], recv_sem=self.recv.at[key, cell],
            device_id=self.plane.partner(dim), device_id_type=MESH,
        )

    def each(self, mask, act):
        @pl.when(self.condition(self.number(mask)))
        def _():
            for cell in range(self.cells):
                act(cell)

    def stage(self, mask):
        return max([i for i, dim in enumerate(self.outer) if mask >> dim & 1], default=-1)

    def forward(self, mask):
        later = self.outer[self.stage(mask) + 1 :] + [0]

        def act(cell):
            for dim in later:
                self.copy(mask, dim, cell).start()

        self.each(mask, act)

    def begin(self):
        self.each(0, lambda cell: self.copy(0, 1, cell).start())
        self.forward(0)

    def arrived(self, mask):
        def act(cell):
            view = self.view(self.number(mask), cell)
            pltpu.make_async_remote_copy(
                src_ref=view, dst_ref=view, send_sem=self.send.at[mask, cell], recv_sem=self.recv.at[mask, cell],
                device_id=self.plane.partner(0), device_id_type=MESH,
            ).wait_recv()

        self.each(mask, act)

    def step(self, stage):
        for mask in self.plane.masks[1:]:
            if self.stage(mask) == stage:
                self.arrived(mask)
                self.forward(mask)

    def finish(self):
        for mask in self.plane.masks:
            self.arrived(mask + 1)

    def drain(self):
        for mask in self.plane.masks:
            dims = self.outer[self.stage(mask) + 1 :] + [0] + ([1] if mask == 0 else [])

            def act(cell, mask=mask, dims=dims):
                for dim in dims:
                    self.copy(mask, dim, cell).wait_send()

            self.each(mask, act)


def publish_kernel(
    layers, ranks, parts, wide, pr,
    gx0, gx1, o0, o1, thin_ref, sm_ref, gn_ref, swap_ref,
    gall, oall, tall, sm_all, gn_out, got_ref,
    tmp_o, sm_in, gn_in, gn_plane,
    own_sem, swap_send, swap_recv, z_send, z_recv, g_send, g_recv, p_send, p_recv, q_send, q_recv, t_send, t_recv,
    s_send, s_recv, n_send, n_recv, zs_send, zs_recv, zn_send, zn_recv,
):
    place, count = lax.axis_index("fsdp"), lax.axis_size("fsdp")
    plane = Plane(layers, ranks)
    low = plane.sec == 0
    here = plane.sec * ranks + plane.seq
    rows, cols = gx0.shape
    cw = cols // 2
    piece = rows // parts
    per = plane.size // count
    chain_barrier(plane, place, count)

    sm_lines = Row(place, count, lambda d: sm_ref, lambda d: sm_in.at[d], zs_send, zs_recv)
    gn_lines = Row(place, count, lambda d: gn_ref, lambda d: gn_in.at[d], zn_send, zn_recv)
    sm_lines.begin()
    gn_lines.begin()

    def gx_window(d, cell):
        k, w = cell // wide, cell % wide
        span = pl.ds(k * piece, piece)
        if wide == 1:
            return gall.at[d, span, :]
        start = pl.multiple_of(d * cw + w * cw * plane.size, STATE)
        return gall.at[span, pl.ds(start, cw)]

    def gx_source(ref, cell):
        k, w = cell // wide, cell % wide
        span = pl.ds(k * piece, piece)
        return ref.at[span, :] if wide == 1 else ref.at[span, pl.ds(w * cw, cw)]

    home = here // per
    at_home = home == place

    def gather_o(layer, ref):
        def copy(local):
            dst = oall.at[lax.rem(here, per) * count + place] if local else tmp_o.at[place]
            return dst

        def remote(dst, number):
            return pltpu.make_async_remote_copy(
                src_ref=ref, dst_ref=dst, send_sem=z_send.at[layer], recv_sem=z_recv.at[layer, number],
                device_id={"fsdp": home}, device_id_type=MESH,
            )

        def begin():
            for mine in (True, False):
                which = (plane.sec == layer) if mine else (plane.sec != layer)

                @pl.when(which & at_home)
                def _(mine=mine):
                    pltpu.make_async_copy(ref, copy(mine), own_sem.at[1 + layer]).start()

                @pl.when(which & ~at_home)
                def _(mine=mine):
                    remote(copy(mine), place).start()

        def finish():
            @pl.when(at_home)
            def _():
                pltpu.make_async_copy(ref, tmp_o.at[place], own_sem.at[1 + layer]).wait()
                for d in range(1, count):
                    remote(tmp_o.at[place], lax.rem(place + d, count)).wait_recv()

            @pl.when(~at_home)
            def _():
                remote(tmp_o.at[place], place).wait_send()

        return begin, finish

    gathers = [gather_o(0, o0), gather_o(1, o1)]
    for begin, _ in gathers:
        begin()

    gpub = [
        Publish(plane, parts * wide, gx_window, lambda cell, ref=ref: gx_source(ref, cell), lambda d: d >= 0, g_send, g_recv)
        for ref in (gx1, gx0)
    ]
    opub = Publish(
        plane, count, lambda d, cell: oall.at[lax.rem(d, per) * count + cell], lambda cell: tmp_o.at[cell],
        lambda d: d // per == place, p_send, p_recv,
    )
    cells = parts * wide

    def own(ref):
        return [pltpu.make_async_copy(gx_source(ref, c), gx_window(here, c), own_sem.at[4 + c]) for c in range(cells)]

    for number, ref in enumerate((gx0, gx1)):
        @pl.when(plane.sec == number)
        def _(ref=ref):
            for c in own(ref):
                c.start()

    for number in range(layers):
        @pl.when(plane.sec == number)
        def _(number=number):
            gpub[number].each(0, lambda cell: gpub[number].copy(0, 1, cell).start())

    for c in own(gx0):
        c.wait()
    gpub[0].forward(0)

    spread = Spread(
        plane, tall, lambda sec, seq: (seq * layers + sec) * pr, pr, t_send, t_recv
    )
    tall[pl.ds(pl.multiple_of((plane.seq * layers + plane.sec) * pr, 16), pr), :] = thin_ref[...]
    spread.begin()
    sm_lines.finish()
    gn_lines.finish()
    mine, gain = sm_ref[...], gn_ref[...]
    for d in range(1, count):
        mine, gain = mine + sm_in[d], gain + gn_in[d]
    sm_all[here] = mine
    gn_plane[0] = gain
    shares = [
        Share(plane, sm_all.at[here], lambda mask: sm_all.at[here], s_send, s_recv),
        Share(plane, gn_plane.at[0], lambda mask: gn_plane.at[mask], n_send, n_recv),
    ]
    for share in shares:
        share.begin()
    spread.hop(0)
    for _, finish in gathers:
        finish()
    opub.begin()
    swap = pltpu.make_async_remote_copy(
        src_ref=swap_ref, dst_ref=got_ref, send_sem=swap_send.at[0], recv_sem=swap_recv.at[0],
        device_id=plane.partner(1), device_id_type=MESH,
    )
    swap.start()
    gpub[0].step(-1)
    for stage in range(1, plane.stages):
        spread.hop(stage)
    for stage in range(len(opub.outer)):
        gpub[0].step(stage)
    opub.step(-1)
    for stage in range(len(opub.outer)):
        opub.step(stage)
    gpub[0].finish()
    opub.finish()
    spread.finish()
    for share in shares:
        share.finish()
    total = gn_plane[0]
    for mask in range(1, plane.size):
        total = total + gn_plane[mask]
    gn_out[...] = total
    swap.wait()
    for each in [gpub[0], opub, spread, sm_lines, gn_lines] + shares:
        each.drain()


def publish(gx0, gx1, o0, o1, thin, sm, gn, swap, number):
    layers, ranks, count = lax.axis_size("section"), lax.axis_size("seq"), lax.axis_size("fsdp")
    size = layers * ranks
    rows, cols = gx0.shape
    cw = cols // 2
    wide = 2 if cw % STATE == 0 else 1
    parts = 2
    cells = parts * wide
    per = size // count
    orows, width = o0.shape
    pr, tcols = thin.shape
    dma = pltpu.SemaphoreType.DMA
    anywhere = pl.BlockSpec(memory_space=pl.ANY)
    vmem = pl.BlockSpec(memory_space=pltpu.VMEM)
    gall = (rows, size * cols) if wide == 2 else (size, rows, cols)
    return pl.pallas_call(
        functools.partial(publish_kernel, layers, ranks, parts, wide, pr),
        in_specs=[anywhere] * 4 + [vmem] * 3 + [anywhere],
        out_specs=[anywhere, anywhere, vmem, vmem, vmem, anywhere],
        out_shape=[
            jax.ShapeDtypeStruct(gall, BF16),
            jax.ShapeDtypeStruct((per * count, orows, width), BF16),
            jax.ShapeDtypeStruct((size * pr, tcols), BF16),
            jax.ShapeDtypeStruct((size,) + sm.shape, F32),
            jax.ShapeDtypeStruct(gn.shape, F32),
            jax.ShapeDtypeStruct(swap.shape, BF16),
        ],
        scratch_shapes=[
            pltpu.VMEM((count, orows, width), BF16),
            pltpu.VMEM((count,) + sm.shape, F32),
            pltpu.VMEM((count,) + gn.shape, F32),
            pltpu.VMEM((size,) + gn.shape, F32),
            dma((4 + cells,)),
            dma((1,)),
            dma((1,)),
            dma((layers,)),
            dma((layers, count)),
            dma((size, cells)),
            dma((size, cells)),
            dma((size, count)),
            dma((size, count)),
            dma((1,)),
            dma((1,)),
            dma((2, size)),
            dma((2, size)),
            dma((size,)),
            dma((size,)),
            dma((size,)),
            dma((size,)),
            dma((count,)),
            dma((count,)),
            dma((count,)),
            dma((count,)),
        ],
        compiler_params=pltpu.CompilerParams(
            collective_id=number, has_side_effects=True, vmem_limit_bytes=40 << 20
        ),
        name="publish",
    )(gx0, gx1, o0, o1, thin, sm, gn, swap)


def start_kernel(
    layers, ranks, parts, oparts,
    mine, theirs, mine_o, theirs_o, ends_ref, strip_ref, packed_ref,
    full, all_o, next_gx, next_o, got_ref, thin_ref, params_ref,
    own_sem, y_send, y_recv, x_send, x_recv, send, recv, o_send, o_recv, cut_send, cut_recv,
    st_send, st_recv, ag_send, ag_recv, pa_send, pa_recv,
):
    place, count = lax.axis_index("fsdp"), lax.axis_size("fsdp")
    plane = Plane(layers, ranks)
    low = plane.sec == 0
    rows = mine.shape[0]
    piece = rows // parts
    opiece = mine_o.shape[1] // oparts
    orows = mine_o.shape[0] * mine_o.shape[1]
    out_rows = layers * ranks * orows // count
    here = plane.sec * ranks + plane.seq
    there = (layers - 1 - plane.sec) * ranks + plane.seq
    source = (here * orows) // out_rows == place
    source_there = (there * orows) // out_rows == place
    across = plane.partner(1)

    def block(j, k):
        return full.at[pl.ds(pl.multiple_of(j * rows + k * piece, 16), piece), :]

    def oblock(j, k):
        return all_o.at[j, pl.ds(k * opiece, opiece), :]

    def y_copy(k, dst):
        return pltpu.make_async_remote_copy(
            src_ref=theirs.at[pl.ds(k * piece, piece), :], dst_ref=dst, send_sem=y_send.at[k], recv_sem=y_recv.at[k],
            device_id=across, device_id_type=MESH,
        )

    def cut(d, same, first):
        spot = lax.rem(place + d, count)
        return pltpu.make_async_remote_copy(
            src_ref=(mine_o if same else theirs_o).at[spot], dst_ref=all_o.at[spot] if first else next_o,
            send_sem=cut_send.at[0 if same else 1, d], recv_sem=cut_recv.at[0 if first else 1],
            device_id={"section": plane.sec if same else layers - 1 - plane.sec, "fsdp": spot}, device_id_type=MESH,
        )

    def own_cut(first):
        return pltpu.make_async_copy(mine_o.at[place], all_o.at[place] if first else next_o, own_sem.at[3])

    def begin_cuts(same, first, condition):
        @pl.when(condition)
        def _():
            if same:
                own_cut(first).start()
            for d in range(1 if same else 0, count):
                cut(d, same, first).start()

    half = ends_ref.shape[1] // layers
    x_copy = pltpu.make_async_remote_copy(
        src_ref=ends_ref.at[:, pl.ds(pl.multiple_of((layers - 1 - plane.sec) * half, 16), half), :], dst_ref=got_ref,
        send_sem=x_send.at[0], recv_sem=x_recv.at[0], device_id=across, device_id_type=MESH,
    )
    strips = Row(
        place, count, lambda d: strip_ref, lambda d: thin_ref.at[plane.sec, plane.seq, place], st_send, st_recv
    )
    hold = count // 2
    spread = Spread(plane, thin_ref, None, 0, ag_send, ag_recv)
    spread.view = lambda h, mask: thin_ref.at[plane.owner(mask)[0], plane.owner(mask)[1], pl.ds(h * hold, hold)]

    def p_copy(d, same):
        sec = plane.sec if same else layers - 1 - plane.sec
        number = d if same else count + d
        return pltpu.make_async_remote_copy(
            src_ref=packed_ref, dst_ref=params_ref.at[plane.sec, place], send_sem=pa_send.at[number],
            recv_sem=pa_recv.at[number], device_id={"section": sec, "fsdp": lax.rem(place + d, count)},
            device_id_type=MESH,
        )

    pairs = [(d, same) for d in range(count) for same in (True, False) if d or not same]
    own_strip = pltpu.make_async_copy(strip_ref, thin_ref.at[plane.sec, plane.seq, place], own_sem.at[0])
    own_packed = pltpu.make_async_copy(packed_ref, params_ref.at[plane.sec, place], own_sem.at[1])
    own_block = pltpu.make_async_copy(mine, full.at[pl.ds(pl.multiple_of(place * rows, 16), rows), :], own_sem.at[2])
    own_next = pltpu.make_async_copy(mine, next_gx, own_sem.at[2])
    line = Line(place, count, block, parts, send, recv)
    oline = Line(place, count, oblock, oparts, o_send, o_recv)

    chain_barrier(plane, place, count)
    own_strip.start()
    own_packed.start()

    @pl.when(low)
    def _():
        own_block.start()
        for k in range(parts):
            y_copy(k, block(place, k)).start()

    strips.begin()
    for d, same in pairs:
        p_copy(d, same).start()
    begin_cuts(True, True, low & source)

    @pl.when(low)
    def _():
        own_block.wait()

    for k in range(parts):
        @pl.when(~low)
        def _(k=k):
            y_copy(k, block(place, k)).wait_recv()

        line.begin(k)

    @pl.when(low)
    def _():
        for k in range(parts):
            y_copy(k, block(place, k)).wait_send()

    begin_cuts(False, True, low & source_there)
    x_copy.start()
    for k in range(parts):
        line.forward(1, k)

    @pl.when(~low)
    def _():
        own_next.start()
        for k in range(parts):
            y_copy(k, next_gx.at[pl.ds(k * piece, piece), :]).start()

    own_strip.wait()
    strips.finish()
    spread.begin()

    @pl.when(low & source)
    def _():
        own_cut(True).wait()

    @pl.when(~(low & source))
    def _():
        cut(0, True, True).wait_recv()

    for k in range(oparts):
        oline.begin(k)
    spread.hop(0)
    begin_cuts(True, False, ~low & source)
    begin_cuts(False, False, ~low & source_there)
    for d in range(2, count):
        for k in range(parts):
            line.forward(d, k)
        for k in range(oparts):
            oline.forward(d - 1, k)
        if d == 2:
            for stage in range(1, plane.stages):
                spread.hop(stage)
    for k in range(oparts):
        oline.forward(count - 1, k)
    spread.finish()

    own_packed.wait()
    x_copy.wait()

    @pl.when(low)
    def _():
        for k in range(parts):
            y_copy(k, next_gx.at[pl.ds(k * piece, piece), :]).wait_recv()

    @pl.when(~low)
    def _():
        own_next.wait()
        for k in range(parts):
            y_copy(k, block(place, k)).wait_send()

    @pl.when(~low & source)
    def _():
        own_cut(False).wait()

    @pl.when(~(~low & source))
    def _():
        cut(0, True, False).wait_recv()

    @pl.when(source)
    def _():
        for d in range(1, count):
            cut(d, True, False).wait_send()

    @pl.when(source_there)
    def _():
        for d in range(count):
            cut(d, False, False).wait_send()

    for d, same in pairs:
        p_copy(d, same).wait()
    strips.drain()
    spread.drain()
    line.drain()
    oline.drain()


def start_up(mine, theirs, mine_o, theirs_o, ends, strip, packed, number):
    layers, ranks, count = lax.axis_size("section"), lax.axis_size("seq"), lax.axis_size("fsdp")
    parts = 4 if mine.shape[0] % 64 == 0 else 2
    mine_o = mine_o.reshape(count, -1, mine_o.shape[1])
    theirs_o = theirs_o.reshape(mine_o.shape)
    oparts = 2 if mine_o.shape[1] % 32 == 0 else 1
    anywhere = pl.BlockSpec(memory_space=pl.ANY)
    dma = pltpu.SemaphoreType.DMA
    size = layers * ranks
    half = ends.shape[1] // layers
    return pl.pallas_call(
        functools.partial(start_kernel, layers, ranks, parts, oparts),
        in_specs=[anywhere] * 7,
        out_specs=[anywhere] * 7,
        out_shape=[
            jax.ShapeDtypeStruct((count * mine.shape[0], mine.shape[1]), BF16),
            jax.ShapeDtypeStruct(mine_o.shape, BF16),
            jax.ShapeDtypeStruct(mine.shape, BF16),
            jax.ShapeDtypeStruct(mine_o.shape[1:], BF16),
            jax.ShapeDtypeStruct((ends.shape[0], half, ends.shape[2]), BF16),
            jax.ShapeDtypeStruct((layers, ranks, count) + strip.shape, BF16),
            jax.ShapeDtypeStruct((layers, count) + packed.shape, BF16),
        ],
        scratch_shapes=[
            dma((4,)),
            dma((parts,)),
            dma((parts,)),
            dma((1,)),
            dma((1,)),
            dma((2, count, parts)),
            dma((2, count, parts)),
            dma((2, count, oparts)),
            dma((2, count, oparts)),
            dma((2, count)),
            dma((2,)),
            dma((count,)),
            dma((count,)),
            dma((2, size)),
            dma((2, size)),
            dma((2 * count,)),
            dma((2 * count,)),
        ],
        compiler_params=pltpu.CompilerParams(collective_id=number, has_side_effects=True),
        name="start_up",
    )(mine, theirs, mine_o, theirs_o, ends, strip, packed)


def swapped(value, axis):
    count = lax.axis_size(axis)
    return lax.ppermute(value, axis, [(i, count - 1 - i) for i in range(count)])


PLANE = ("section", "seq")
EVERY = ("section", "seq", "fsdp")


def per_device(
    section_ends, norm_gain, in_weight, conv_weight, conv_bias, step_bias, log_decay, skip_gain, gate_gain, out_weight
):
    sec, seq, dep = lax.axis_index("section"), lax.axis_index("seq"), lax.axis_index("fsdp")
    layers, ranks, depth = lax.axis_size("section"), lax.axis_size("seq"), lax.axis_size("fsdp")
    group = layers * ranks
    here = sec * ranks + seq
    there = (layers - 1 - sec) * ranks + seq
    low_layer = sec == 0
    width = in_weight.shape[1] * depth
    inner = gate_gain.shape[1] * depth
    chans = conv_bias.shape[1] * depth
    heads_all = step_bias.shape[1] * depth
    taps = conv_weight.shape[1]
    cw = inner // group
    heads = cw // HEAD
    shared = 2 * STATE

    ends = section_ends[0, :, 0]
    piece = ends.shape[1] // layers

    def head_columns(v, begin, count):
        return lax.dynamic_slice_in_dim(v, begin, count, v.ndim - 1)

    def own_columns(rank):
        return jnp.concatenate(
            [head_columns(in_weight[0], rank * cw, cw), head_columns(in_weight[0], inner + rank * cw, cw)], 1
        )

    out_rows = out_weight.shape[1]

    def own_rows(rank):
        start = jnp.clip(rank * cw - dep * out_rows, 0, out_rows - cw)
        return lax.dynamic_slice_in_dim(out_weight[0], start, cw, 0)

    strip = in_weight.shape[1] // ranks
    thin = lax.dynamic_slice(in_weight[0], (seq * strip, inner + chans - shared), (strip, shared + heads_all))
    thin = jnp.pad(thin, ((0, 0), (0, STATE - heads_all)))
    flat = [norm_gain, conv_weight, conv_bias, step_bias, log_decay, skip_gain, gate_gain]
    sizes = [v.size for v in flat]
    packed = jnp.concatenate([v.reshape(-1) for v in flat])
    packed = jnp.pad(packed, (0, -packed.size % 2048)).reshape(-1, STATE)
    wgx, wo, next_gx, next_o, got, thin, packed = start_up(
        own_columns(here), own_columns(there), own_rows(here), own_rows(there), ends, thin, packed, 0
    )
    packed = packed.reshape(layers, depth, -1).astype(F32)
    thin = jnp.transpose(thin, (0, 2, 1, 3, 4)).reshape(layers, width, -1)
    hidden = jnp.where(low_layer, ends[:, :piece], got).astype(F32).reshape(layers * piece, width)
    cot = jnp.where(low_layer, got, ends[:, piece:]).astype(F32).reshape(layers * piece, width)

    def own_tokens(v):
        v = lax.dynamic_slice_in_dim(v, seq, 1, 1)[:, 0]
        return lax.dynamic_slice_in_dim(v, sec * piece, piece, 1).reshape(-1, 1)

    def member(layer, number):
        begin = sum(sizes[:number])
        return packed[layer, :, begin : begin + sizes[number]]

    def vectors(layer):
        kernel = jnp.transpose(member(layer, 1).reshape(depth, taps, -1), (1, 0, 2)).reshape(taps, chans)
        rows = jnp.concatenate([kernel, member(layer, 2).reshape(1, chans)], 0)
        rows = jnp.concatenate([head_columns(rows, here * cw, cw), rows[:, inner:]], 1)
        total = cw + shared

        def padded(v):
            return jnp.pad(v[None], ((0, 0), (0, total - v.shape[0])))

        gain = head_columns(member(layer, 6).reshape(-1), here * cw, cw)
        by_head = [head_columns(member(layer, n).reshape(-1), here * heads, heads) for n in (3, 4, 5)]
        return jnp.concatenate(
            [rows, jnp.zeros((5 - taps - 1, total), F32), padded(gain), padded(by_head[0]), padded(by_head[1]),
             padded(jnp.repeat(by_head[2], HEAD)), jnp.zeros((7, total), F32)], 0)

    gains = [member(layer, 0).reshape(1, -1) for layer in range(layers)]
    vecs = [vectors(layer) for layer in range(layers)]

    saved, weights = [], []
    for layer in range(layers):
        ws, wo = thin[layer], wo.reshape(cw, width)
        weights.append((wgx, ws, wo))
        rs = lax.rsqrt(jnp.mean(hidden * hidden, axis=-1, keepdims=True) + EPS)
        following = (next_gx, next_o) if layer + 1 < layers else ()
        raw, ss, pgx, ps, res, ent, full, *after = layer_forward(
            (hidden * rs * gains[layer]).astype(BF16), wgx, ws, wo, vecs[layer], taps, 2 * layers + layer, *following
        )
        if after:
            wgx, wo = after
        r_rows = lax.rsqrt(ss / inner + EPS)
        r = own_tokens(r_rows)
        saved.append((hidden, rs, full, pgx, ps, res, ent, raw, r, r_rows))
        hidden = hidden + r * raw
        if layer + 1 < layers:
            hidden = hidden.astype(BF16).astype(F32)
    output = hidden

    grad = cot
    big, small = [None] * layers, [None] * layers
    for layer in reversed(range(layers)):
        wgx, ws, wo = weights[layer]
        before, rs, full, pgx, ps, res, ent, raw, r, r_rows = saved[layer]
        low = grad.astype(BF16)
        pull = r * r * r * jnp.sum(low.astype(F32) * raw, axis=-1, keepdims=True) / inner
        pull = jnp.broadcast_to(pull.reshape(layers, 1, piece), (layers, 8, piece))
        gn, gpgx, gps, no, tiny, gb = layer_backward(
            low, pull, r_rows, pgx, ps, res, ent, wgx, ws, wo, vecs[layer], taps, 3 * layers + layer
        )
        big[layer] = reduce_gradients(full, gpgx, gps, no, gb, 4 * layers + layer)
        unit = before * rs
        g_gain = jnp.sum(gn * unit, axis=0)
        gn = gn * gains[layer]
        grad = grad + rs * (gn - unit * jnp.mean(gn * unit, axis=-1, keepdims=True))
        if layer > 0:
            grad = grad.astype(BF16).astype(F32)

        small[layer] = (tiny, g_gain)

    output = output.reshape(layers, piece, width)
    grad = grad.reshape(layers, piece, width)
    g_norm = jnp.pad(jnp.stack([s[1] for s in small]), ((0, 8 - layers), (0, 0)))
    gall, oall, tall, sm, g_norm, got = publish(
        big[0][0], big[1][0], big[0][1], big[1][1], jnp.concatenate([b[2] for b in big], 1),
        jnp.stack([s[0] for s in small]), g_norm, jnp.where(low_layer, output, grad).astype(BF16), 6 * layers
    )
    got = got.astype(F32)
    results = jnp.where(low_layer, jnp.concatenate([grad, got], 1), jnp.concatenate([got, output], 1))
    section_results = results[None, :, None]
    if gall.ndim == 3:
        rows = gall.shape[1]
        gall = jnp.transpose(gall.reshape(group, rows, 2, cw), (1, 2, 0, 3)).reshape(rows, 2 * inner)
    share_d = tall.shape[1] // layers
    thin = jnp.where(low_layer, tall[: shared + heads_all, :share_d], tall[: shared + heads_all, share_d:])
    grad_in = jnp.concatenate([gall.astype(F32), thin.astype(F32).T], 1)[None]
    grad_out = oall.reshape(out_rows, width).astype(F32)[None]

    sm = jnp.where(low_layer, sm[:, 0], sm[:, 1])
    conv = jnp.transpose(sm[:, : taps + 1, :cw], (1, 0, 2)).reshape(taps + 1, inner)
    conv = jnp.concatenate([conv, jnp.sum(sm[:, : taps + 1, cw:], 0)], 1)
    by_head = jnp.transpose(sm[:, 6:9, :heads], (1, 0, 2)).reshape(3, heads_all)
    g_norm = jnp.where(low_layer, g_norm[0], g_norm[1])

    def share(v):
        count = v.shape[-1] // depth
        return lax.dynamic_slice_in_dim(v, dep * count, count, v.ndim - 1)[None]

    return (
        section_results,
        share(g_norm),
        grad_in,
        share(conv[:taps]),
        share(conv[taps]),
        share(by_head[0]),
        share(by_head[1]),
        share(by_head[2]),
        share(sm[:, 5, :cw].reshape(-1)),
        grad_out,
    )


def solution(mesh):
    weight = P("section", "fsdp")
    matrix = P("section", "fsdp", None)
    ends = P("section", None, "fsdp", "seq", None)
    kernel = P("section", None, "fsdp")
    return jax.shard_map(
        per_device,
        mesh=mesh,
        in_specs=(ends, weight, matrix, kernel, weight, weight, weight, weight, weight, matrix),
        out_specs=(ends, weight, matrix, kernel, weight, weight, weight, weight, weight, matrix),
        check_vma=False,
    )
```

```python
import functools

import jax
import jax.numpy as jnp
import numpy as np
from jax import lax
from jax.experimental import pallas as pl
from jax.experimental.pallas import tpu as pltpu
from jax.sharding import PartitionSpec as P

SPAN = 256
HEAD = 64
STATE = 128
EPS = 1e-05
F32 = jnp.float32
BF16 = jnp.bfloat16


def dot(a, b, ca, cb):
    return lax.dot_general(a, b, (((ca,), (cb,)), ((), ())), preferred_element_type=F32)


def split3(v):
    hi = v.astype(BF16)
    rest = v - hi.astype(F32)
    mid = rest.astype(BF16)
    low = (rest - mid.astype(F32)).astype(BF16)
    return hi, mid, low


def sigmoid(v):
    return 1.0 / (1.0 + jnp.exp(-v))


def running_conv(pad_ref, vec_ref, taps):
    run = vec_ref[taps : taps + 1, :] + vec_ref[0:1, :] * pad_ref[pl.ds(8 - taps + 1, SPAN), :]
    for k in range(1, taps):
        run = run + vec_ref[k : k + 1, :] * pad_ref[pl.ds(8 - taps + 1 + k, SPAN), :]
    return run


def step_sizes(dt_raw, vec_ref, tri):
    x = dt_raw + vec_ref[6:7, :STATE]
    e = jnp.exp(-jnp.abs(x))
    dt = jnp.maximum(x, 0.0) + jnp.log1p(e)
    decay = jnp.exp(vec_ref[7:8, :STATE])
    rate = -dt * decay
    hi, mid, low = split3(rate)
    packed = dot(tri, jnp.concatenate([hi, mid, low], 1), 1, 0)
    cum = packed[:, :STATE] + packed[:, STATE : 2 * STATE] + packed[:, 2 * STATE :]
    return x, e, dt, decay, rate, cum


def expand(v, spread3):
    return dot(jnp.concatenate(split3(v), 1), spread3, 1, 0)


def per_head(v, gather2):
    return dot(jnp.concatenate(split3(v)[:2], 1), gather2, 1, 0)


def fading(cum, cum_t, dt_t, h, inside):
    spread = cum[:, h : h + 1] - cum_t[h : h + 1, :]
    return jnp.exp(jnp.where(inside, spread, -1e30)) * dt_t[h : h + 1, :]


def inside_mask():
    rows = lax.broadcasted_iota(jnp.int32, (SPAN, SPAN), 0)
    cols = lax.broadcasted_iota(jnp.int32, (SPAN, SPAN), 1)
    return cols <= rows


MESH = pl.DeviceIdType.MESH


class Plane:
    def __init__(self, layers, ranks):
        self.layers, self.ranks = layers, ranks
        self.sec, self.seq = lax.axis_index("section"), lax.axis_index("seq")
        self.low = lax.rem(self.seq, 2)
        count = ranks.bit_length() - 1
        outer = list(range(1, count + 1))
        self.size = layers * ranks
        self.orders = (outer, outer[::-1])
        self.stages = len(outer)
        self.masks = [m for m in range(self.size) if m % 2 == 0]

    def weight(self, dim):
        return 1 if dim == 0 else 1 << (dim - 1)

    def flipped(self, dim):
        w = self.weight(dim)
        return self.seq + (1 - 2 * lax.rem(self.seq // w, 2)) * w

    def partner(self, dim):
        if dim == 1:
            return {"section": self.layers - 1 - self.sec}
        return {"seq": self.flipped(dim)}

    def owner(self, mask):
        seq = self.seq
        for dim in range(self.stages + 1):
            if dim != 1 and mask >> dim & 1:
                w = self.weight(dim)
                seq = seq + (1 - 2 * lax.rem(self.seq // w, 2)) * w
        sec = self.layers - 1 - self.sec if mask & 2 else self.sec
        return sec, seq

    def device(self, mask):
        sec, seq = self.owner(mask)
        return {"section": sec, "seq": seq}

    def arrival(self, half, mask):
        order = self.orders[half]
        return max(i for i, dim in enumerate(order) if mask >> dim & 1)

    def own_lanes(self, v, heads):
        return pltpu.roll(v, STATE - (self.sec * self.ranks + self.seq) * heads, 1)

    def all_lanes(self, v, heads):
        return pltpu.roll(v, (self.sec * self.ranks + self.seq) * heads, 1)

    def barrier(self):
        sem = pltpu.get_barrier_semaphore()
        for mask in range(1, self.size):
            pl.semaphore_signal(sem, inc=1, device_id=self.device(mask), device_id_type=MESH)
        pl.semaphore_wait(sem, self.size - 1)


class Spread:
    def __init__(self, plane, ref, start, rows, send, recv):
        self.plane, self.ref, self.start, self.rows, self.send, self.recv = plane, ref, start, rows, send, recv

    def view(self, half, mask):
        sec, seq = self.plane.owner(mask)
        count = self.rows // 2
        return self.ref.at[pl.ds(pl.multiple_of(self.start(sec, seq) + half * count, 16), count), :]

    def copy(self, half, mask, dim):
        view = self.view(half, mask)
        key = mask ^ (1 << dim)
        return pltpu.make_async_remote_copy(
            src_ref=view, dst_ref=view, send_sem=self.send.at[half, key], recv_sem=self.recv.at[half, key],
            device_id=self.plane.partner(dim), device_id_type=MESH,
        )

    def arrived(self, half, mask):
        view = self.view(half, mask)
        pltpu.make_async_remote_copy(
            src_ref=view, dst_ref=view, send_sem=self.send.at[half, mask], recv_sem=self.recv.at[half, mask],
            device_id=self.plane.partner(0), device_id_type=MESH,
        ).wait_recv()

    def begin(self):
        for stage in range(self.plane.stages):
            for half in (0, 1):
                self.copy(half, 0, self.plane.orders[half][stage]).start()
        for half in (0, 1):
            self.copy(half, 0, 0).start()

    def hop(self, stage):
        for half in (0, 1):
            order = self.plane.orders[half]
            for mask in self.plane.masks[1:]:
                if self.plane.arrival(half, mask) == stage:
                    self.arrived(half, mask)
                    for later in order[stage + 1 :]:
                        self.copy(half, mask, later).start()
                    self.copy(half, mask, 0).start()

    def finish(self):
        for half in (0, 1):
            for mask in self.plane.masks:
                self.arrived(half, mask + 1)

    def drain(self):
        for half in (0, 1):
            for mask in range(1, self.plane.size):
                self.copy(half, mask ^ 1, 0).wait_send()


class Collect:
    def __init__(self, plane, ref, base, span, core_in, stage_in, core_send, core_recv, send, recv):
        self.plane, self.ref, self.base, self.blocks, self.span = plane, ref, base, plane.ranks, span
        self.core_in, self.stage_in = core_in, stage_in
        self.core_send, self.core_recv, self.send, self.recv = core_send, core_recv, send, recv

    def core_copy(self, c):
        return pltpu.make_async_remote_copy(
            src_ref=self.ref.at[pl.ds(self.base + c * self.span, self.span), :], dst_ref=self.core_in.at[c // 2],
            send_sem=self.core_send.at[c], recv_sem=self.core_recv.at[c],
            device_id=self.plane.partner(0), device_id_type=MESH,
        )

    def block_done(self, c):
        @pl.when(self.plane.low != c % 2)
        def _():
            self.core_copy(c).start()

    def block_add(self, c):
        @pl.when(self.plane.low == c % 2)
        def _():
            self.core_copy(c).wait_recv()
            rows = pl.ds(self.base + c * self.span, self.span)
            self.ref[rows, :] = (self.ref[rows, :].astype(F32) + self.core_in[c // 2].astype(F32)).astype(BF16)

    def rows(self, half, mask):
        sec, seq = self.plane.owner(mask)
        count = self.span // self.plane.layers // 2
        begin = self.base + seq * self.span + sec * (2 * count) + half * count
        return pl.ds(pl.multiple_of(begin, 16), count)

    def copy(self, half, mask, dim):
        return pltpu.make_async_remote_copy(
            src_ref=self.ref.at[self.rows(half, mask), :], dst_ref=self.stage_in.at[half, mask // 2],
            send_sem=self.send.at[half, mask // 2], recv_sem=self.recv.at[half, mask // 2],
            device_id=self.plane.partner(dim), device_id_type=MESH,
        )

    def plan(self, stage):
        for half in (0, 1):
            order = self.plane.orders[half][::-1]
            for mask in self.plane.masks[1:]:
                if mask >> order[stage] & 1 and not any(mask >> dim & 1 for dim in order[:stage]):
                    yield half, mask, order[stage]

    def begin(self, stage):
        for half, mask, dim in self.plan(stage):
            self.copy(half, mask, dim).start()

    def add(self, stage, out_ref=None, out_base=0):
        for half, mask, dim in self.plan(stage):
            self.copy(half, mask, dim).wait_recv()
            rows = self.rows(half, mask ^ (1 << dim))
            value = self.ref[rows, :].astype(F32) + self.stage_in[half, mask // 2].astype(F32)
            if stage == self.plane.stages - 1:
                count = value.shape[0]
                out_ref[pl.ds(out_base + half * count, count), :] = value
            else:
                self.ref[rows, :] = value.astype(BF16)

    def drain(self):
        for c in range(self.blocks):
            @pl.when(self.plane.low != c % 2)
            def _(c=c):
                self.core_copy(c).wait_send()

        for stage in range(self.plane.stages):
            for half, mask, dim in self.plan(stage):
                self.copy(half, mask, dim).wait_send()


class Share:
    def __init__(self, plane, source, target, send, recv):
        self.plane, self.source, self.target, self.send, self.recv = plane, source, target, send, recv

    def copy(self, mask):
        return pltpu.make_async_remote_copy(
            src_ref=self.source(mask), dst_ref=self.target(mask), send_sem=self.send.at[mask],
            recv_sem=self.recv.at[mask], device_id=self.plane.device(mask), device_id_type=MESH,
        )

    def begin(self):
        for mask in range(1, self.plane.size):
            self.copy(mask).start()

    def finish(self):
        for mask in range(1, self.plane.size):
            self.copy(mask).wait_recv()

    def drain(self):
        for mask in range(1, self.plane.size):
            self.copy(mask).wait_send()


def chain_barrier(plane, place, count):
    sem = pltpu.get_barrier_semaphore()
    for mask in range(1, plane.size):
        pl.semaphore_signal(sem, inc=1, device_id=plane.device(mask), device_id_type=MESH)
    for d in range(1, count):
        other = lax.rem(place + d, count)
        for sec in (plane.sec, plane.layers - 1 - plane.sec):
            pl.semaphore_signal(sem, inc=1, device_id={"section": sec, "fsdp": other}, device_id_type=MESH)
    pl.semaphore_wait(sem, plane.size - 1 + 2 * (count - 1))


class Row:
    def __init__(self, place, count, source, target, send, recv):
        self.place, self.count, self.source, self.target, self.send, self.recv = place, count, source, target, send, recv

    def copy(self, d):
        return pltpu.make_async_remote_copy(
            src_ref=self.source(d), dst_ref=self.target(d), send_sem=self.send.at[d], recv_sem=self.recv.at[d],
            device_id={"fsdp": lax.rem(self.place + d, self.count)}, device_id_type=MESH,
        )

    def begin(self):
        for d in range(1, self.count):
            self.copy(d).start()

    def finish(self):
        for d in range(1, self.count):
            self.copy(d).wait_recv()

    def drain(self):
        for d in range(1, self.count):
            self.copy(d).wait_send()


class Line:
    def __init__(self, place, count, block, parts, send, recv):
        self.place, self.count, self.block, self.parts, self.send, self.recv = place, count, block, parts, send, recv
        self.ends = (place < count - 1, place > 0)

    def hop(self, side, d, k):
        j = self.place - d if side == 0 else self.place + d
        return pltpu.make_async_remote_copy(
            src_ref=self.block(j, k), dst_ref=self.block(j, k), send_sem=self.send.at[side, d, k],
            recv_sem=self.recv.at[side, d, k], device_id={"fsdp": self.place + 1 if side == 0 else self.place - 1},
            device_id_type=MESH,
        )

    def arrived(self, side, d, k):
        j = self.place - d if side == 0 else self.place + d
        pltpu.make_async_remote_copy(
            src_ref=self.block(j, k), dst_ref=self.block(j, k), send_sem=self.send.at[side, d, k],
            recv_sem=self.recv.at[side, d - 1, k], device_id={"fsdp": self.place + 1 if side == 0 else self.place - 1},
            device_id_type=MESH,
        ).wait_recv()

    def have(self, side, d):
        return self.place >= d if side == 0 else self.place + d < self.count

    def begin(self, k):
        for side in (0, 1):
            @pl.when(self.ends[side])
            def _(side=side):
                self.hop(side, 0, k).start()

    def forward(self, d, k):
        for side in (0, 1):
            @pl.when(self.have(side, d))
            def _(side=side):
                self.arrived(side, d, k)

            if d < self.count - 1:
                @pl.when(self.have(side, d) & self.ends[side])
                def _(side=side):
                    self.hop(side, d, k).start()

    def drain(self):
        for k in range(self.parts):
            for d in range(self.count - 1):
                for side in (0, 1):
                    @pl.when(self.have(side, d) & self.ends[side])
                    def _(side=side, d=d, k=k):
                        self.hop(side, d, k).wait_send()


def forward_kernel(
    layers, heads, blocks, taps, ahead, *refs
):
    own_ref, wgx_ref, ws_ref, wo_ref, vec_ref, tri_ref, spread_ref = refs[:7]
    refs = refs[7:]
    if ahead:
        next_gx, next_o = refs[:2]
        refs = refs[2:]
    raw_ref, ss_ref, pgx_ref, ps_ref, res_ref, ent_ref, full_out_ref = refs[:7]
    refs = refs[7:]
    if ahead:
        ahead_gx, ahead_o = refs[:2]
        refs = refs[2:]
    full_ref, part_ref, pad_ref, state_ref, within_ref, ss_mine, ss_in, core_in, stage_in = refs[:9]
    out_sem, ag_send, ag_recv, core_send, core_recv, rs_send, rs_recv, ss_send, ss_recv = refs[9:18]
    cw = heads * HEAD
    t = pl.program_id(0)
    steps = layers * blocks
    plane = Plane(layers, blocks)
    piece = SPAN // layers
    length = blocks * SPAN

    def start(m):
        return lambda sec, seq: m * length + seq * SPAN + sec * piece

    gathers = [Spread(plane, full_ref, start(m), piece, ag_send.at[m], ag_recv.at[m]) for m in range(layers)]
    sums = [
        Collect(plane, part_ref, m * length, SPAN, core_in.at[m], stage_in.at[m], core_send.at[m], core_recv.at[m],
                rs_send.at[m], rs_recv.at[m])
        for m in range(layers)
    ]
    shares = [
        Share(plane, lambda mask, m=m: ss_mine.at[m], lambda mask, m=m: ss_in.at[m, mask], ss_send.at[m], ss_recv.at[m])
        for m in range(layers)
    ]

    def keep(m):
        rows = pl.ds(m * length, length)
        return pltpu.make_async_copy(full_ref.at[rows, :], full_out_ref.at[rows, :], out_sem.at[m])

    if ahead:
        own_sem, row_send, row_recv, o_send, o_recv = refs[18:]
        spot, count = lax.axis_index("fsdp"), lax.axis_size("fsdp")
        grows = next_gx.shape[0]
        target = ahead_gx.at[pl.ds(pl.multiple_of(spot * grows, 16), grows), :]
        row = Row(spot, count, lambda d: next_gx, lambda d: target, row_send, row_recv)
        orow = Row(spot, count, lambda d: next_o, lambda d: ahead_o.at[spot], o_send, o_recv)
        own_gx = pltpu.make_async_copy(next_gx, target, own_sem.at[0])
        own_o = pltpu.make_async_copy(next_o, ahead_o.at[spot], own_sem.at[1])

        @pl.when(t == 0)
        def _():
            chain_barrier(plane, spot, count)
            own_gx.start()
            own_o.start()

    @pl.when(t == 0)
    def _():
        for m in range(layers):
            rows = pl.multiple_of(start(m)(plane.sec, plane.seq), 16)
            full_ref[pl.ds(rows, piece), :] = own_ref[m * piece : (m + 1) * piece, :]
        ss_mine[...] = jnp.zeros_like(ss_mine)
        if not ahead:
            plane.barrier()
        gathers[0].begin()
        if ahead:
            row.begin()
            orow.begin()
        gathers[0].hop(0)
        gathers[1].begin()
        for stage in range(1, plane.stages):
            gathers[0].hop(stage)
        gathers[0].finish()
        keep(0).start()

    @pl.when(t == blocks)
    def _():
        gathers[1].finish()
        keep(1).start()

    first = lax.rem(t, blocks) == 0

    @pl.when(first)
    def _():
        pad_ref[pl.ds(SPAN, 8), :] = jnp.zeros((8, pad_ref.shape[1]), F32)
        state_ref[...] = jnp.zeros_like(state_ref)

    x = full_ref[pl.ds(pl.multiple_of(t * SPAN, SPAN), SPAN), :]
    pgx = dot(x, wgx_ref[...], 1, 0).astype(BF16)
    ps = dot(x, ws_ref[...], 1, 0).astype(BF16)
    pgx_ref[...] = pgx
    ps_ref[...] = ps
    pad_ref[pl.ds(0, 8), :] = pad_ref[pl.ds(SPAN, 8), :]
    pad_ref[pl.ds(8, SPAN), :cw] = pgx[:, cw:].astype(F32)
    pad_ref[pl.ds(8, SPAN), cw:] = ps[:, : 2 * STATE].astype(F32)
    run = running_conv(pad_ref, vec_ref, taps)
    mixed = (run * sigmoid(run)).astype(BF16)
    xs, b, c = mixed[:, :cw], mixed[:, cw : cw + STATE], mixed[:, cw + STATE :]
    _, _, dt, _, _, cum = step_sizes(plane.own_lanes(ps[:, 2 * STATE :].astype(F32), heads), vec_ref, tri_ref[...])
    cum_t, dt_t = cum.T, dt.T
    inside = inside_mask()
    scores = dot(c, b, 1, 1)
    for h in range(heads):
        mixing = (scores * fading(cum, cum_t, dt_t, h, inside)).astype(BF16)
        within_ref[:, h * HEAD : (h + 1) * HEAD] = dot(mixing, xs[:, h * HEAD : (h + 1) * HEAD], 1, 0)
    tail = jnp.exp(cum[SPAN - 1 : SPAN, :] - cum) * dt
    growth = jnp.exp(cum)
    both = expand(jnp.concatenate([tail, growth], 0), spread_ref[...])
    tail_e, growth_e = both[:SPAN], both[SPAN:]
    xs_f = xs.astype(F32)
    state = state_ref[...]
    state_low = state.astype(BF16)
    ent_ref[0] = state_low
    reach = dot(c, state_low, 1, 0)
    state_ref[...] = growth_e[SPAN - 1 : SPAN, :] * state + dot(b, (xs_f * tail_e).astype(BF16), 0, 0)
    result = (within_ref[...] + growth_e * reach + vec_ref[8:9, :cw] * xs_f).astype(BF16)
    res_ref[...] = result
    gate = pgx[:, :cw].astype(F32)
    g = result.astype(F32) * (gate * sigmoid(gate))
    ss = jnp.sum(g * g, axis=1, keepdims=True)
    ss_mine[t // blocks, pl.ds(lax.rem(t, blocks), 1), :] = jnp.broadcast_to(ss, (SPAN, STATE)).T[0:1, :]
    part_ref[pl.ds(pl.multiple_of(t * SPAN, SPAN), SPAN), :] = dot(
        (g * vec_ref[5:6, :cw]).astype(BF16), wo_ref[...], 1, 0
    ).astype(BF16)

    for m in range(layers):
        for c in range(blocks):
            @pl.when(t == m * blocks + c)
            def _(m=m, c=c):
                sums[m].block_done(c)

    for stage in range(plane.stages):
        @pl.when(t == min(stage * 2, blocks - 1))
        def _(stage=stage):
            gathers[1].hop(stage)

    @pl.when(t == blocks - 1)
    def _():
        shares[0].begin()

    @pl.when(t == blocks)
    def _():
        for c in range(blocks):
            sums[0].block_add(c)
        sums[0].begin(0)

    for stage in range(plane.stages):
        @pl.when(t == blocks + 1 + stage)
        def _(stage=stage):
            sums[0].add(stage, raw_ref, 0)
            if stage + 1 < plane.stages:
                sums[0].begin(stage + 1)

    for c in range(blocks - 1):
        @pl.when(t == blocks + c + 1)
        def _(c=c):
            sums[1].block_add(c)

    @pl.when(t == steps - 1)
    def _():
        shares[1].begin()
        sums[1].block_add(blocks - 1)
        sums[1].begin(0)
        for m in range(layers):
            shares[m].finish()
            total = ss_mine[m]
            for mask in range(1, plane.size):
                total = total + ss_in[m, mask]
            ss_ref[m] = total
        for m in range(layers):
            gathers[m].drain()
            keep(m).wait()
            shares[m].drain()
        sums[0].drain()
        for stage in range(plane.stages):
            sums[1].add(stage, raw_ref, piece)
            if stage + 1 < plane.stages:
                sums[1].begin(stage + 1)
        sums[1].drain()
        if ahead:
            own_gx.wait()
            own_o.wait()
            for each in (row, orow):
                each.finish()
                each.drain()


def backward_kernel(
    layers, heads, blocks, taps, behind, *refs
):
    own_ref, pull_own, r_ref, pgx_ref, ps_ref, hgx_ref, hs_ref, res_ref, ent_ref = refs[:9]
    wgx_ref, ws_ref, wo_ref, vec_ref, tri_ref, spread_ref, gather_ref = refs[9:16]
    refs = refs[16:]
    if behind:
        late_gx, late_o = refs[:2]
        refs = refs[2:]
    raw_ref, gpgx_ref, gps_ref, no_ref, small_ref, full_out_ref = refs[:6]
    refs = refs[6:]
    if behind:
        met_gx, home_o = refs[:2]
        refs = refs[2:]
    full_ref, part_ref, pad_ref, next_ref, ge_ref, within_ref, gxm_ref, pull_ref, core_in, stage_in = refs[:10]
    out_sem, ag_send, ag_recv, core_send, core_recv, rs_send, rs_recv, ss_send, ss_recv = refs[10:19]
    cw = heads * HEAD
    t = pl.program_id(0)
    steps = layers * blocks
    place = lax.rem(t, blocks)
    micro, block = t // blocks, blocks - 1 - place
    plane = Plane(layers, blocks)
    piece = SPAN // layers
    length = blocks * SPAN
    rows_now = pl.ds(pl.multiple_of(micro * length + block * SPAN, SPAN), SPAN)

    def start(m):
        return lambda sec, seq: m * length + seq * SPAN + sec * piece

    gathers = [Spread(plane, full_ref, start(m), piece, ag_send.at[m], ag_recv.at[m]) for m in range(layers)]
    collects = [
        Collect(plane, part_ref, m * length, SPAN, core_in.at[m], stage_in.at[m], core_send.at[m], core_recv.at[m],
                rs_send.at[m], rs_recv.at[m])
        for m in range(layers)
    ]

    def pull_place(sec, seq):
        return pull_ref.at[:, seq, :, pl.ds(pl.multiple_of(sec * piece, piece), piece)]

    share = Share(plane, lambda mask: pull_own, lambda mask: pull_place(plane.sec, plane.seq), ss_send, ss_recv)

    def saving(m):
        rows = pl.ds(m * length, length)
        return pltpu.make_async_copy(full_ref.at[rows, :], full_out_ref.at[rows, :], out_sem.at[m])

    if behind:
        own_sem, row_send, row_recv, o_send, o_recv, h_send, h_recv, met_o, sum_o = refs[19:]
        spot, count = lax.axis_index("fsdp"), lax.axis_size("fsdp")

        def shard(j):
            return late_gx.at[j]

        row = Row(
            spot, count, lambda d: shard(lax.rem(spot + d, count)), lambda d: met_gx.at[spot], row_send, row_recv
        )
        orow = Row(
            spot, count, lambda d: late_o.at[lax.rem(spot + d, count)], lambda d: met_o.at[spot], o_send, o_recv
        )
        own_gx = pltpu.make_async_copy(shard(spot), met_gx.at[spot], own_sem.at[0])
        own_o = pltpu.make_async_copy(late_o.at[spot], met_o.at[spot], own_sem.at[1])
        home = (plane.sec * blocks + plane.seq) // (steps // count)
        to_home = pltpu.make_async_remote_copy(
            src_ref=sum_o, dst_ref=home_o.at[spot], send_sem=h_send.at[0], recv_sem=h_recv.at[spot],
            device_id={"fsdp": home}, device_id_type=MESH,
        )
        at_home = pltpu.make_async_copy(sum_o, home_o.at[spot], h_send.at[0])

        @pl.when(t == 0)
        def _():
            chain_barrier(plane, spot, count)
            own_gx.start()
            own_o.start()

    @pl.when(t == 0)
    def _():
        small_ref[...] = jnp.zeros_like(small_ref)
        for m in range(layers):
            rows = pl.multiple_of(start(m)(plane.sec, plane.seq), 16)
            full_ref[pl.ds(rows, piece), :] = own_ref[m * piece : (m + 1) * piece, :]
        for m in range(layers):
            pull_ref[m, plane.seq, :, pl.ds(pl.multiple_of(plane.sec * piece, piece), piece)] = pull_own[m]
        if not behind:
            plane.barrier()
        share.begin()
        gathers[0].begin()
        if behind:
            orow.begin()
            row.begin()
        gathers[0].hop(0)
        gathers[1].begin()
        for stage in range(1, plane.stages):
            gathers[0].hop(stage)
        gathers[0].finish()
        share.finish()
        saving(0).start()

    @pl.when(t == blocks)
    def _():
        gathers[1].finish()
        saving(1).start()

    @pl.when(place == 0)
    def _():
        next_ref[pl.ds(0, 8), :] = jnp.zeros((8, next_ref.shape[1]), F32)
        ge_ref[...] = jnp.zeros_like(ge_ref)

    pgx, ps = pgx_ref[...], ps_ref[...]
    keep = jnp.where(place == blocks - 1, 0.0, 1.0)
    pad_ref[pl.ds(0, 8), :cw] = hgx_ref[8:, cw:].astype(F32) * keep
    pad_ref[pl.ds(0, 8), cw:] = hs_ref[8:, : 2 * STATE].astype(F32) * keep
    pad_ref[pl.ds(8, SPAN), :cw] = pgx[:, cw:].astype(F32)
    pad_ref[pl.ds(8, SPAN), cw:] = ps[:, : 2 * STATE].astype(F32)
    run = running_conv(pad_ref, vec_ref, taps)
    sig = sigmoid(run)
    mixed = (run * sig).astype(BF16)
    slope = sig * (1.0 + run * (1.0 - sig))
    xs, b, c = mixed[:, :cw], mixed[:, cw : cw + STATE], mixed[:, cw + STATE :]
    xs_f = xs.astype(F32)
    tri = tri_ref[...]
    x, e, dt, decay, rate, cum = step_sizes(plane.own_lanes(ps[:, 2 * STATE :].astype(F32), heads), vec_ref, tri)
    cum_t, dt_t = cum.T, dt.T
    tail = jnp.exp(cum[SPAN - 1 : SPAN, :] - cum) * dt
    growth = jnp.exp(cum)
    both = expand(jnp.concatenate([tail, growth], 0), spread_ref[...])
    tail_e, growth_e = both[:SPAN], both[SPAN:]

    gu = dot(full_ref[rows_now, :], wo_ref[...], 1, 1)
    r = jnp.broadcast_to(r_ref[micro, pl.ds(block, 1), :], (STATE, SPAN)).T[:, 0:1]
    pull = jnp.broadcast_to(pull_ref[micro, block][0:1, :], (STATE, SPAN)).T[:, 0:1]
    gain = vec_ref[5:6, :cw]
    gate = pgx[:, :cw].astype(F32)
    sg = sigmoid(gate)
    sl = gate * sg
    res = res_ref[...].astype(F32)
    g = res * sl
    rg = r * g
    no_ref[...] = (rg * gain).astype(BF16)
    dg = r * (gu * gain) - pull * g
    gr = (dg * sl).astype(BF16)
    gr_f = gr.astype(F32)
    ggate = dg * res * (sg + sl * (1.0 - sg))

    ent = ent_ref[0]
    ge = ge_ref[...]
    gl = ge.astype(BF16)
    reach = dot(c, ent, 1, 0)
    pulled = tail_e * dot(b, gl, 1, 0)
    gq = (growth_e * gr_f).astype(BF16)
    grad_c = dot(gq, ent, 1, 1)
    grad_b = dot((xs_f * tail_e).astype(BF16), gl, 1, 1)
    fade = growth_e[SPAN - 1 : SPAN, :]
    ge_ref[...] = fade * ge + dot(c, gq, 0, 0)
    grad_fade = fade * jnp.sum(ge * ent.astype(F32), axis=0, keepdims=True)
    inside = inside_mask()
    scores = dot(c, b, 1, 1)
    gs = jnp.zeros((SPAN, SPAN), F32)
    for h in range(heads):
        cols = slice(h * HEAD, (h + 1) * HEAD)
        fade_in = fading(cum, cum_t, dt_t, h, inside)
        mixing = (scores * fade_in).astype(BF16)
        gs = gs + dot(gr[:, cols], xs[:, cols], 1, 1) * fade_in
        within_ref[:, cols] = dot(mixing, xs[:, cols], 1, 0)
        gxm_ref[:, cols] = dot(mixing, gr[:, cols], 0, 0)
    gs = gs.astype(BF16)
    grad_c = grad_c + dot(gs, b, 1, 0)
    grad_b = grad_b + dot(gs, c, 0, 0)
    gxm = gxm_ref[...]
    grad_x = vec_ref[8:9, :cw] * gr_f + pulled + gxm

    gather = gather_ref[...]
    last = xs_f * pulled
    sums = per_head(jnp.concatenate([gr_f * (within_ref[...] + growth_e * reach), xs_f * gxm + last], 0), gather)
    s1, s2 = sums[:SPAN], sums[SPAN:]
    thin = jnp.concatenate(
        [
            jnp.sum(gr_f * xs_f, axis=0, keepdims=True),
            grad_fade + jnp.sum(last, axis=0, keepdims=True),
            jnp.zeros((6, cw), F32),
        ],
        0,
    )
    thin = per_head(thin, gather)
    hi, mid, low = split3(s1 - s2)
    packed = dot(tri, jnp.concatenate([hi, mid, low], 1), 0, 0)
    grad_rate = packed[:, :STATE] + packed[:, STATE : 2 * STATE] + packed[:, 2 * STATE :]
    grad_rate = grad_rate + thin[1:2, :]
    denominator = 1.0 + e
    slope_x = jnp.where(x >= 0, 1.0, e) / denominator
    ratio = jnp.where(x < -20.0, 1.0, slope_x / jnp.maximum(dt, 1e-12))
    grad_raw = s2 * ratio - decay * grad_rate * slope_x
    small_ref[6:7, :STATE] += jnp.sum(grad_raw, axis=0, keepdims=True)
    small_ref[7:8, :STATE] += jnp.sum(grad_rate * rate, axis=0, keepdims=True)
    small_ref[8:9, :STATE] += thin[0:1, :]
    small_ref[5:6, :cw] += jnp.sum(gu * rg, axis=0, keepdims=True)

    grun = jnp.concatenate([grad_x, grad_b, grad_c], 1) * slope
    next_ref[pl.ds(SPAN, 8), :] = next_ref[pl.ds(0, 8), :]
    next_ref[pl.ds(0, SPAN), :] = grun
    small_ref[taps : taps + 1, :] += jnp.sum(grun, axis=0, keepdims=True)
    gbefore = jnp.zeros_like(grun)
    for k in range(taps):
        small_ref[k : k + 1, :] += jnp.sum(
            grun * pad_ref[pl.ds(8 - taps + 1 + k, SPAN), :], axis=0, keepdims=True
        )
        gbefore = gbefore + vec_ref[k : k + 1, :] * next_ref[pl.ds(taps - 1 - k, SPAN), :]
    gpgx = jnp.concatenate([ggate, gbefore[:, :cw]], 1).astype(BF16)
    gps = jnp.concatenate([gbefore[:, cw:], plane.all_lanes(grad_raw, heads)], 1).astype(BF16)
    gpgx_ref[...] = gpgx
    gps_ref[...] = gps
    part_ref[rows_now, :] = (dot(gpgx, wgx_ref[...], 1, 1) + dot(gps, ws_ref[...], 1, 1)).astype(BF16)

    for m in range(layers):
        for c in range(blocks):
            @pl.when(t == m * blocks + blocks - 1 - c)
            def _(m=m, c=c):
                collects[m].block_done(c)

    for stage in range(plane.stages):
        @pl.when(t == min(stage, blocks - 1))
        def _(stage=stage):
            gathers[1].hop(stage)

    if behind:
        @pl.when(t == steps - 3)
        def _():
            own_o.wait()
            orow.finish()
            total = met_o[0].astype(F32)
            for j in range(1, count):
                total = total + met_o[j].astype(F32)
            sum_o[...] = total.astype(BF16)

            @pl.when(spot == home)
            def _():
                at_home.start()

            @pl.when(spot != home)
            def _():
                to_home.start()

    @pl.when(t == blocks)
    def _():
        for c in range(blocks):
            collects[0].block_add(c)
        collects[0].begin(0)

    for stage in range(plane.stages):
        @pl.when(t == blocks + 1 + stage)
        def _(stage=stage):
            collects[0].add(stage, raw_ref, 0)
            if stage + 1 < plane.stages:
                collects[0].begin(stage + 1)

    for c in range(1, blocks):
        @pl.when(t == blocks + blocks - c)
        def _(c=c):
            collects[1].block_add(c)

    @pl.when(t == steps - 1)
    def _():
        collects[1].block_add(0)
        collects[1].begin(0)
        share.drain()
        for m in range(layers):
            gathers[m].drain()
            saving(m).wait()
        collects[0].drain()
        for stage in range(plane.stages):
            collects[1].add(stage, raw_ref, piece)
            if stage + 1 < plane.stages:
                collects[1].begin(stage + 1)
        collects[1].drain()
        if behind:
            own_gx.wait()
            row.finish()
            row.drain()
            orow.drain()

            @pl.when(spot == home)
            def _():
                at_home.wait()
                for d in range(1, count):
                    other = lax.rem(spot + d, count)
                    pltpu.make_async_remote_copy(
                        src_ref=sum_o, dst_ref=home_o.at[other], send_sem=h_send.at[0], recv_sem=h_recv.at[other],
                        device_id={"fsdp": home}, device_id_type=MESH,
                    ).wait_recv()

            @pl.when(spot != home)
            def _():
                to_home.wait_send()


def tables(heads):
    cw = heads * HEAD
    tri = np.tril(np.ones((SPAN, SPAN), np.float32))
    one = (np.arange(cw)[None, :] // HEAD == np.arange(STATE)[:, None]).astype(np.float32)
    spread3 = np.concatenate([one] * 3, 0)
    gather3 = np.concatenate([one.T] * 2, 0)
    return jnp.asarray(tri, BF16), jnp.asarray(spread3, BF16), jnp.asarray(gather3, BF16)


def whole(a):
    return pl.BlockSpec(memory_space=pltpu.VMEM)


def plane_scratch(layers, blocks, width):
    size, piece = layers * blocks, SPAN // layers
    dma = pltpu.SemaphoreType.DMA
    return [
        pltpu.VMEM((layers, blocks // 2, SPAN, width), BF16),
        pltpu.VMEM((layers, 2, size // 2, piece // 2, width), BF16),
        dma((layers,)),
        dma((layers, 2, size)),
        dma((layers, 2, size)),
        dma((layers, blocks)),
        dma((layers, blocks)),
        dma((layers, 2, size // 2)),
        dma((layers, 2, size // 2)),
    ]


def layer_forward(own, wgx, ws, wo, vec, taps, number, *following):
    layers, blocks, depth = lax.axis_size("section"), lax.axis_size("seq"), lax.axis_size("fsdp")
    width = own.shape[1]
    cw = wo.shape[0]
    heads = cw // HEAD
    steps = layers * blocks
    tokens = steps * SPAN
    tri, spread3, _ = tables(heads)
    rows = lambda w: pl.BlockSpec((SPAN, w), lambda t: (t, 0))
    chans = cw + 2 * STATE
    vmem = pl.BlockSpec(memory_space=pltpu.VMEM)
    dma = pltpu.SemaphoreType.DMA
    return pl.pallas_call(
        functools.partial(forward_kernel, layers, heads, blocks, taps, bool(following)),
        grid=(steps,),
        in_specs=[vmem] * 7 + [pl.BlockSpec(memory_space=pl.ANY)] * len(following),
        out_specs=[
            vmem,
            vmem,
            rows(2 * cw),
            rows(3 * STATE),
            rows(cw),
            pl.BlockSpec((1, STATE, cw), lambda t: (t, 0, 0)),
            pl.BlockSpec(memory_space=pl.ANY),
        ]
        + [pl.BlockSpec(memory_space=pl.ANY)] * len(following),
        out_shape=[
            jax.ShapeDtypeStruct(own.shape, F32),
            jax.ShapeDtypeStruct((layers, 8, SPAN), F32),
            jax.ShapeDtypeStruct((tokens, 2 * cw), BF16),
            jax.ShapeDtypeStruct((tokens, 3 * STATE), BF16),
            jax.ShapeDtypeStruct((tokens, cw), BF16),
            jax.ShapeDtypeStruct((steps, STATE, cw), BF16),
            jax.ShapeDtypeStruct((tokens, width), BF16),
        ]
        + ([jax.ShapeDtypeStruct(wgx.shape, BF16), jax.ShapeDtypeStruct((depth,) + following[1].shape, BF16)] if following else []),
        scratch_shapes=[
            pltpu.VMEM((tokens, width), BF16),
            pltpu.VMEM((tokens, width), BF16),
            pltpu.VMEM((SPAN + 8, chans), F32),
            pltpu.VMEM((STATE, cw), F32),
            pltpu.VMEM((SPAN, cw), F32),
            pltpu.VMEM((layers, 8, SPAN), F32),
            pltpu.VMEM((layers, steps, 8, SPAN), F32),
        ]
        + plane_scratch(layers, blocks, width)
        + [dma((layers, steps)), dma((layers, steps))]
        + ([dma((2,))] + [dma((depth,))] * 4 if following else []),
        compiler_params=pltpu.CompilerParams(
            vmem_limit_bytes=60 << 20, collective_id=number, has_side_effects=True
        ),
        cost_estimate=pl.CostEstimate(
            flops=2 * tokens * width * (3 * cw + 3 * STATE) + 2 * tokens * cw * 700,
            bytes_accessed=4 * tokens * width + 2 * width * (3 * cw + 3 * STATE) + 8 * tokens * cw,
            transcendentals=tokens * SPAN * heads,
        ),
        name="layer_forward",
    )(own, wgx, ws, wo, vec, tri, spread3, *following)


def layer_backward(own, pull, r_rows, pgx, ps, res, ent, wgx, ws, wo, vec, taps, number, *late):
    layers, blocks, depth = lax.axis_size("section"), lax.axis_size("seq"), lax.axis_size("fsdp")
    width = own.shape[1]
    cw = wo.shape[0]
    heads = cw // HEAD
    steps = layers * blocks
    tokens = steps * SPAN
    tri, spread3, gather3 = tables(heads)
    chans = cw + 2 * STATE
    vmem = pl.BlockSpec(memory_space=pltpu.VMEM)
    dma = pltpu.SemaphoreType.DMA

    def at(t):
        return t - lax.rem(t, blocks) + (blocks - 1 - lax.rem(t, blocks))

    rows = lambda w: pl.BlockSpec((SPAN, w), lambda t: (at(t), 0))
    edge = lambda w: pl.BlockSpec((16, w), lambda t: (jnp.maximum(at(t) * (SPAN // 16) - 1, 0), 0))
    return pl.pallas_call(
        functools.partial(backward_kernel, layers, heads, blocks, taps, bool(late)),
        grid=(steps,),
        in_specs=[
            vmem,
            vmem,
            vmem,
            rows(2 * cw),
            rows(3 * STATE),
            edge(2 * cw),
            edge(3 * STATE),
            rows(cw),
            pl.BlockSpec((1, STATE, cw), lambda t: (at(t), 0, 0)),
        ]
        + [vmem] * 7
        + [pl.BlockSpec(memory_space=pl.ANY)] * len(late),
        out_specs=[
            vmem,
            rows(2 * cw),
            rows(3 * STATE),
            rows(cw),
            vmem,
            pl.BlockSpec(memory_space=pl.ANY),
        ]
        + [pl.BlockSpec(memory_space=pl.ANY)] * len(late),
        out_shape=[
            jax.ShapeDtypeStruct(own.shape, F32),
            jax.ShapeDtypeStruct((tokens, 2 * cw), BF16),
            jax.ShapeDtypeStruct((tokens, 3 * STATE), BF16),
            jax.ShapeDtypeStruct((tokens, cw), BF16),
            jax.ShapeDtypeStruct((16, chans), F32),
            jax.ShapeDtypeStruct((tokens, width), BF16),
        ]
        + (
            [
                jax.ShapeDtypeStruct(late[0].shape, BF16),
                jax.ShapeDtypeStruct(late[1].shape, BF16),
            ]
            if late
            else []
        ),
        scratch_shapes=[
            pltpu.VMEM((tokens, width), BF16),
            pltpu.VMEM((tokens, width), BF16),
            pltpu.VMEM((SPAN + 8, chans), F32),
            pltpu.VMEM((SPAN + 8, chans), F32),
            pltpu.VMEM((STATE, cw), F32),
            pltpu.VMEM((SPAN, cw), F32),
            pltpu.VMEM((SPAN, cw), F32),
            pltpu.VMEM((layers, blocks, 8, SPAN), F32),
        ]
        + plane_scratch(layers, blocks, width)
        + [dma((steps,)), dma((steps,))]
        + (
            [dma((2,))] + [dma((depth,))] * 4 + [dma((1,)), dma((depth,))]
            + [pltpu.VMEM(late[1].shape, BF16), pltpu.VMEM(late[1].shape[1:], BF16)]
            if late
            else []
        ),
        compiler_params=pltpu.CompilerParams(
            vmem_limit_bytes=60 << 20, collective_id=number, has_side_effects=True
        ),
        cost_estimate=pl.CostEstimate(
            flops=2 * tokens * width * (3 * cw + 3 * STATE) + 2 * tokens * cw * 2000,
            bytes_accessed=4 * tokens * width + 2 * width * (3 * cw + 3 * STATE) + 8 * tokens * cw,
            transcendentals=tokens * SPAN * heads,
        ),
        name="layer_backward",
    )(own, pull, r_rows, pgx, ps, pgx, ps, res, ent, wgx, ws, wo, vec, tri, spread3, gather3, *late)


class Publish:
    def __init__(self, plane, cells, view, own, other, condition, send, recv):
        self.plane, self.cells, self.view, self.own, self.other = plane, cells, view, own, other
        self.condition = condition
        self.send, self.recv = send, recv
        self.outer = [dim for dim in range(2, plane.stages + 1)]

    def number(self, mask):
        sec, seq = self.plane.owner(mask)
        return sec * self.plane.ranks + seq

    def copy(self, mask, dim, cell):
        dst = self.view(self.number(mask), cell)
        src = self.other(cell) if dim == 1 else self.own(cell) if mask == 0 else dst
        key = mask ^ (1 << dim)
        return pltpu.make_async_remote_copy(
            src_ref=src, dst_ref=dst, send_sem=self.send.at[key, cell], recv_sem=self.recv.at[key, cell],
            device_id=self.plane.partner(dim), device_id_type=MESH,
        )

    def when(self, mask, act):
        pl.when(self.condition(self.number(mask)))(act)

    def stage(self, mask):
        return max([i for i, dim in enumerate(self.outer) if mask >> dim & 1], default=-1)

    def across(self, cell):
        self.when(0, lambda: self.copy(0, 1, cell).start())

    def forward(self, mask, cell):
        def act():
            for dim in self.outer[self.stage(mask) + 1 :] + [0]:
                self.copy(mask, dim, cell).start()

        self.when(mask, act)

    def arrived(self, mask, cell):
        def act():
            view = self.view(self.number(mask), cell)
            pltpu.make_async_remote_copy(
                src_ref=view, dst_ref=view, send_sem=self.send.at[mask, cell], recv_sem=self.recv.at[mask, cell],
                device_id=self.plane.partner(0), device_id_type=MESH,
            ).wait_recv()

        self.when(mask, act)

    def step(self, mask, cell):
        self.arrived(mask, cell)
        self.forward(mask, cell)

    def finish(self):
        for mask in self.plane.masks:
            for cell in range(self.cells):
                self.arrived(mask + 1, cell)

    def drain(self):
        for mask in self.plane.masks:
            dims = self.outer[self.stage(mask) + 1 :] + [0] + ([1] if mask == 0 else [])

            def act(mask=mask, dims=dims):
                for cell in range(self.cells):
                    for dim in dims:
                        self.copy(mask, dim, cell).wait_send()

            self.when(mask, act)


def finish_kernel(
    layers, ranks, parts, oparts, tr, thin_rows,
    full_ref, gp_ref, gps_ref, no_ref, gb_ref, late_ref, met_ref, home_ref, sm_ref, gn_ref, swap_ref,
    gall, oall, sm_all, gn_out, got_ref,
    sum_ref, osum_ref, in_ref, oin_ref, late_gx, done_gx, thin_ref, thin_f, tz_ref, tin_ref, core_in, stage_in, tall,
    sm_in, sm_sum, gn_in, gn_plane,
    send_sem, recv_sem, osend_sem, orecv_sem, core_send, core_recv, rs_send, rs_recv, tz_send, tz_recv,
    g_send, g_recv, p_send, p_recv, t_send, t_recv, s_send, s_recv, n_send, n_recv, zs_send, zs_recv, zn_send, zn_recv,
    swap_send, swap_recv, own_sem,
):
    place, count = lax.axis_index("fsdp"), lax.axis_size("fsdp")
    plane = Plane(layers, ranks)
    here = plane.sec * ranks + plane.seq
    per = plane.size // count
    home = here // per
    cols, rows = late_gx.shape
    cw = cols // 2
    piece = cols // parts
    opiece = osum_ref.shape[1]
    chain_barrier(plane, place, count)

    swap = pltpu.make_async_remote_copy(
        src_ref=swap_ref, dst_ref=got_ref, send_sem=swap_send.at[0], recv_sem=swap_recv.at[0],
        device_id=plane.partner(1), device_id_type=MESH,
    )
    sm_lines = Row(place, count, lambda d: sm_ref, lambda d: sm_in.at[d], zs_send, zs_recv)
    gn_lines = Row(place, count, lambda d: gn_ref, lambda d: gn_in.at[d], zn_send, zn_recv)
    sm_lines.begin()
    gn_lines.begin()
    shares = [
        Share(plane, lambda mask: sm_sum.at[plane.owner(mask)[0]], lambda mask: sm_all.at[here], s_send, s_recv),
        Share(plane, lambda mask: gn_plane.at[0], lambda mask: gn_plane.at[mask], n_send, n_recv),
    ]

    def gx_window(d, cell):
        half, rest = cell // (parts // 2), cell % (parts // 2)
        at = half * (cw * plane.size) + d * cw + rest * piece
        return gall.at[pl.ds(pl.multiple_of(at, 16), piece), :]

    def gx_source(ref):
        return lambda cell: ref.at[pl.ds(cell * piece, piece), :]

    def o_window(d, cell):
        return oall.at[lax.rem(d, per), pl.ds(cell * opiece, opiece), :]

    def early_o(cell):
        return home_ref.at[pl.ds(cell * opiece, opiece), :]

    def new_o(cell):
        return osum_ref.at[cell]

    always, at_home = (lambda d: d >= 0), (lambda d: d // per == place)
    early_gx, new_gx = gx_source(late_gx), gx_source(done_gx)
    gpub = [
        Publish(plane, parts, gx_window, new_gx, early_gx, always, g_send, g_recv),
        Publish(plane, parts, gx_window, early_gx, new_gx, always, g_send, g_recv),
    ]
    opub = [
        Publish(plane, oparts, o_window, new_o, early_o, at_home, p_send, p_recv),
        Publish(plane, oparts, o_window, early_o, new_o, at_home, p_send, p_recv),
    ]
    locals_of = {}
    base = 0
    for name, pubs in (("gx", gpub), ("o", opub)):
        for number in range(layers):
            locals_of[name, number] = base
        base += pubs[0].cells

    def side(number):
        return pltpu.make_async_copy(
            tall.at[pl.ds(number * thin_rows, thin_rows), :],
            gall.at[pl.ds(plane.size * cols, thin_rows), :], own_sem.at[parts + oparts],
        )

    def store(pub, name, number, cell):
        return pltpu.make_async_copy(pub.own(cell), pub.view(here, cell), own_sem.at[locals_of[name, number] + cell])

    def release(layer, name, cells):
        for number in range(layers):
            pub = (gpub if name == "gx" else opub)[number]

            @pl.when(plane.sec == number)
            def _(number=number, pub=pub):
                for cell in cells:
                    if number == layer:
                        pub.when(0, store(pub, name, number, cell).start)
                        pub.forward(0, cell)
                    else:
                        pub.across(cell)

    def flow(layer, name, mask, cells):
        pub = (gpub if name == "gx" else opub)[layer]

        @pl.when(plane.sec == layer)
        def _():
            for cell in cells:
                pub.step(mask, cell)

    upper = [m for m in plane.masks if m > 2]
    upper = sorted(upper, key=lambda m: (gpub[0].stage(m), m & 2))
    gcells, ocells = range(parts), range(oparts)

    total = met_ref[0].astype(F32)
    for j in range(1, count):
        total = total + met_ref[j].astype(F32)
    late_gx[...] = total.astype(BF16)
    release(1, "gx", gcells)
    release(1, "o", ocells)
    swap.start()

    first = dot(gps_ref[...], full_ref[...], 0, 0).astype(BF16)
    thin_ref[pl.ds(0, thin_rows), :] = first[:thin_rows, :]
    thin_ref[pl.ds(thin_rows, thin_rows), :] = late_ref[:thin_rows, :]
    rest = thin_ref.shape[0] - layers * thin_rows
    thin_ref[pl.ds(layers * thin_rows, rest), :] = jnp.zeros((rest, thin_ref.shape[1]), BF16)
    thin = Collect(plane, thin_ref, 0, layers * tr, core_in, stage_in, core_send, core_recv, rs_send, rs_recv)
    for c in range(ranks):
        thin.block_done(c)
    lines = Row(
        place, count, lambda d: tz_ref.at[lax.rem(place + d, count)], lambda d: tin_ref.at[place], tz_send, tz_recv
    )
    spread = Spread(plane, tall, lambda sec, seq: (seq * layers + sec) * tr, tr, t_send, t_recv)

    behind = (place > 0, place < count - 1)

    def hop(j, k, side):
        return pltpu.make_async_remote_copy(
            src_ref=sum_ref.at[j, k], dst_ref=in_ref.at[side, j, k], send_sem=send_sem.at[j, k],
            recv_sem=recv_sem.at[side, j, k], device_id={"fsdp": place + 1 if side == 0 else place - 1},
            device_id_type=MESH,
        )

    def ohop(k, side):
        return pltpu.make_async_remote_copy(
            src_ref=osum_ref.at[k], dst_ref=oin_ref.at[side, k], send_sem=osend_sem.at[k],
            recv_sem=orecv_sem.at[side, k], device_id={"fsdp": place + 1 if side == 0 else place - 1},
            device_id_type=MESH,
        )

    def absorb(j, k, side):
        hop(j, k, side).wait_recv()
        sum_ref[j, k] = (sum_ref[j, k].astype(F32) + in_ref[side, j, k].astype(F32)).astype(BF16)

    def oabsorb(k, side):
        ohop(k, side).wait_recv()
        osum_ref[k] = (osum_ref[k].astype(F32) + oin_ref[side, k].astype(F32)).astype(BF16)

    def oitem(k):
        osum_ref[k] = dot(no_ref[:, k * opiece : (k + 1) * opiece], gb_ref[...], 0, 0).astype(BF16)
        for side in (0, 1):
            beyond = (place < home) if side == 0 else (place > home)

            @pl.when(beyond & behind[side])
            def _(side=side):
                oabsorb(k, side)

            @pl.when(beyond)
            def _(side=side):
                ohop(k, side).start()

    def work(j, k):
        sum_ref[j, k] = dot(
            gp_ref[:, k * piece : (k + 1) * piece], full_ref[:, j * rows : (j + 1) * rows], 0, 0
        ).astype(BF16)

    def shift(j, k):
        for side in (0, 1):
            beyond = (place < j) if side == 0 else (place > j)

            @pl.when(beyond & behind[side])
            def _(side=side):
                absorb(j, k, side)

            @pl.when(beyond)
            def _(side=side):
                hop(j, k, side).start()

    def items(pair, k):
        for j in pair:
            work(j, k)

        @pl.when(place < count // 2)
        def _():
            for j in pair:
                shift(j, k)

        @pl.when(place >= count // 2)
        def _():
            for j in pair[::-1]:
                shift(j, k)

    def final(k):
        for j in range(count):
            @pl.when(place == j)
            def _(j=j):
                for side in (0, 1):
                    @pl.when(behind[side])
                    def _(side=side):
                        absorb(j, k, side)

                done_gx[pl.ds(k * piece, piece), :] = sum_ref[j, k]

        release(0, "gx", [k])

    def ofinal(k):
        for side in (0, 1):
            @pl.when((place == home) & behind[side])
            def _(side=side):
                oabsorb(k, side)

        release(0, "o", [k])

    def small_sums():
        sm_lines.finish()
        gn_lines.finish()
        mine, gain = sm_ref[...].astype(F32), gn_ref[...]
        for d in range(1, count):
            mine, gain = mine + sm_in[d].astype(F32), gain + gn_in[d]
        sm_sum[...] = mine.astype(BF16)
        sm_all[here] = sm_sum[plane.sec]
        gn_plane[0] = gain
        for share in shares:
            share.begin()

    def thin_stage(stage):
        thin.add(stage, thin_f, 0)
        if stage + 1 < plane.stages:
            thin.begin(stage + 1)

    def thin_across():
        span = tz_ref.shape[2]
        for j in range(count):
            tz_ref[j] = thin_f[:, j * span : (j + 1) * span].astype(BF16)
        lines.begin()

    def thin_back():
        lines.finish()
        value = tz_ref[place].astype(F32)
        for d in range(1, count):
            value = value + tin_ref[lax.rem(place + d, count)].astype(F32)
        at = pl.multiple_of((plane.seq * layers + plane.sec) * tr, 16)
        tall[pl.ds(at, tr), :] = value.astype(BF16)
        spread.begin()

    todo = [lambda: ([thin.block_add(c) for c in range(ranks)], thin.begin(0)), small_sums]
    todo += [lambda stage=stage: thin_stage(stage) for stage in range(plane.stages)]
    todo += [thin_across, thin_back]
    todo += [lambda stage=stage: spread.hop(stage) for stage in range(plane.stages)]

    def advance(n):
        for _ in range(n):
            if todo:
                todo.pop(0)()

    def part(k):
        return [k]

    pairs = [(count - 1 - i, i) for i in range(count // 2)]
    done = {}

    def onward(name, stage, upto):
        begin = done.get((name, stage), 0)
        cells = list(range(begin, max(begin, min(upto, parts if name == "gx" else oparts))))
        if cells:
            done[name, stage] = cells[-1] + 1
            for mask in [2] if stage == 0 else upper:
                flow(0, name, mask, cells)

    rounds = max(parts, oparts, 3)
    for k in range(rounds):
        if k < oparts:
            oitem(k)
        if k == 1:
            for mask in upper:
                flow(1, "gx", mask, gcells)
        if 1 <= k <= oparts:
            ofinal(k - 1)
        advance(1)
        for number, pair in enumerate(pairs):
            if k < parts:
                items(pair, k)
            advance(1)
            if number == 0:
                onward("gx", 0, k - 1)
                onward("o", 0, k - 1)
        onward("gx", 1, k - 1)
        onward("o", 1, k - 2)
        if k == 0:
            flow(1, "gx", 2, gcells)
        if k == 1:
            flow(1, "o", 2, ocells)
        if k == 2:
            for mask in upper:
                flow(1, "o", mask, ocells)
        if 1 <= k <= parts:
            final(k - 1)
    if rounds == oparts:
        ofinal(oparts - 1)
    advance(len(todo))
    if rounds == parts:
        onward("gx", 0, parts - 1)
        onward("gx", 1, parts - 1)
        final(parts - 1)
    onward("o", 0, oparts)
    onward("o", 1, oparts - 1)
    onward("gx", 0, parts)
    onward("gx", 1, parts)
    onward("o", 1, oparts)

    spread.finish()
    for number in range(layers):
        @pl.when(plane.sec == number)
        def _(number=number):
            side(number).start()
            for name, pubs in (("gx", gpub), ("o", opub)):
                for cell in range(pubs[number].cells):
                    pubs[number].when(0, store(pubs[number], name, number, cell).wait)
            side(number).wait()
    for share in shares:
        share.finish()
    value = gn_plane[0]
    for mask in range(1, plane.size):
        value = value + gn_plane[mask]
    gn_out[...] = value
    gpub[0].finish()
    opub[0].finish()
    swap.wait()
    for each in [gpub[0], opub[0], spread, lines, thin, sm_lines, gn_lines] + shares:
        each.drain()
    for k in range(oparts):
        @pl.when(place != home)
        def _(k=k):
            ohop(k, 0).wait_send()

    for k in range(parts):
        for j in range(count):
            @pl.when(place != j)
            def _(k=k, j=j):
                hop(j, k, 0).wait_send()


def finish(full, gp, gps, no, gb, late, met, home, sm, gn, swap, number):
    layers, ranks, count = lax.axis_size("section"), lax.axis_size("seq"), lax.axis_size("fsdp")
    size = layers * ranks
    tokens, width = full.shape
    rows, cols, cw = width // count, gp.shape[1], no.shape[1]
    parts = 4 if cw % 384 == 0 else 2
    oparts = cw // STATE if cw % STATE == 0 else 1
    thin_rows = 2 * STATE + size * cw // HEAD
    tr = -(-layers * thin_rows // (32 * size)) * 32
    piece, opiece = cols // parts, cw // oparts
    dma = pltpu.SemaphoreType.DMA
    anywhere, vmem = pl.BlockSpec(memory_space=pl.ANY), pl.BlockSpec(memory_space=pltpu.VMEM)
    return pl.pallas_call(
        functools.partial(finish_kernel, layers, ranks, parts, oparts, tr, thin_rows),
        in_specs=[vmem] * 7 + [anywhere, vmem, vmem, anywhere],
        out_specs=[anywhere, anywhere, vmem, vmem, anywhere],
        out_shape=[
            jax.ShapeDtypeStruct((size * cols + thin_rows, rows), BF16),
            jax.ShapeDtypeStruct((size // count, cw, width), BF16),
            jax.ShapeDtypeStruct((size,) + sm.shape[1:], BF16),
            jax.ShapeDtypeStruct(gn.shape, F32),
            jax.ShapeDtypeStruct(swap.shape, BF16),
        ],
        scratch_shapes=[
            pltpu.VMEM((count, parts, piece, rows), BF16),
            pltpu.VMEM((oparts, opiece, width), BF16),
            pltpu.VMEM((2, count, parts, piece, rows), BF16),
            pltpu.VMEM((2, oparts, opiece, width), BF16),
            pltpu.VMEM((cols, rows), BF16),
            pltpu.VMEM((cols, rows), BF16),
            pltpu.VMEM((size * tr, width), BF16),
            pltpu.VMEM((tr, width), F32),
            pltpu.VMEM((count, tr, rows), BF16),
            pltpu.VMEM((count, tr, rows), BF16),
            pltpu.VMEM((ranks // 2, layers * tr, width), BF16),
            pltpu.VMEM((2, size // 2, tr // 2, width), BF16),
            pltpu.VMEM((size * tr, rows), BF16),
            pltpu.VMEM((count,) + sm.shape, BF16),
            pltpu.VMEM(sm.shape, BF16),
            pltpu.VMEM((count,) + gn.shape, F32),
            pltpu.VMEM((size,) + gn.shape, F32),
            dma((count, parts)),
            dma((2, count, parts)),
            dma((oparts,)),
            dma((2, oparts)),
            dma((ranks,)),
            dma((ranks,)),
            dma((2, size // 2)),
            dma((2, size // 2)),
            dma((count,)),
            dma((count,)),
            dma((size, parts)),
            dma((size, parts)),
            dma((size, oparts)),
            dma((size, oparts)),
            dma((2, size)),
            dma((2, size)),
            dma((size,)),
            dma((size,)),
            dma((size,)),
            dma((size,)),
            dma((count,)),
            dma((count,)),
            dma((count,)),
            dma((count,)),
            dma((1,)),
            dma((1,)),
            dma((parts + oparts + 1,)),
        ],
        compiler_params=pltpu.CompilerParams(
            collective_id=number, has_side_effects=True, vmem_limit_bytes=60 << 20
        ),
        cost_estimate=pl.CostEstimate(
            flops=2 * tokens * width * (cols + cw + gps.shape[1]),
            bytes_accessed=2 * tokens * (2 * width + cols + cw), transcendentals=0,
        ),
        name="finish",
    )(full, gp, gps, no, gb, late, met, home, sm, gn, swap)


def start_kernel(
    layers, ranks, parts, oparts,
    mine, theirs, mine_o, theirs_o, ends_ref, strip_ref, packed_ref,
    full, all_o, next_gx, next_o, got_ref, thin_ref, params_ref,
    own_sem, y_send, y_recv, x_send, x_recv, send, recv, o_send, o_recv, cut_send, cut_recv,
    st_send, st_recv, ag_send, ag_recv, pa_send, pa_recv,
):
    place, count = lax.axis_index("fsdp"), lax.axis_size("fsdp")
    plane = Plane(layers, ranks)
    low = plane.sec == 0
    rows = mine.shape[0]
    piece = rows // parts
    opiece = mine_o.shape[1] // oparts
    orows = mine_o.shape[0] * mine_o.shape[1]
    out_rows = layers * ranks * orows // count
    here = plane.sec * ranks + plane.seq
    there = (layers - 1 - plane.sec) * ranks + plane.seq
    source = (here * orows) // out_rows == place
    source_there = (there * orows) // out_rows == place
    across = plane.partner(1)

    def block(j, k):
        return full.at[pl.ds(pl.multiple_of(j * rows + k * piece, 16), piece), :]

    def oblock(j, k):
        return all_o.at[j, pl.ds(k * opiece, opiece), :]

    def y_copy(k, dst):
        return pltpu.make_async_remote_copy(
            src_ref=theirs.at[pl.ds(k * piece, piece), :], dst_ref=dst, send_sem=y_send.at[k], recv_sem=y_recv.at[k],
            device_id=across, device_id_type=MESH,
        )

    def cut(d, same, first):
        spot = lax.rem(place + d, count)
        return pltpu.make_async_remote_copy(
            src_ref=(mine_o if same else theirs_o).at[spot], dst_ref=all_o.at[spot] if first else next_o,
            send_sem=cut_send.at[0 if same else 1, d], recv_sem=cut_recv.at[0 if first else 1],
            device_id={"section": plane.sec if same else layers - 1 - plane.sec, "fsdp": spot}, device_id_type=MESH,
        )

    def own_cut(first):
        return pltpu.make_async_copy(mine_o.at[place], all_o.at[place] if first else next_o, own_sem.at[3])

    def begin_cuts(same, first, condition):
        @pl.when(condition)
        def _():
            if same:
                own_cut(first).start()
            for d in range(1 if same else 0, count):
                cut(d, same, first).start()

    half = ends_ref.shape[1] // layers
    x_copy = pltpu.make_async_remote_copy(
        src_ref=ends_ref.at[:, pl.ds(pl.multiple_of((layers - 1 - plane.sec) * half, 16), half), :], dst_ref=got_ref,
        send_sem=x_send.at[0], recv_sem=x_recv.at[0], device_id=across, device_id_type=MESH,
    )
    strips = Row(
        place, count, lambda d: strip_ref, lambda d: thin_ref.at[plane.sec, plane.seq, place], st_send, st_recv
    )
    hold = count // 2
    spread = Spread(plane, thin_ref, None, 0, ag_send, ag_recv)
    spread.view = lambda h, mask: thin_ref.at[plane.owner(mask)[0], plane.owner(mask)[1], pl.ds(h * hold, hold)]

    def p_copy(d, same):
        sec = plane.sec if same else layers - 1 - plane.sec
        number = d if same else count + d
        return pltpu.make_async_remote_copy(
            src_ref=packed_ref, dst_ref=params_ref.at[plane.sec, place], send_sem=pa_send.at[number],
            recv_sem=pa_recv.at[number], device_id={"section": sec, "fsdp": lax.rem(place + d, count)},
            device_id_type=MESH,
        )

    pairs = [(d, same) for d in range(count) for same in (True, False) if d or not same]
    own_strip = pltpu.make_async_copy(strip_ref, thin_ref.at[plane.sec, plane.seq, place], own_sem.at[0])
    own_packed = pltpu.make_async_copy(packed_ref, params_ref.at[plane.sec, place], own_sem.at[1])
    own_block = pltpu.make_async_copy(mine, full.at[pl.ds(pl.multiple_of(place * rows, 16), rows), :], own_sem.at[2])
    own_next = pltpu.make_async_copy(mine, next_gx, own_sem.at[2])
    line = Line(place, count, block, parts, send, recv)
    oline = Line(place, count, oblock, oparts, o_send, o_recv)

    chain_barrier(plane, place, count)
    own_strip.start()
    own_packed.start()

    @pl.when(low)
    def _():
        own_block.start()
        for k in range(parts):
            y_copy(k, block(place, k)).start()

    strips.begin()
    for d, same in pairs:
        p_copy(d, same).start()
    begin_cuts(True, True, low & source)

    @pl.when(low)
    def _():
        own_block.wait()

    for k in range(parts):
        @pl.when(~low)
        def _(k=k):
            y_copy(k, block(place, k)).wait_recv()

        line.begin(k)

    @pl.when(low)
    def _():
        for k in range(parts):
            y_copy(k, block(place, k)).wait_send()

    begin_cuts(False, True, low & source_there)
    x_copy.start()
    for k in range(parts):
        line.forward(1, k)

    @pl.when(~low)
    def _():
        own_next.start()
        for k in range(parts):
            y_copy(k, next_gx.at[pl.ds(k * piece, piece), :]).start()

    own_strip.wait()
    strips.finish()
    spread.begin()

    @pl.when(low & source)
    def _():
        own_cut(True).wait()

    @pl.when(~(low & source))
    def _():
        cut(0, True, True).wait_recv()

    for k in range(oparts):
        oline.begin(k)
    spread.hop(0)
    begin_cuts(True, False, ~low & source)
    begin_cuts(False, False, ~low & source_there)
    for d in range(2, count):
        for k in range(parts):
            line.forward(d, k)
        for k in range(oparts):
            oline.forward(d - 1, k)
        if d == 2:
            for stage in range(1, plane.stages):
                spread.hop(stage)
    for k in range(oparts):
        oline.forward(count - 1, k)
    spread.finish()

    own_packed.wait()
    x_copy.wait()

    @pl.when(low)
    def _():
        for k in range(parts):
            y_copy(k, next_gx.at[pl.ds(k * piece, piece), :]).wait_recv()

    @pl.when(~low)
    def _():
        own_next.wait()
        for k in range(parts):
            y_copy(k, block(place, k)).wait_send()

    @pl.when(~low & source)
    def _():
        own_cut(False).wait()

    @pl.when(~(~low & source))
    def _():
        cut(0, True, False).wait_recv()

    @pl.when(source)
    def _():
        for d in range(1, count):
            cut(d, True, False).wait_send()

    @pl.when(source_there)
    def _():
        for d in range(count):
            cut(d, False, False).wait_send()

    for d, same in pairs:
        p_copy(d, same).wait()
    strips.drain()
    spread.drain()
    line.drain()
    oline.drain()


def start_up(mine, theirs, mine_o, theirs_o, ends, strip, packed, number):
    layers, ranks, count = lax.axis_size("section"), lax.axis_size("seq"), lax.axis_size("fsdp")
    parts = 4 if mine.shape[0] % 64 == 0 else 2
    mine_o = mine_o.reshape(count, -1, mine_o.shape[1])
    theirs_o = theirs_o.reshape(mine_o.shape)
    oparts = 2 if mine_o.shape[1] % 32 == 0 else 1
    anywhere = pl.BlockSpec(memory_space=pl.ANY)
    dma = pltpu.SemaphoreType.DMA
    size = layers * ranks
    half = ends.shape[1] // layers
    return pl.pallas_call(
        functools.partial(start_kernel, layers, ranks, parts, oparts),
        in_specs=[anywhere] * 7,
        out_specs=[anywhere] * 7,
        out_shape=[
            jax.ShapeDtypeStruct((count * mine.shape[0], mine.shape[1]), BF16),
            jax.ShapeDtypeStruct(mine_o.shape, BF16),
            jax.ShapeDtypeStruct(mine.shape, BF16),
            jax.ShapeDtypeStruct(mine_o.shape[1:], BF16),
            jax.ShapeDtypeStruct((ends.shape[0], half, ends.shape[2]), BF16),
            jax.ShapeDtypeStruct((layers, ranks, count) + strip.shape, BF16),
            jax.ShapeDtypeStruct((layers, count) + packed.shape, BF16),
        ],
        scratch_shapes=[
            dma((4,)),
            dma((parts,)),
            dma((parts,)),
            dma((1,)),
            dma((1,)),
            dma((2, count, parts)),
            dma((2, count, parts)),
            dma((2, count, oparts)),
            dma((2, count, oparts)),
            dma((2, count)),
            dma((2,)),
            dma((count,)),
            dma((count,)),
            dma((2, size)),
            dma((2, size)),
            dma((2 * count,)),
            dma((2 * count,)),
        ],
        compiler_params=pltpu.CompilerParams(collective_id=number, has_side_effects=True),
        name="start_up",
    )(mine, theirs, mine_o, theirs_o, ends, strip, packed)


def swapped(value, axis):
    count = lax.axis_size(axis)
    return lax.ppermute(value, axis, [(i, count - 1 - i) for i in range(count)])


PLANE = ("section", "seq")
EVERY = ("section", "seq", "fsdp")


def per_device(
    section_ends, norm_gain, in_weight, conv_weight, conv_bias, step_bias, log_decay, skip_gain, gate_gain, out_weight
):
    sec, seq, dep = lax.axis_index("section"), lax.axis_index("seq"), lax.axis_index("fsdp")
    layers, ranks, depth = lax.axis_size("section"), lax.axis_size("seq"), lax.axis_size("fsdp")
    group = layers * ranks
    here = sec * ranks + seq
    there = (layers - 1 - sec) * ranks + seq
    low_layer = sec == 0
    width = in_weight.shape[1] * depth
    inner = gate_gain.shape[1] * depth
    chans = conv_bias.shape[1] * depth
    heads_all = step_bias.shape[1] * depth
    taps = conv_weight.shape[1]
    cw = inner // group
    heads = cw // HEAD
    shared = 2 * STATE

    ends = section_ends[0, :, 0]
    piece = ends.shape[1] // layers

    def head_columns(v, begin, count):
        return lax.dynamic_slice_in_dim(v, begin, count, v.ndim - 1)

    def own_columns(rank):
        return jnp.concatenate(
            [head_columns(in_weight[0], rank * cw, cw), head_columns(in_weight[0], inner + rank * cw, cw)], 1
        )

    out_rows = out_weight.shape[1]

    def own_rows(rank):
        start = jnp.clip(rank * cw - dep * out_rows, 0, out_rows - cw)
        return lax.dynamic_slice_in_dim(out_weight[0], start, cw, 0)

    strip = in_weight.shape[1] // ranks
    thin = lax.dynamic_slice(in_weight[0], (seq * strip, inner + chans - shared), (strip, shared + heads_all))
    thin = jnp.pad(thin, ((0, 0), (0, STATE - heads_all)))
    flat = [norm_gain, conv_weight, conv_bias, step_bias, log_decay, skip_gain, gate_gain]
    sizes = [v.size for v in flat]
    packed = jnp.concatenate([v.reshape(-1) for v in flat])
    packed = jnp.pad(packed, (0, -packed.size % 2048)).reshape(-1, STATE)
    wgx, wo, next_gx, next_o, got, thin, packed = start_up(
        own_columns(here), own_columns(there), own_rows(here), own_rows(there), ends, thin, packed, 0
    )
    packed = packed.reshape(layers, depth, -1).astype(F32)
    thin = jnp.transpose(thin, (0, 2, 1, 3, 4)).reshape(layers, width, -1)
    hidden = jnp.where(low_layer, ends[:, :piece], got).astype(F32).reshape(layers * piece, width)
    cot = jnp.where(low_layer, got, ends[:, piece:]).astype(F32).reshape(layers * piece, width)

    def own_tokens(v):
        v = lax.dynamic_slice_in_dim(v, seq, 1, 1)[:, 0]
        return lax.dynamic_slice_in_dim(v, sec * piece, piece, 1).reshape(-1, 1)

    def member(layer, number):
        begin = sum(sizes[:number])
        return packed[layer, :, begin : begin + sizes[number]]

    def vectors(layer):
        kernel = jnp.transpose(member(layer, 1).reshape(depth, taps, -1), (1, 0, 2)).reshape(taps, chans)
        rows = jnp.concatenate([kernel, member(layer, 2).reshape(1, chans)], 0)
        rows = jnp.concatenate([head_columns(rows, here * cw, cw), rows[:, inner:]], 1)
        total = cw + shared

        def padded(v):
            return jnp.pad(v[None], ((0, 0), (0, total - v.shape[0])))

        gain = head_columns(member(layer, 6).reshape(-1), here * cw, cw)
        by_head = [head_columns(member(layer, n).reshape(-1), here * heads, heads) for n in (3, 4, 5)]
        return jnp.concatenate(
            [rows, jnp.zeros((5 - taps - 1, total), F32), padded(gain), padded(by_head[0]), padded(by_head[1]),
             padded(jnp.repeat(by_head[2], HEAD)), jnp.zeros((7, total), F32)], 0)

    gains = [member(layer, 0).reshape(1, -1) for layer in range(layers)]
    vecs = [vectors(layer) for layer in range(layers)]

    saved, weights = [], []
    for layer in range(layers):
        ws, wo = thin[layer], wo.reshape(cw, width)
        weights.append((wgx, ws, wo))
        rs = lax.rsqrt(jnp.mean(hidden * hidden, axis=-1, keepdims=True) + EPS)
        following = (next_gx, next_o) if layer + 1 < layers else ()
        raw, ss, pgx, ps, res, ent, full, *after = layer_forward(
            (hidden * rs * gains[layer]).astype(BF16), wgx, ws, wo, vecs[layer], taps, 2 * layers + layer, *following
        )
        if after:
            wgx, wo = after
        r_rows = lax.rsqrt(ss / inner + EPS)
        r = own_tokens(r_rows)
        saved.append((hidden, rs, full, pgx, ps, res, ent, raw, r, r_rows))
        hidden = hidden + r * raw
        if layer + 1 < layers:
            hidden = hidden.astype(BF16).astype(F32)
    output = hidden

    grad, late = cot, ()
    small = [None] * layers
    for layer in reversed(range(layers)):
        wgx, ws, wo = weights[layer]
        before, rs, full, pgx, ps, res, ent, raw, r, r_rows = saved[layer]
        low = grad.astype(BF16)
        pull = r * r * r * jnp.sum(low.astype(F32) * raw, axis=-1, keepdims=True) / inner
        pull = jnp.broadcast_to(pull.reshape(layers, 1, piece), (layers, 8, piece))
        gn, gpgx, gps, no, tiny, gb, *met = layer_backward(
            low, pull, r_rows, pgx, ps, res, ent, wgx, ws, wo, vecs[layer], taps, 3 * layers + layer, *late
        )
        if layer > 0:
            late = (
                jnp.stack([dot(gpgx, v, 0, 0).astype(BF16) for v in jnp.split(full, depth, 1)]),
                dot(no, gb, 0, 0).astype(BF16).reshape(depth, -1, width),
            )
            late_thin = dot(gps, full, 0, 0).astype(BF16)
        else:
            last = (full, gpgx, gps, no, gb, late_thin, met[0], met[1].reshape(cw, width))
        unit = before * rs
        g_gain = jnp.sum(gn * unit, axis=0)
        gn = gn * gains[layer]
        grad = grad + rs * (gn - unit * jnp.mean(gn * unit, axis=-1, keepdims=True))
        if layer > 0:
            grad = grad.astype(BF16).astype(F32)

        by_head = lax.dynamic_update_slice(jnp.zeros((3, STATE), F32), tiny[6:9, :heads], (0, here * heads))
        small[layer] = (tiny, jnp.concatenate([g_gain, by_head.reshape(-1)]))

    output = output.reshape(layers, piece, width)
    grad = grad.reshape(layers, piece, width)
    g_norm = jnp.concatenate([s[1] for s in small])
    lasting = g_norm.size // layers
    g_norm = jnp.pad(g_norm, (0, -g_norm.size % (8 * STATE))).reshape(8, -1)
    gall, oall, sm, g_norm, got = finish(
        *last, jnp.stack([s[0] for s in small]).astype(BF16), g_norm, jnp.where(low_layer, output, grad).astype(BF16), 4 * layers
    )
    got = got.astype(F32)
    results = jnp.where(low_layer, jnp.concatenate([grad, got], 1), jnp.concatenate([got, output], 1))
    section_results = results[None, :, None]
    grad_in = gall.astype(F32).T[None]
    grad_out = oall.reshape(out_rows, width).astype(F32)[None]

    sm = sm.astype(F32)
    conv = jnp.transpose(sm[:, : taps + 1, :cw], (1, 0, 2)).reshape(taps + 1, inner)
    conv = jnp.concatenate([conv, jnp.sum(sm[:, : taps + 1, cw:], 0)], 1)
    g_norm = g_norm.reshape(-1)
    g_norm = jnp.where(low_layer, g_norm[:lasting], g_norm[lasting : 2 * lasting])
    by_head = g_norm[width:].reshape(3, STATE)[:, :heads_all]
    g_norm = g_norm[:width]

    def share(v):
        count = v.shape[-1] // depth
        return lax.dynamic_slice_in_dim(v, dep * count, count, v.ndim - 1)[None]

    return (
        section_results,
        share(g_norm),
        grad_in,
        share(conv[:taps]),
        share(conv[taps]),
        share(by_head[0]),
        share(by_head[1]),
        share(by_head[2]),
        share(sm[:, 5, :cw].reshape(-1)),
        grad_out,
    )


def solution(mesh):
    weight = P("section", "fsdp")
    matrix = P("section", "fsdp", None)
    ends = P("section", None, "fsdp", "seq", None)
    kernel = P("section", None, "fsdp")
    return jax.shard_map(
        per_device,
        mesh=mesh,
        in_specs=(ends, weight, matrix, kernel, weight, weight, weight, weight, weight, matrix),
        out_specs=(ends, weight, matrix, kernel, weight, weight, weight, weight, weight, matrix),
        check_vma=False,
    )
```
